256 devices in a mesh: cell: 32 (over z, y), spot: 8 (over x, core).
Axes of the slice: x: 4, y: 4, z: 8, core: 2. Of those that a mesh axis runs over, the one named last changes fastest.
Arguments:
- logits: float32 [45056, 8192], P('cell', 'spot'), may hold values from -8 to 8
- filter_logits: float32 [45056], P('cell'), may hold values from -6 to 6
- expression: bfloat16 [45056, 2048], P('cell', 'spot'), may hold values from 0.049804688 to 20
- spatial: float32 [8192, 2048], P('spot'), may hold values from 0.05 to 20
- prior: float32 [8192], P('spot'), may hold values from 0.2 to 5
- slide_sizes: int32 [4], replicated, may hold values from 1 to 4096, 8192 in all
- target: int32 [1], replicated, may hold values from 11264 to 33791
Outputs:
- losses: float32 [5], replicated
- predicted: float32 [8192, 2048], P('spot', 'cell')
- grad_logits: float32 [45056, 8192], P('cell', 'spot')
- grad_filter: float32 [45056], P('cell')
- grad_expression: float32 [45056, 2048], P('cell', 'spot')
The draws below stay inside these ranges and needn't reach their ends.
Inputs may be any that keep to these rules, and one draw needn't show every extreme that they name: `slide_sizes`: the sizes sum to 8192; each slide is a run of consecutive spots, in order.
All inputs are finite; a program needn't handle non-finite values.
Results may differ from the reference program's by a relative error of at most 0.00035.
Values may be sent and summed in bfloat16 or wider, within the bound.
A program may use at most 192 MiB of HBM per device.

```python
import math
import jax
import jax.numpy as jnp
import numpy as np
from jax import lax

GENES = 2048
SLIDES = 4
CELLS = 45056
SPOTS = 8192


def shard_levels(key, extent, split, smallest, high):
    def one(position, shards_of):
        heights = jax.random.uniform(jax.random.fold_in(jax.random.fold_in(key, 6), position), (shards_of,), jnp.float32, smallest / len(split), high / len(split))
        return jnp.repeat(jnp.exp(heights), extent[position] // shards_of).reshape((-1,) + (1,) * (len(extent) - position - 1))

    loudness = one(*split[0])
    for cut in split[1:]:
        loudness = loudness * one(*cut)
    return loudness


def length_profile(count, total, limit, slope):
    portions = [(1 << 20) // math.isqrt(standing ** slope) + 1 for standing in range(2, count + 1)]
    rest, holding = total - limit - (count - 1), [1] * (count - 1)
    while rest > 0:
        free = [i for i in range(count - 1) if holding[i] < limit]
        pool, budget = sum([portions[i] for i in free]), rest
        for i in free:
            more = min(limit - holding[i], max(1, budget * portions[i] // pool), rest)
            holding[i] = holding[i] + more
            rest = rest - more
    return np.array([limit] + holding)


def ragged(rng, amount, total, most, lean):
    if amount == 2:
        one = jax.random.randint(rng, (), max(1, total - most), min(most, total - 1) + 1)
        return jnp.stack([one, total - one])
    tallies = jnp.asarray(length_profile(amount, total, most, lean), jnp.int32)
    twos = (amount - 1) // 2
    giver, receiver = tallies[1:1 + 2 * twos:2], tallies[2:2 + 2 * twos:2]
    slack = jnp.minimum(giver - 1, most - receiver)
    moved = jax.random.randint(jax.random.fold_in(rng, 1), (twos,), 0, 1 << 20) % (slack + 1)
    tallies = tallies.at[1:1 + 2 * twos:2].set(giver - moved).at[2:2 + 2 * twos:2].set(receiver + moved)
    return tallies[jax.random.permutation(jax.random.fold_in(rng, 2), amount)]


def noise(stream_key, extent, deviation, most, split=(), kind=jnp.bfloat16):
    entries = deviation * jax.random.normal(stream_key, extent, jnp.float32)
    if split:
        entries = entries * shard_levels(stream_key, extent, split, -0.22, 0.18)
    return jnp.clip(entries, -most, most).astype(kind)


def setup_inputs(seed: int = 0) -> dict:
    seeds = jax.random.split(jax.random.key(seed), 8)
    return {
        "logits": noise(seeds[0], (CELLS, SPOTS), 2.0, 8.0, ((0, 32), (1, 8)), jnp.float32),
        "filter_logits": noise(seeds[1], (CELLS,), 1.5, 6.0, ((0, 32),), jnp.float32),
        "expression": jnp.clip(jnp.exp(math.log(20.0) - 5.9953784 * jax.random.uniform(seeds[2], (CELLS, GENES), jnp.float32) ** shard_levels(seeds[2], (CELLS, GENES), ((0, 32), (1, 8)), -0.2, 0.2)), 0.049804688, 20.0).astype(jnp.bfloat16),
        "spatial": jnp.clip(jnp.exp(math.log(20.0) - 5.9914645 * jax.random.uniform(seeds[3], (SPOTS, GENES), jnp.float32) ** shard_levels(seeds[3], (SPOTS, GENES), ((0, 8),), -0.2, 0.2)), 0.05, 20.0),
        "prior": jnp.clip(jnp.exp(math.log(5.0) - 3.218876 * jax.random.uniform(seeds[4], (SPOTS,), jnp.float32) ** shard_levels(seeds[4], (SPOTS,), ((0, 8),), -0.2, 0.2)), 0.2, 5.0),
        "slide_sizes": ragged(seeds[5], SLIDES, SPOTS, SPOTS // 2, 0).astype(jnp.int32),
        "target": jax.random.randint(seeds[6], (1,), CELLS // 4, 3 * CELLS // 4).astype(jnp.int32),
    }


epsilon = 1e-06
HIGHEST = lax.Precision.HIGHEST

@jax.custom_vjp
def low(v):
    return lax.optimization_barrier(v.astype(jnp.bfloat16)).astype(jnp.float32)

@jax.custom_vjp
def low_back(v):
    return v

def low_keep(v):
    return (low(v), None)

def low_pass(kept, grad):
    return (grad,)

def back_keep(v):
    return (v, None)

def back_low(kept, grad):
    return (low(grad),)
low.defvjp(low_keep, low_pass)
low_back.defvjp(back_keep, back_low)

def slide_onehot(slide_sizes, positions):
    ends = jnp.cumsum(slide_sizes)
    owner = lax.optimization_barrier(jnp.sum((positions[:, None] >= ends[None, :]).astype(jnp.int32), axis=1))
    labels = jnp.arange(slide_sizes.shape[0], dtype=jnp.int32)
    return (owner[:, None] == labels[None, :]).astype(jnp.float32)

def reference(logits, filter_logits, expression, spatial, prior, slide_sizes, target):
    membership = slide_onehot(slide_sizes, jnp.arange(SPOTS, dtype=jnp.int32))
    goal_count = target[0].astype(jnp.float32)
    profiles32 = expression.astype(jnp.float32)

    def forward(logit_map, logit_filter, profiles):
        shifted = logit_map - lax.optimization_barrier(jnp.max(logit_map, axis=0, keepdims=True))
        exponent = jnp.exp(shifted)
        mapping = exponent / lax.optimization_barrier(jnp.sum(exponent, axis=0, keepdims=True))
        filter_on = jax.nn.sigmoid(logit_filter)
        weights = mapping * filter_on[:, None]
        predicted = low_back(jnp.dot(low(weights).T, profiles, precision=HIGHEST))
        density = lax.optimization_barrier(jnp.sum(weights, axis=0))
        slide_inner = jnp.dot(membership.T, predicted * spatial, precision=HIGHEST)
        slide_square = jnp.dot(membership.T, predicted * predicted, precision=HIGHEST)
        slide_truth = jnp.dot(membership.T, spatial * spatial, precision=HIGHEST)
        gene_cos = slide_inner * lax.rsqrt(slide_square + epsilon) * lax.rsqrt(slide_truth + epsilon)
        loss_gene = -jnp.mean(gene_cos)
        spot_cos = lax.optimization_barrier(jnp.sum(predicted * spatial, axis=1)) * lax.rsqrt(lax.optimization_barrier(jnp.sum(predicted * predicted, axis=1)) + epsilon) * lax.rsqrt(lax.optimization_barrier(jnp.sum(spatial * spatial, axis=1)) + epsilon)
        loss_spot = -jnp.mean(spot_cos)
        slide_density = jnp.dot(membership, jnp.dot(membership.T, density, precision=HIGHEST), precision=HIGHEST)
        slide_prior = jnp.dot(membership, jnp.dot(membership.T, prior, precision=HIGHEST), precision=HIGHEST)
        target_share = prior / slide_prior
        pred_share = density / slide_density
        loss_density = jnp.sum(target_share * (jnp.log(target_share) - jnp.log(pred_share))) / SLIDES
        count_gap = jnp.sum(filter_on) - goal_count
        loss_count = jnp.sqrt(count_gap * count_gap + 1.0) / CELLS
        loss_filter = jnp.mean(filter_on - filter_on * filter_on)
        losses = jnp.stack([loss_gene, loss_spot, loss_density, loss_count, loss_filter])
        return (jnp.sum(losses), (losses, predicted))
    total, backward, extras = jax.vjp(forward, logits, filter_logits, profiles32, has_aux=True)
    grad_logits, grad_filter, grad_expression = backward(jnp.ones_like(total))
    losses, predicted = extras
    return (losses, predicted, grad_logits, grad_filter, grad_expression)
```

```python
import functools

import jax
import jax.numpy as jnp
from jax import lax
from jax.experimental import pallas as pl
from jax.experimental.pallas import tpu as pltpu
from jax.sharding import Mesh
from jax.sharding import PartitionSpec as P

CELL = ("z", "y")
SPOT = ("x", "c")
SIZE = {"z": 8, "y": 4, "x": 4, "c": 2}
MESH = pl.DeviceIdType.MESH
ROWS = 1408
COLS = 1024
OWN = 256
PIECE = 64
LANES = 128
BLOCKS = ROWS // LANES
SPLIT = 384
NEARBY = COLS - SPLIT
GROUPS = SPLIT // LANES
LIMIT = 60 * 1024 * 1024

epsilon = 1e-06
HIGHEST = lax.Precision.HIGHEST


def away(axis, step):
    return {axis: lax.rem(lax.axis_index(axis) + step + SIZE[axis], SIZE[axis])}


def ring(position, step, size):
    return lax.rem(position + step + size, size)


def greet(targets):
    barrier = pltpu.get_barrier_semaphore()
    for target in targets:
        pl.semaphore_signal(barrier, inc=1, device_id=target, device_id_type=MESH)


def greeted(targets):
    pl.semaphore_wait(pltpu.get_barrier_semaphore(), len(targets))


class Wires:
    def __init__(self, send_sems, recv_sems):
        self.send_sems, self.recv_sems, self.used, self.sent = send_sems, recv_sems, 0, []

    def send(self, source, target, device):
        at = self.used
        self.used += 1
        copy = pltpu.make_async_remote_copy(
            src_ref=source,
            dst_ref=target,
            send_sem=self.send_sems.at[at],
            recv_sem=self.recv_sems.at[at],
            device_id=device,
            device_id_type=MESH,
        )
        copy.start()
        self.sent.append(copy)
        return copy

    def close(self):
        for copy in self.sent:
            copy.wait_send()


def pick(order, at):
    return order[at]


def forward_kernel(
    logits,
    filters,
    expression,
    spatial,
    pred_out,
    truth_out,
    stats_out,
    grown_out,
    weights_out,
    profiles_out,
    grown,
    weights,
    profiles,
    turned,
    part,
    slab,
    truth_all,
    gate,
    mine,
    near_stats,
    far_stats,
    half_y,
    full_y,
    half_bz,
    full_bz,
    half_az,
    full_az,
    half_ay,
    full_ay,
    send_sems,
    recv_sems,
    local_sems,
):
    z, y = lax.axis_index("z"), lax.axis_index("y")
    x, c = lax.axis_index("x"), lax.axis_index("c")
    wires = Wires(send_sems, recv_sems)
    own = x * 2 + c
    loads = []
    for b in range(BLOCKS):
        rows = pl.ds(b * LANES, LANES)
        loads.append(
            pltpu.make_async_copy(logits.at[rows, :], grown.at[rows, :], local_sems.at[b])
        )
    load_own = pltpu.make_async_copy(expression, profiles.at[own], local_sems.at[BLOCKS])
    cell = z * 4 + y
    aligned = pl.multiple_of((cell // 2) * LANES, LANES)
    load_truth = pltpu.make_async_copy(
        spatial.at[:, pl.ds(aligned, LANES)], slab, local_sems.at[BLOCKS + 1]
    )
    load_own.start()
    for load in loads:
        load.start()
    load_truth.start()
    targets = (
        [away("y", d) for d in (1, 2, 3)]
        + [away("z", d) for d in range(1, 8)]
        + [away("x", 1), away("x", 3), away("c", 1)]
    )
    greet(targets)

    gates = jax.nn.sigmoid(filters[...])
    for b in range(BLOCKS):
        gate[pl.ds(b * LANES, LANES), :] = jnp.broadcast_to(
            gates[b : b + 1, :], (LANES, LANES)
        ).T
    kept = jnp.sum(gates, keepdims=True)
    spread = jnp.sum(gates - gates * gates, keepdims=True)
    lane = lax.broadcasted_iota(jnp.int32, (1, COLS), 1)
    mine[3:4, :] = jnp.where(lane == 0, kept, jnp.where(lane == 1, spread, 0.0))

    load_own.wait()
    greeted(targets)
    half = ROWS // 2
    low_rows, high_rows = pl.ds(0, half), pl.ds(half, half)

    def share(block, rows, device):
        return wires.send(profiles.at[block, rows], profiles.at[block, rows], device)

    def share_whole(block, device):
        return wires.send(profiles.at[block], profiles.at[block], device)

    right, left, twin = away("x", 1), away("x", 3), away("c", 1)
    right_low = share(own, low_rows, right)
    left_high = share(own, high_rows, left)
    twin_own = share_whole(own, twin)
    right_high = share(own, high_rows, right)
    left_low = share(own, low_rows, left)

    mine[0:3, :] = jnp.zeros((3, COLS), jnp.float32)
    for b in range(BLOCKS):
        loads[b].wait()

        @pl.loop(0, COLS // LANES)
        def _(j, b=b):
            rows = pl.ds(b * LANES, LANES)
            lanes = pl.ds(pl.multiple_of(j * LANES, LANES), LANES)
            e = jnp.exp(grown[rows, lanes])
            grown[rows, lanes] = e
            mine[0:1, lanes] += jnp.sum(e, axis=0, keepdims=True)
            mine[1:2, lanes] += jnp.sum(e * gate[rows, :], axis=0, keepdims=True)

    load_truth.wait()
    truth_all[...] = slab[...].T
    truth = truth_all.at[pl.ds(pl.multiple_of(lax.rem(cell, 2) * PIECE, PIECE), PIECE), :]
    held = truth[...]
    mine[2:3, :] = jnp.sum(held * held, axis=0, keepdims=True)

    near = [wires.send(mine, near_stats.at[d - 1], away("y", d)) for d in (1, 2, 3)]
    save_grown = pltpu.make_async_copy(grown, grown_out, local_sems.at[0])
    save_grown.start()
    for copy in near:
        copy.wait_recv()
    far_stats[0] = mine[...] + near_stats[0] + near_stats[1] + near_stats[2]
    far = [wires.send(far_stats.at[0], far_stats.at[d], away("z", d)) for d in range(1, 8)]
    right_low.wait_recv()
    onward_low = share(own_of(x, 3, c), low_rows, right)
    left_high.wait_recv()
    onward_high = share(own_of(x, 1, c), high_rows, left)
    for copy in far:
        copy.wait_recv()
    total = far_stats[0]
    for d in range(1, 8):
        total = total + far_stats[d]
    stats_out[...] = total
    scale = 1.0 / total[0:1, :]

    @pl.loop(0, BLOCKS)
    def _(b):
        rows = pl.ds(pl.multiple_of(b * LANES, LANES), LANES)
        for j in range(COLS // LANES):
            lanes = pl.ds(j * LANES, LANES)
            weights[rows, lanes] = (
                grown[rows, lanes] * scale[:, j * LANES : (j + 1) * LANES] * gate[rows, :]
            ).astype(jnp.bfloat16)

    save_weights = pltpu.make_async_copy(weights, weights_out, local_sems.at[1])
    save_weights.start()
    save_truth = pltpu.make_async_copy(truth, truth_out, local_sems.at[2])
    save_truth.start()

    def multiply(block):
        turned[...] = profiles[block].T

        @pl.loop(0, COLS // OWN)
        def _(j):
            lanes = pl.ds(pl.multiple_of(j * OWN, OWN), OWN)
            part[block, :, lanes] = jnp.dot(
                turned[...], weights[:, lanes], preferred_element_type=jnp.float32
            )

    sought = [ring(z, d, 8) for d in (4, 3, 5, 2, 6, 1, 7, 0)]
    order = [own, own_of(x, 0, 1 - c)] + [jnp.int32(0)] * 6
    at = jnp.int32(2)
    for block in sought:
        other = jnp.where(block // 2 != x, 1, 0)
        for i in range(2, 8):
            order[i] = order[i] + block * other * jnp.where(at == i, 1, 0)
        at = at + other

    B = pl.ds(SPLIT, NEARBY)
    y_up, y_down, z_up, z_down = away("y", 1), away("y", 3), away("z", 1), away("z", 7)

    def piece(position, extra=0, size=PIECE):
        return pl.ds(pl.multiple_of(position * PIECE, PIECE) + extra, size)

    hop = PIECE // 2
    started, passed = {}, {}

    def y_start(i):
        s, p = order[i], ring(y, 2, 4)
        started[i] = (
            wires.send(part.at[s, piece(p, 0, hop), B], half_y.at[i, 0], y_up),
            wires.send(part.at[s, piece(p, hop, hop), B], half_y.at[i, 1], y_down),
        )

    def y_pass(i):
        s, up, down = order[i], ring(y, 1, 4), ring(y, 3, 4)
        started[i][0].wait_recv()
        part[s, piece(up, 0, hop), B] += half_y[i, 0]
        first = wires.send(part.at[s, piece(up), B], full_y.at[i, 0], y_up)
        started[i][1].wait_recv()
        part[s, piece(down, hop, hop), B] += half_y[i, 1]
        second = wires.send(part.at[s, piece(down), B], full_y.at[i, 1], y_down)
        passed[i] = (first, second)

    def y_end(i):
        passed[i][0].wait_recv()
        passed[i][1].wait_recv()
        part[order[i], piece(y), B] += full_y[i, 0] + full_y[i, 1]

    bz = {}

    def bz_start():
        d = ring(z, 4, 8)
        bz[0] = (
            wires.send(part.at[d, piece(y, 0, hop), B], half_bz.at[0], z_up),
            wires.send(part.at[d, piece(y, hop, hop), B], half_bz.at[1], z_down),
        )

    def bz_pass(t):
        up, down = ring(z, 4 - t, 8), ring(z, t - 4, 8)
        bz[t - 1][0].wait_recv()
        if t == 1:
            part[up, piece(y, 0, hop), B] += half_bz[0]
        else:
            part[up, piece(y), B] += full_bz[t - 2, 0]
        first = wires.send(part.at[up, piece(y), B], full_bz.at[t - 1, 0], z_up)
        bz[t - 1][1].wait_recv()
        if t == 1:
            part[down, piece(y, hop, hop), B] += half_bz[1]
        else:
            part[down, piece(y), B] += full_bz[t - 2, 1]
        second = wires.send(part.at[down, piece(y), B], full_bz.at[t - 1, 1], z_down)
        bz[t] = (first, second)

    def bz_end():
        bz[3][0].wait_recv()
        bz[3][1].wait_recv()
        part[z, piece(y), B] += full_bz[2, 0] + full_bz[2, 1]

    az = {}

    def lanes_of(a):
        return pl.ds(a * LANES, LANES)

    def az_start(a):
        d, lanes = ring(z, 4, 8), lanes_of(a)
        az[a, 0] = (
            wires.send(part.at[d, pl.ds(0, LANES), lanes], half_az.at[a, 0], z_up),
            wires.send(part.at[d, pl.ds(LANES, LANES), lanes], half_az.at[a, 1], z_down),
        )

    def az_pass(a, t):
        up, down, lanes = ring(z, 4 - t, 8), ring(z, t - 4, 8), lanes_of(a)
        az[a, t - 1][0].wait_recv()
        if t == 1:
            part[up, pl.ds(0, LANES), lanes] += half_az[a, 0]
        else:
            part[up, :, lanes] += full_az[a, t - 2, 0]
        first = wires.send(part.at[up, :, lanes], full_az.at[a, t - 1, 0], z_up)
        az[a, t - 1][1].wait_recv()
        if t == 1:
            part[down, pl.ds(LANES, LANES), lanes] += half_az[a, 1]
        else:
            part[down, :, lanes] += full_az[a, t - 2, 1]
        second = wires.send(part.at[down, :, lanes], full_az.at[a, t - 1, 1], z_down)
        az[a, t] = (first, second)

    def az_end(a):
        az[a, 3][0].wait_recv()
        az[a, 3][1].wait_recv()
        part[z, :, lanes_of(a)] += full_az[a, 2, 0] + full_az[a, 2, 1]

    A = pl.ds(0, SPLIT)
    ay = {}

    def ay_start():
        p = ring(y, 2, 4)
        ay[0] = (
            wires.send(part.at[z, piece(p, 0, hop), A], half_ay.at[0], y_up),
            wires.send(part.at[z, piece(p, hop, hop), A], half_ay.at[1], y_down),
        )

    def ay_pass():
        up, down = ring(y, 1, 4), ring(y, 3, 4)
        ay[0][0].wait_recv()
        part[z, piece(up, 0, hop), A] += half_ay[0]
        first = wires.send(part.at[z, piece(up), A], full_ay.at[0], y_up)
        ay[0][1].wait_recv()
        part[z, piece(down, hop, hop), A] += half_ay[1]
        second = wires.send(part.at[z, piece(down), A], full_ay.at[1], y_down)
        ay[1] = (first, second)

    def ay_end():
        ay[1][0].wait_recv()
        ay[1][1].wait_recv()
        part[z, piece(y), A] += full_ay[0] + full_ay[1]

    multiply(own)
    y_start(0)
    twin_own.wait_recv()
    multiply(own_of(x, 0, 1 - c))
    y_start(1)
    y_pass(0)
    right_high.wait_recv()
    twin_left = share_whole(own_of(x, 3, c), twin)
    left_low.wait_recv()
    twin_right = share_whole(own_of(x, 1, c), twin)
    multiply(own_of(x, 3, c))
    multiply(own_of(x, 1, c))
    y_pass(1)
    twin_left.wait_recv()
    multiply(own_of(x, 3, 1 - c))
    twin_right.wait_recv()
    multiply(own_of(x, 1, 1 - c))
    onward_low.wait_recv()
    twin_low = share(own_of(x, 2, c), low_rows, twin)
    onward_high.wait_recv()
    twin_high = share(own_of(x, 2, c), high_rows, twin)
    multiply(own_of(x, 2, c))
    twin_low.wait_recv()
    twin_high.wait_recv()
    multiply(own_of(x, 2, 1 - c))
    save_profiles = pltpu.make_async_copy(profiles, profiles_out, local_sems.at[3])
    save_profiles.start()

    for a in range(GROUPS):
        az_start(a)
    y_start(2)
    y_end(0)
    y_start(3)
    y_end(1)
    y_pass(2)
    for a in range(GROUPS):
        az_pass(a, 1)
    y_start(4)
    y_pass(3)
    y_end(2)
    bz_start()
    y_start(5)
    y_pass(4)
    for a in range(GROUPS):
        az_pass(a, 2)
    y_end(3)
    y_start(6)
    y_pass(5)
    y_end(4)
    bz_pass(1)
    y_start(7)
    y_pass(6)
    for a in range(GROUPS):
        az_pass(a, 3)
    y_end(5)
    y_pass(7)
    y_end(6)
    bz_pass(2)
    for a in range(GROUPS):
        az_end(a)
    ay_start()
    y_end(7)
    bz_pass(3)
    ay_pass()
    bz_end()
    ay_end()
    pred_out[...] = part[z, piece(y), :]
    for save in (save_grown, save_weights, save_truth, save_profiles):
        save.wait()
    wires.close()


def own_of(x, step, c):
    return ring(x, step, 4) * 2 + c


FORWARD_COPIES = 3 + 7 + 5 + 2 + 4 + 32 + 8 + 8 * GROUPS + 4


def forward(logits, filters, expression, spatial):
    f32, bf16 = jnp.float32, jnp.bfloat16
    anywhere = pl.BlockSpec(memory_space=pl.ANY)
    inside = pl.BlockSpec(memory_space=pltpu.VMEM)
    return pl.pallas_call(
        forward_kernel,
        out_shape=(
            jax.ShapeDtypeStruct((PIECE, COLS), f32),
            jax.ShapeDtypeStruct((PIECE, COLS), f32),
            jax.ShapeDtypeStruct((4, COLS), f32),
            jax.ShapeDtypeStruct((ROWS, COLS), f32),
            jax.ShapeDtypeStruct((ROWS, COLS), bf16),
            jax.ShapeDtypeStruct((8, ROWS, OWN), bf16),
        ),
        in_specs=[anywhere, inside, anywhere, anywhere],
        out_specs=(inside, anywhere, inside, anywhere, anywhere, anywhere),
        scratch_shapes=[
            pltpu.VMEM((ROWS, COLS), f32),
            pltpu.VMEM((ROWS, COLS), bf16),
            pltpu.VMEM((8, ROWS, OWN), bf16),
            pltpu.VMEM((OWN, ROWS), bf16),
            pltpu.VMEM((8, OWN, COLS), f32),
            pltpu.VMEM((COLS, LANES), f32),
            pltpu.VMEM((LANES, COLS), f32),
            pltpu.VMEM((ROWS, LANES), f32),
            pltpu.VMEM((4, COLS), f32),
            pltpu.VMEM((3, 4, COLS), f32),
            pltpu.VMEM((8, 4, COLS), f32),
            pltpu.VMEM((8, 2, PIECE // 2, NEARBY), f32),
            pltpu.VMEM((8, 2, PIECE, NEARBY), f32),
            pltpu.VMEM((2, PIECE // 2, NEARBY), f32),
            pltpu.VMEM((3, 2, PIECE, NEARBY), f32),
            pltpu.VMEM((GROUPS, 2, LANES, LANES), f32),
            pltpu.VMEM((GROUPS, 3, 2, OWN, LANES), f32),
            pltpu.VMEM((2, PIECE // 2, SPLIT), f32),
            pltpu.VMEM((2, PIECE, SPLIT), f32),
            pltpu.SemaphoreType.DMA((FORWARD_COPIES,)),
            pltpu.SemaphoreType.DMA((FORWARD_COPIES,)),
            pltpu.SemaphoreType.DMA((BLOCKS + 2,)),
        ],
        compiler_params=pltpu.CompilerParams(
            collective_id=0, has_side_effects=True, vmem_limit_bytes=LIMIT
        ),
        name="forward",
    )(logits, filters, expression, spatial)


def copy_for_each(shard, axis):
    copies = jnp.broadcast_to(shard, (lax.axis_size(axis), *shard.shape))
    return lax.all_to_all(copies, axis, split_axis=0, concat_axis=0, tiled=True)


def together(arrays, axis):
    flat, at, finished = (jnp.concatenate([a.reshape(-1) for a in arrays]), 0, [])
    total = copy_for_each(flat, axis).sum(axis=0)
    for a in arrays:
        finished.append(total[at : at + a.size].reshape(a.shape))
        at += a.size
    return tuple(finished)


def slide_onehot(slide_sizes, positions):
    ends = jnp.cumsum(slide_sizes)
    owner = jnp.sum((positions[:, None] >= ends[None, :]).astype(jnp.int32), axis=1)
    labels = jnp.arange(slide_sizes.shape[0], dtype=jnp.int32)
    return (owner[:, None] == labels[None, :]).astype(jnp.float32)


def on_device(logits, filter_logits, expression, spatial, prior, slide_sizes, target):
    cell_rows, spot_cols = logits.shape
    genes = spatial.shape[1]
    slides = slide_sizes.shape[0]
    cells = cell_rows * lax.axis_size(CELL)
    spots = spot_cols * lax.axis_size(SPOT)
    positions = lax.axis_index(SPOT) * spot_cols + jnp.arange(spot_cols, dtype=jnp.int32)
    membership = slide_onehot(slide_sizes, positions)
    goal_count = target[0].astype(jnp.float32)
    filter_on = jax.nn.sigmoid(filter_logits)
    pred_t, truth_t, stats, grown, weights_low, profiles = forward(
        logits, filter_logits.reshape(BLOCKS, LANES), expression, spatial
    )
    predicted, truth = pred_t.T, truth_t.T
    totals, filtered, spot_truth = stats[0], stats[1], stats[2]
    filter_sums = stats[3, :2]
    mapping = grown / totals[None, :]
    density = filtered / totals
    spot_inner, spot_square = together(
        (jnp.sum(predicted * truth, axis=1), jnp.sum(predicted * predicted, axis=1)), CELL
    )
    slide_inner, slide_square, slide_truth, slide_density, slide_prior = together(
        (
            jnp.dot(membership.T, predicted * truth, precision=HIGHEST),
            jnp.dot(membership.T, predicted * predicted, precision=HIGHEST),
            jnp.dot(membership.T, truth * truth, precision=HIGHEST),
            jnp.dot(membership.T, density, precision=HIGHEST),
            jnp.dot(membership.T, prior, precision=HIGHEST),
        ),
        SPOT,
    )
    gene_left = lax.rsqrt(slide_square + epsilon)
    gene_right = lax.rsqrt(slide_truth + epsilon)
    gene_cos = slide_inner * gene_left * gene_right
    spot_left = lax.rsqrt(spot_square + epsilon)
    spot_right = lax.rsqrt(spot_truth + epsilon)
    spot_cos = spot_inner * spot_left * spot_right
    target_share = prior / jnp.dot(membership, slide_prior, precision=HIGHEST)
    spot_density = jnp.dot(membership, slide_density, precision=HIGHEST)
    pred_share = density / spot_density
    density_part = jnp.sum(target_share * (jnp.log(target_share) - jnp.log(pred_share))) / slides
    gene_scale = 1.0 / (slides * genes)
    spot_scale = 1.0 / spots
    gene_cube = slide_inner * gene_left * gene_left * gene_left * gene_right
    grad_pred = gene_scale * (
        jnp.dot(membership, gene_cube, precision=HIGHEST) * predicted
        - jnp.dot(membership, gene_left * gene_right, precision=HIGHEST) * truth
    )
    spot_cube = spot_inner * spot_left * spot_left * spot_left * spot_right
    grad_pred = grad_pred + spot_scale * (
        spot_cube[:, None] * predicted - (spot_left * spot_right)[:, None] * truth
    )
    grad_low = grad_pred.astype(jnp.bfloat16)
    grad_all = lax.all_gather(
        lax.all_gather(grad_low, "y", axis=1, tiled=True), "z", axis=1, tiled=True
    )
    grad_weights = lax.dot_general(
        jnp.transpose(profiles, (1, 0, 2)).reshape(cell_rows, genes),
        grad_all,
        (((1,), (1,)), ((), ())),
        preferred_element_type=jnp.float32,
    )
    grad_density = (1.0 / spot_density - target_share / density) / slides
    grad_total = grad_weights + grad_density[None, :]
    grad_mapping = filter_on[:, None] * grad_total
    column_dot, gene_total = together(
        (jnp.sum(mapping * grad_mapping, axis=0), jnp.sum(gene_cos)), CELL
    )
    grad_logits = mapping * (grad_mapping - column_dot[None, :])
    filter_part = jnp.sum(mapping * grad_total, axis=1)
    filter_sum, spot_sum, density_sum = together(
        (filter_part, jnp.sum(spot_cos), density_part), SPOT
    )
    count_gap = filter_sums[0] - goal_count
    count_root = jnp.sqrt(count_gap * count_gap + 1.0)
    grad_filter_on = filter_sum + count_gap / count_root / cells + (1.0 - 2.0 * filter_on) / cells
    grad_filter = grad_filter_on * filter_on * (1.0 - filter_on)
    grad_expression = lax.psum_scatter(
        lax.dot_general(
            grad_all, weights_low, (((0,), (1,)), ((), ())), preferred_element_type=jnp.float32
        ),
        SPOT,
        scatter_dimension=0,
        tiled=True,
    ).T
    losses = jnp.stack(
        [
            -gene_total * gene_scale,
            -spot_sum * spot_scale,
            density_sum,
            count_root / cells,
            filter_sums[1] / cells,
        ]
    )
    return (losses, predicted, grad_logits, grad_filter, grad_expression)


def solution(mesh):
    split = Mesh(mesh.devices.reshape(8, 4, 4, 2), ("z", "y", "x", "c"))
    placed = (P(CELL, SPOT), P(CELL), P(CELL, SPOT), P(SPOT, None), P(SPOT), P(), P())
    return jax.shard_map(
        on_device,
        mesh=split,
        in_specs=placed,
        out_specs=(P(), P(SPOT, CELL), P(CELL, SPOT), P(CELL), P(CELL, SPOT)),
        check_vma=False,
    )
```

```python
import functools

import jax
import jax.numpy as jnp
from jax import lax
from jax.experimental import pallas as pl
from jax.experimental.pallas import tpu as pltpu
from jax.sharding import Mesh
from jax.sharding import PartitionSpec as P

CELL = ("z", "y")
SPOT = ("x", "c")
SIZE = {"z": 8, "y": 4, "x": 4, "c": 2}
MESH = pl.DeviceIdType.MESH
ROWS = 1408
COLS = 1024
OWN = 256
PIECE = 64
LANES = 128
BLOCKS = ROWS // LANES
SPLIT = 384
NEARBY = COLS - SPLIT
GROUPS = SPLIT // LANES
LIMIT = 60 * 1024 * 1024

epsilon = 1e-06
HIGHEST = lax.Precision.HIGHEST


def away(axis, step):
    return {axis: lax.rem(lax.axis_index(axis) + step + SIZE[axis], SIZE[axis])}


def ring(position, step, size):
    return lax.rem(position + step + size, size)


def greet(targets):
    barrier = pltpu.get_barrier_semaphore()
    for target in targets:
        pl.semaphore_signal(barrier, inc=1, device_id=target, device_id_type=MESH)


def greeted(targets):
    pl.semaphore_wait(pltpu.get_barrier_semaphore(), len(targets))


class Wires:
    def __init__(self, send_sems, recv_sems):
        self.send_sems, self.recv_sems, self.used, self.sent = send_sems, recv_sems, 0, []

    def send(self, source, target, device):
        at = self.used
        self.used += 1
        copy = pltpu.make_async_remote_copy(
            src_ref=source,
            dst_ref=target,
            send_sem=self.send_sems.at[at],
            recv_sem=self.recv_sems.at[at],
            device_id=device,
            device_id_type=MESH,
        )
        copy.start()
        self.sent.append(copy)
        return copy

    def close(self):
        for copy in self.sent:
            copy.wait_send()


def pick(order, at):
    return order[at]


def forward_kernel(
    logits,
    filters,
    expression,
    spatial,
    pred_out,
    truth_out,
    stats_out,
    grown_out,
    weights_out,
    profiles_out,
    grown,
    weights,
    profiles,
    turned,
    part,
    slab,
    truth_all,
    gate,
    mine,
    near_stats,
    far_stats,
    half_y,
    full_y,
    half_bz,
    full_bz,
    half_az,
    full_az,
    half_ay,
    full_ay,
    send_sems,
    recv_sems,
    local_sems,
):
    z, y = lax.axis_index("z"), lax.axis_index("y")
    x, c = lax.axis_index("x"), lax.axis_index("c")
    wires = Wires(send_sems, recv_sems)
    own = x * 2 + c
    loads = []
    for b in range(BLOCKS):
        rows = pl.ds(b * LANES, LANES)
        loads.append(
            pltpu.make_async_copy(logits.at[rows, :], grown.at[rows, :], local_sems.at[b])
        )
    load_own = pltpu.make_async_copy(expression, profiles.at[own], local_sems.at[BLOCKS])
    cell = z * 4 + y
    aligned = pl.multiple_of((cell // 2) * LANES, LANES)
    load_truth = pltpu.make_async_copy(
        spatial.at[:, pl.ds(aligned, LANES)], slab, local_sems.at[BLOCKS + 1]
    )
    load_own.start()
    for load in loads:
        load.start()
    load_truth.start()
    targets = (
        [away("y", d) for d in (1, 2, 3)]
        + [away("z", d) for d in range(1, 8)]
        + [away("x", 1), away("x", 3), away("c", 1)]
    )
    greet(targets)

    gates = jax.nn.sigmoid(filters[...])
    for b in range(BLOCKS):
        gate[pl.ds(b * LANES, LANES), :] = jnp.broadcast_to(
            gates[b : b + 1, :], (LANES, LANES)
        ).T
    kept = jnp.sum(gates, keepdims=True)
    spread = jnp.sum(gates - gates * gates, keepdims=True)
    lane = lax.broadcasted_iota(jnp.int32, (1, COLS), 1)
    mine[3:4, :] = jnp.where(lane == 0, kept, jnp.where(lane == 1, spread, 0.0))

    load_own.wait()
    greeted(targets)
    half = ROWS // 2
    low_rows, high_rows = pl.ds(0, half), pl.ds(half, half)

    def share(block, rows, device):
        return wires.send(profiles.at[block, rows], profiles.at[block, rows], device)

    def share_whole(block, device):
        return wires.send(profiles.at[block], profiles.at[block], device)

    right, left, twin = away("x", 1), away("x", 3), away("c", 1)
    right_low = share(own, low_rows, right)
    left_high = share(own, high_rows, left)
    twin_own = share_whole(own, twin)
    right_high = share(own, high_rows, right)
    left_low = share(own, low_rows, left)

    mine[0:3, :] = jnp.zeros((3, COLS), jnp.float32)
    for b in range(BLOCKS):
        loads[b].wait()

        @pl.loop(0, COLS // LANES)
        def _(j, b=b):
            rows = pl.ds(b * LANES, LANES)
            lanes = pl.ds(pl.multiple_of(j * LANES, LANES), LANES)
            e = jnp.exp(grown[rows, lanes])
            grown[rows, lanes] = e
            mine[0:1, lanes] += jnp.sum(e, axis=0, keepdims=True)
            mine[1:2, lanes] += jnp.sum(e * gate[rows, :], axis=0, keepdims=True)

    load_truth.wait()
    truth_all[...] = slab[...].T
    truth = truth_all.at[pl.ds(pl.multiple_of(lax.rem(cell, 2) * PIECE, PIECE), PIECE), :]
    held = truth[...]
    mine[2:3, :] = jnp.sum(held * held, axis=0, keepdims=True)

    near = [wires.send(mine, near_stats.at[d - 1], away("y", d)) for d in (1, 2, 3)]
    save_grown = pltpu.make_async_copy(grown, grown_out, local_sems.at[0])
    save_grown.start()
    for copy in near:
        copy.wait_recv()
    far_stats[0] = mine[...] + near_stats[0] + near_stats[1] + near_stats[2]
    far = [wires.send(far_stats.at[0], far_stats.at[d], away("z", d)) for d in range(1, 8)]
    right_low.wait_recv()
    onward_low = share(own_of(x, 3, c), low_rows, right)
    left_high.wait_recv()
    onward_high = share(own_of(x, 1, c), high_rows, left)
    for copy in far:
        copy.wait_recv()
    total = far_stats[0]
    for d in range(1, 8):
        total = total + far_stats[d]
    stats_out[...] = total
    scale = 1.0 / total[0:1, :]

    @pl.loop(0, BLOCKS)
    def _(b):
        rows = pl.ds(pl.multiple_of(b * LANES, LANES), LANES)
        for j in range(COLS // LANES):
            lanes = pl.ds(j * LANES, LANES)
            weights[rows, lanes] = (
                grown[rows, lanes] * scale[:, j * LANES : (j + 1) * LANES] * gate[rows, :]
            ).astype(jnp.bfloat16)

    save_weights = pltpu.make_async_copy(weights, weights_out, local_sems.at[1])
    save_weights.start()
    save_truth = pltpu.make_async_copy(truth, truth_out, local_sems.at[2])
    save_truth.start()

    def multiply(block):
        turned[...] = profiles[block].T

        @pl.loop(0, COLS // OWN)
        def _(j):
            lanes = pl.ds(pl.multiple_of(j * OWN, OWN), OWN)
            part[block, :, lanes] = jnp.dot(
                turned[...], weights[:, lanes], preferred_element_type=jnp.float32
            )

    sought = [ring(z, d, 8) for d in (4, 3, 5, 2, 6, 1, 7, 0)]
    order = [own, own_of(x, 0, 1 - c)] + [jnp.int32(0)] * 6
    at = jnp.int32(2)
    for block in sought:
        other = jnp.where(block // 2 != x, 1, 0)
        for i in range(2, 8):
            order[i] = order[i] + block * other * jnp.where(at == i, 1, 0)
        at = at + other

    B = pl.ds(SPLIT, NEARBY)
    y_up, y_down, z_up, z_down = away("y", 1), away("y", 3), away("z", 1), away("z", 7)

    def piece(position, extra=0, size=PIECE):
        return pl.ds(pl.multiple_of(position * PIECE, PIECE) + extra, size)

    hop = PIECE // 2
    started, passed = {}, {}

    def y_start(i):
        s, p = order[i], ring(y, 2, 4)
        started[i] = (
            wires.send(part.at[s, piece(p, 0, hop), B], half_y.at[i, 0], y_up),
            wires.send(part.at[s, piece(p, hop, hop), B], half_y.at[i, 1], y_down),
        )

    def y_pass(i):
        s, up, down = order[i], ring(y, 1, 4), ring(y, 3, 4)
        started[i][0].wait_recv()
        part[s, piece(up, 0, hop), B] += half_y[i, 0]
        first = wires.send(part.at[s, piece(up), B], full_y.at[i, 0], y_up)
        started[i][1].wait_recv()
        part[s, piece(down, hop, hop), B] += half_y[i, 1]
        second = wires.send(part.at[s, piece(down), B], full_y.at[i, 1], y_down)
        passed[i] = (first, second)

    def y_end(i):
        passed[i][0].wait_recv()
        passed[i][1].wait_recv()
        part[order[i], piece(y), B] += full_y[i, 0] + full_y[i, 1]

    bz = {}

    def bz_start():
        d = ring(z, 4, 8)
        bz[0] = (
            wires.send(part.at[d, piece(y, 0, hop), B], half_bz.at[0], z_up),
            wires.send(part.at[d, piece(y, hop, hop), B], half_bz.at[1], z_down),
        )

    def bz_pass(t):
        up, down = ring(z, 4 - t, 8), ring(z, t - 4, 8)
        bz[t - 1][0].wait_recv()
        if t == 1:
            part[up, piece(y, 0, hop), B] += half_bz[0]
        else:
            part[up, piece(y), B] += full_bz[t - 2, 0]
        first = wires.send(part.at[up, piece(y), B], full_bz.at[t - 1, 0], z_up)
        bz[t - 1][1].wait_recv()
        if t == 1:
            part[down, piece(y, hop, hop), B] += half_bz[1]
        else:
            part[down, piece(y), B] += full_bz[t - 2, 1]
        second = wires.send(part.at[down, piece(y), B], full_bz.at[t - 1, 1], z_down)
        bz[t] = (first, second)

    def bz_end():
        bz[3][0].wait_recv()
        bz[3][1].wait_recv()
        part[z, piece(y), B] += full_bz[2, 0] + full_bz[2, 1]

    az = {}

    def lanes_of(a):
        return pl.ds(a * LANES, LANES)

    def az_start(a):
        d, lanes = ring(z, 4, 8), lanes_of(a)
        az[a, 0] = (
            wires.send(part.at[d, pl.ds(0, LANES), lanes], half_az.at[a, 0], z_up),
            wires.send(part.at[d, pl.ds(LANES, LANES), lanes], half_az.at[a, 1], z_down),
        )

    def az_pass(a, t):
        up, down, lanes = ring(z, 4 - t, 8), ring(z, t - 4, 8), lanes_of(a)
        az[a, t - 1][0].wait_recv()
        if t == 1:
            part[up, pl.ds(0, LANES), lanes] += half_az[a, 0]
        else:
            part[up, :, lanes] += full_az[a, t - 2, 0]
        first = wires.send(part.at[up, :, lanes], full_az.at[a, t - 1, 0], z_up)
        az[a, t - 1][1].wait_recv()
        if t == 1:
            part[down, pl.ds(LANES, LANES), lanes] += half_az[a, 1]
        else:
            part[down, :, lanes] += full_az[a, t - 2, 1]
        second = wires.send(part.at[down, :, lanes], full_az.at[a, t - 1, 1], z_down)
        az[a, t] = (first, second)

    def az_end(a):
        az[a, 3][0].wait_recv()
        az[a, 3][1].wait_recv()
        part[z, :, lanes_of(a)] += full_az[a, 2, 0] + full_az[a, 2, 1]

    A = pl.ds(0, SPLIT)
    ay = {}

    def ay_start():
        p = ring(y, 2, 4)
        ay[0] = (
            wires.send(part.at[z, piece(p, 0, hop), A], half_ay.at[0], y_up),
            wires.send(part.at[z, piece(p, hop, hop), A], half_ay.at[1], y_down),
        )

    def ay_pass():
        up, down = ring(y, 1, 4), ring(y, 3, 4)
        ay[0][0].wait_recv()
        part[z, piece(up, 0, hop), A] += half_ay[0]
        first = wires.send(part.at[z, piece(up), A], full_ay.at[0], y_up)
        ay[0][1].wait_recv()
        part[z, piece(down, hop, hop), A] += half_ay[1]
        second = wires.send(part.at[z, piece(down), A], full_ay.at[1], y_down)
        ay[1] = (first, second)

    def ay_end():
        ay[1][0].wait_recv()
        ay[1][1].wait_recv()
        part[z, piece(y), A] += full_ay[0] + full_ay[1]

    multiply(own)
    y_start(0)
    twin_own.wait_recv()
    multiply(own_of(x, 0, 1 - c))
    y_start(1)
    y_pass(0)
    right_high.wait_recv()
    twin_left = share_whole(own_of(x, 3, c), twin)
    left_low.wait_recv()
    twin_right = share_whole(own_of(x, 1, c), twin)
    multiply(own_of(x, 3, c))
    multiply(own_of(x, 1, c))
    y_pass(1)
    twin_left.wait_recv()
    multiply(own_of(x, 3, 1 - c))
    twin_right.wait_recv()
    multiply(own_of(x, 1, 1 - c))
    onward_low.wait_recv()
    twin_low = share(own_of(x, 2, c), low_rows, twin)
    onward_high.wait_recv()
    twin_high = share(own_of(x, 2, c), high_rows, twin)
    multiply(own_of(x, 2, c))
    twin_low.wait_recv()
    twin_high.wait_recv()
    multiply(own_of(x, 2, 1 - c))
    save_profiles = pltpu.make_async_copy(profiles, profiles_out, local_sems.at[3])
    save_profiles.start()

    for a in range(GROUPS):
        az_start(a)
    y_start(2)
    y_end(0)
    y_start(3)
    y_end(1)
    y_pass(2)
    for a in range(GROUPS):
        az_pass(a, 1)
    y_start(4)
    y_pass(3)
    y_end(2)
    bz_start()
    y_start(5)
    y_pass(4)
    for a in range(GROUPS):
        az_pass(a, 2)
    y_end(3)
    y_start(6)
    y_pass(5)
    y_end(4)
    bz_pass(1)
    y_start(7)
    y_pass(6)
    for a in range(GROUPS):
        az_pass(a, 3)
    y_end(5)
    y_pass(7)
    y_end(6)
    bz_pass(2)
    for a in range(GROUPS):
        az_end(a)
    ay_start()
    y_end(7)
    bz_pass(3)
    ay_pass()
    bz_end()
    ay_end()
    pred_out[...] = part[z, piece(y), :]
    for save in (save_grown, save_weights, save_truth, save_profiles):
        save.wait()
    wires.close()


def own_of(x, step, c):
    return ring(x, step, 4) * 2 + c


FORWARD_COPIES = 3 + 7 + 5 + 2 + 4 + 32 + 8 + 8 * GROUPS + 4


def forward(logits, filters, expression, spatial):
    f32, bf16 = jnp.float32, jnp.bfloat16
    anywhere = pl.BlockSpec(memory_space=pl.ANY)
    inside = pl.BlockSpec(memory_space=pltpu.VMEM)
    return pl.pallas_call(
        forward_kernel,
        out_shape=(
            jax.ShapeDtypeStruct((PIECE, COLS), f32),
            jax.ShapeDtypeStruct((PIECE, COLS), f32),
            jax.ShapeDtypeStruct((4, COLS), f32),
            jax.ShapeDtypeStruct((ROWS, COLS), f32),
            jax.ShapeDtypeStruct((ROWS, COLS), bf16),
            jax.ShapeDtypeStruct((8, ROWS, OWN), bf16),
        ),
        in_specs=[anywhere, inside, anywhere, anywhere],
        out_specs=(inside, anywhere, inside, anywhere, anywhere, anywhere),
        scratch_shapes=[
            pltpu.VMEM((ROWS, COLS), f32),
            pltpu.VMEM((ROWS, COLS), bf16),
            pltpu.VMEM((8, ROWS, OWN), bf16),
            pltpu.VMEM((OWN, ROWS), bf16),
            pltpu.VMEM((8, OWN, COLS), f32),
            pltpu.VMEM((COLS, LANES), f32),
            pltpu.VMEM((LANES, COLS), f32),
            pltpu.VMEM((ROWS, LANES), f32),
            pltpu.VMEM((4, COLS), f32),
            pltpu.VMEM((3, 4, COLS), f32),
            pltpu.VMEM((8, 4, COLS), f32),
            pltpu.VMEM((8, 2, PIECE // 2, NEARBY), f32),
            pltpu.VMEM((8, 2, PIECE, NEARBY), f32),
            pltpu.VMEM((2, PIECE // 2, NEARBY), f32),
            pltpu.VMEM((3, 2, PIECE, NEARBY), f32),
            pltpu.VMEM((GROUPS, 2, LANES, LANES), f32),
            pltpu.VMEM((GROUPS, 3, 2, OWN, LANES), f32),
            pltpu.VMEM((2, PIECE // 2, SPLIT), f32),
            pltpu.VMEM((2, PIECE, SPLIT), f32),
            pltpu.SemaphoreType.DMA((FORWARD_COPIES,)),
            pltpu.SemaphoreType.DMA((FORWARD_COPIES,)),
            pltpu.SemaphoreType.DMA((BLOCKS + 2,)),
        ],
        compiler_params=pltpu.CompilerParams(
            collective_id=0, has_side_effects=True, vmem_limit_bytes=LIMIT
        ),
        name="forward",
    )(logits, filters, expression, spatial)


CLOSE = 384
REACH = (0, 1, 7, 2, 6, 3, 5, 4)


def spot_peer(step):
    place = lax.rem(lax.axis_index("x") * 2 + lax.axis_index("c") + step, 8)
    return {"x": place // 2, "c": lax.rem(place, 2)}


def backward_kernel(
    pred,
    truth,
    stats,
    member,
    prior,
    filters,
    target,
    grown_in,
    weights_in,
    profiles_in,
    logits_out,
    profile_out,
    filter_out,
    losses_out,
    grown,
    weights,
    profiles,
    grads,
    sums,
    xp,
    xc,
    far_in,
    dest_in,
    gate,
    board,
    slide_msgs,
    spot_near,
    spot_far,
    column_near,
    column_far,
    column_mine,
    filter_msgs,
    spot_mine,
    send_sems,
    recv_sems,
    local_sems,
):
    f32, bf16 = jnp.float32, jnp.bfloat16
    z, y = lax.axis_index("z"), lax.axis_index("y")
    x, c = lax.axis_index("x"), lax.axis_index("c")
    wires = Wires(send_sems, recv_sems)
    load_weights = pltpu.make_async_copy(weights_in, weights, local_sems.at[0])
    load_profiles = pltpu.make_async_copy(profiles_in, profiles, local_sems.at[1])
    load_grown = pltpu.make_async_copy(grown_in, grown, local_sems.at[2])
    load_weights.start()
    load_profiles.start()
    load_grown.start()
    targets = (
        [away("y", d) for d in (1, 2, 3)]
        + [away("z", d) for d in range(1, 8)]
        + [spot_peer(d) for d in range(1, 8)]
    )
    greet(targets)
    cells, spots, genes, slides = ROWS * 32, COLS * 8, PIECE * 32, 4
    gene_scale, spot_scale = 1.0 / (slides * genes), 1.0 / spots

    pv, tv = pred[...], truth[...]
    cross, square, tsquare = pv * tv, pv * pv, tv * tv
    spot_mine[0:1, :] = jnp.sum(cross, axis=0, keepdims=True)
    spot_mine[1:2, :] = jnp.sum(square, axis=0, keepdims=True)
    totals, filtered = stats[0:1, :], stats[1:2, :]
    density = filtered / totals
    lane = lax.broadcasted_iota(jnp.int32, (PIECE, LANES), 1)
    packed = jnp.zeros((PIECE, LANES), f32)
    for k in range(slides):
        inside = member[k : k + 1, :]
        for q, field in enumerate((cross, square, tsquare)):
            column = jnp.sum(field * inside, axis=1, keepdims=True)
            packed = packed + jnp.where(lane == q * 4 + k, column, 0.0)
    board[...] = jnp.zeros((LANES, LANES), f32)
    board[0:PIECE, :] = packed
    slide_msgs[0] = board[...].T[0:16, :]
    row_lane = lax.broadcasted_iota(jnp.int32, (1, LANES), 1)
    extra = jnp.zeros((1, LANES), f32)
    for k in range(slides):
        inside = member[k : k + 1, :]
        extra = extra + jnp.where(
            row_lane == k, jnp.sum(density * inside, axis=1, keepdims=True), 0.0
        )
        extra = extra + jnp.where(
            row_lane == 4 + k, jnp.sum(prior[...] * inside, axis=1, keepdims=True), 0.0
        )
    slide_msgs[0, 12:13, :] = extra
    greeted(targets)
    near = [wires.send(spot_mine, spot_near.at[d - 1], away("y", d)) for d in (1, 2, 3)]
    slide = [wires.send(slide_msgs.at[0], slide_msgs.at[d], spot_peer(d)) for d in range(1, 8)]
    for copy in near:
        copy.wait_recv()
    spot_far[0] = spot_mine[...] + spot_near[0] + spot_near[1] + spot_near[2]
    far = [wires.send(spot_far.at[0], spot_far.at[d], away("z", d)) for d in range(1, 8)]
    gates = jax.nn.sigmoid(filters[...])
    for b in range(BLOCKS):
        gate[pl.ds(b * LANES, LANES), :] = jnp.broadcast_to(
            gates[b : b + 1, :], (LANES, LANES)
        ).T
    for copy in slide:
        copy.wait_recv()
    slide_total = slide_msgs[0]
    for d in range(1, 8):
        slide_total = slide_total + slide_msgs[d]
    s_inner, s_square, s_truth = slide_total[0:4], slide_total[4:8], slide_total[8:12]
    left, right = lax.rsqrt(s_square + epsilon), lax.rsqrt(s_truth + epsilon)
    gene_cos = s_inner * left * right
    mine_genes = lax.broadcasted_iota(jnp.int32, (4, LANES), 1) < PIECE
    gene_sum = jnp.sum(jnp.where(mine_genes, gene_cos, 0.0), keepdims=True)
    board[...] = jnp.zeros((LANES, LANES), f32)
    board[0:4, :] = s_inner * left * left * left * right
    board[4:8, :] = left * right
    columns = board[...].T[0:PIECE, :]
    cube_of, flat_of = jnp.zeros((PIECE, COLS), f32), jnp.zeros((PIECE, COLS), f32)
    spot_density, spot_prior = jnp.zeros((1, COLS), f32), jnp.zeros((1, COLS), f32)
    for k in range(slides):
        inside = member[k : k + 1, :]
        cube_of = cube_of + columns[:, k : k + 1] * inside
        flat_of = flat_of + columns[:, 4 + k : 5 + k] * inside
        spot_density = spot_density + slide_total[12:13, k : k + 1] * inside
        spot_prior = spot_prior + slide_total[12:13, 4 + k : 5 + k] * inside
    share = prior[...] / spot_prior
    pred_share = density / spot_density
    density_part = jnp.sum(share * (jnp.log(share) - jnp.log(pred_share)), keepdims=True) / slides
    grad_density = (1.0 / spot_density - share / density) / slides
    gene_part = gene_scale * (cube_of * pv - flat_of * tv)

    for copy in far:
        copy.wait_recv()
    spot_total = spot_far[0]
    for d in range(1, 8):
        spot_total = spot_total + spot_far[d]
    p_inner, p_square = spot_total[0:1, :], spot_total[1:2, :]
    p_left, p_right = lax.rsqrt(p_square + epsilon), lax.rsqrt(stats[2:3, :] + epsilon)
    spot_sum = jnp.sum(p_inner * p_left * p_right, keepdims=True)
    spot_cube = p_inner * p_left * p_left * p_left * p_right
    grad = gene_part + spot_scale * (spot_cube * pv - (p_left * p_right) * tv)

    A, B, hop = pl.ds(0, CLOSE), pl.ds(CLOSE, COLS - CLOSE), PIECE // 2

    def piece(position, extra=0, size=PIECE):
        return pl.ds(pl.multiple_of(position * PIECE, PIECE) + extra, size)

    grads[z, piece(y), :] = grad.astype(bf16)
    y_up, y_down, z_up, z_down = away("y", 1), away("y", 3), away("z", 1), away("z", 7)

    def put(block, rows, lanes, device):
        view = grads.at[block, rows, lanes]
        return wires.send(view, view, device)

    def y_share(block, lanes):
        return put(block, piece(y), lanes, y_up), put(block, piece(y), lanes, y_down)

    def y_onward(block, lanes, shared):
        shared[0].wait_recv()
        up = put(block, piece(ring(y, 3, 4), 0, hop), lanes, y_up)
        shared[1].wait_recv()
        down = put(block, piece(ring(y, 1, 4), hop, hop), lanes, y_down)
        return up, down

    def both(copies):
        copies[0].wait_recv()
        copies[1].wait_recv()

    blocks = [ring(z, d, 8) for d in REACH]

    def z_share(step, rows, lanes):
        above, below = ring(z, 1 - step, 8), ring(z, step - 1, 8)
        first, second = rows
        return put(above, first, lanes, z_up), put(below, second, lanes, z_down)

    own_rows, all_rows = (piece(y), piece(y)), (pl.ds(0, OWN), pl.ds(0, OWN))
    own_halves = (piece(y, 0, hop), piece(y, hop, hop))
    all_halves = (pl.ds(0, LANES), pl.ds(LANES, LANES))

    half = ROWS // 2
    low_rows, high_rows = pl.ds(0, half), pl.ds(half, half)
    right_x, left_x, twin = away("x", 1), away("x", 3), away("c", 1)
    base = 96

    def link(source, to, device, at):
        return pltpu.make_async_remote_copy(
            src_ref=source,
            dst_ref=to,
            send_sem=send_sems.at[at],
            recv_sem=recv_sems.at[at],
            device_id=device,
            device_id_type=MESH,
        )

    def twin_link(n):
        return link(xp.at[n], xc.at[blocks[n] // 2], twin, base + n)

    def far_low(n):
        return link(xp.at[n, low_rows], far_in.at[0], right_x, base + 8)

    def far_high(n):
        return link(xp.at[n, high_rows], far_in.at[1], left_x, base + 9)

    def near_link(n, rows, side, at):
        device = right_x if side == 0 else left_x
        return link(xp.at[n, rows], dest_in.at[side, rows], device, base + at)

    CHUNK = 352

    def profile_part(n):
        block = blocks[n]

        @pl.loop(0, ROWS // CHUNK)
        def _(i):
            rows = pl.ds(pl.multiple_of(i * CHUNK, CHUNK), CHUNK)
            xp[n, rows, :] = lax.dot_general(
                weights[rows, :],
                grads[block],
                (((1,), (1,)), ((), ())),
                preferred_element_type=f32,
            )

    def cell_part(n):
        block = blocks[n]

        @pl.loop(0, COLS // OWN)
        def _(j):
            lanes = pl.ds(pl.multiple_of(j * OWN, OWN), OWN)
            product = jnp.dot(profiles[block], grads[block, :, lanes], preferred_element_type=f32)
            if n == 0:
                sums[:, lanes] = product
            else:
                sums[:, lanes] += product

    def is_mine(n):
        return lax.rem(blocks[n], 2) == c

    def distance(n):
        return ring(blocks[n] // 2 - x, 0, 4)

    def block_first(n):
        profile_part(n)

        @pl.when(jnp.logical_not(is_mine(n)))
        def _():
            twin_link(n).start()

    def block_second(n):
        @pl.when(is_mine(n))
        def _():
            twin_link(n).wait_recv()

            @pl.loop(0, BLOCKS)
            def _(b):
                rows = pl.ds(pl.multiple_of(b * LANES, LANES), LANES)
                xp[n, rows, :] += xc[blocks[n] // 2, rows, :]

            @pl.when(distance(n) == 2)
            def _():
                far_low(n).start()
                far_high(n).start()

            @pl.when(distance(n) == 1)
            def _():
                near_link(n, high_rows, 0, 10).start()

            @pl.when(distance(n) == 3)
            def _():
                near_link(n, low_rows, 1, 11).start()

    def block_third(n):
        @pl.when(is_mine(n))
        def _():
            @pl.when(distance(n) == 1)
            def _():
                far_low(n).wait_recv()

                @pl.loop(0, 4)
                def _(i):
                    rows = pl.ds(pl.multiple_of(i * (half // 4), 16), half // 4)
                    xp[n, rows, :] += far_in[0, rows, :]

                near_link(n, low_rows, 0, 12).start()

            @pl.when(distance(n) == 3)
            def _():
                far_high(n).wait_recv()

                @pl.loop(0, 4)
                def _(i):
                    rows = pl.ds(pl.multiple_of(i * (half // 4), 16), half // 4)
                    more = pl.ds(pl.multiple_of(half + i * (half // 4), 16), half // 4)
                    xp[n, more, :] += far_in[1, rows, :]

                near_link(n, high_rows, 1, 13).start()

    bz = {1: z_share(1, own_rows, B)}
    shared_a = y_share(z, A)
    shared_b = {0: y_share(z, B)}
    onward_a = y_onward(z, A, shared_a)
    onward_b = {0: y_onward(z, B, shared_b[0])}
    both(onward_a)
    az = {1: z_share(1, all_rows, A)}
    both(onward_b[0])
    load_weights.wait()
    load_profiles.wait()
    load_grown.wait()
    block_first(0)
    cell_part(0)
    for step in (1, 2, 3, 4):
        ns = (2 * step - 1, 2 * step) if step < 4 else (7,)
        both(bz[step])
        if step < 4:
            bz[step + 1] = z_share(step + 1, own_rows if step < 3 else own_halves, B)
        for n in ns:
            shared_b[n] = y_share(blocks[n], B)
        both(az[step])
        if step < 4:
            az[step + 1] = z_share(step + 1, all_rows if step < 3 else all_halves, A)
        if step == 1:
            block_second(0)
        else:
            block_second(2 * step - 3)
            block_second(2 * step - 2)
        for n in ns:
            onward_b[n] = y_onward(blocks[n], B, shared_b[n])
        if step == 2:
            block_third(0)
        if step > 2:
            block_third(2 * step - 5)
            block_third(2 * step - 4)
        for n in ns:
            both(onward_b[n])
            block_first(n)
        for n in ns:
            cell_part(n)
    block_second(7)
    block_third(5)
    block_third(6)

    scale = 1.0 / totals
    column_mine[...] = jnp.zeros((2, COLS), f32)
    lane_row = lax.broadcasted_iota(jnp.int32, (1, COLS), 1)
    column_mine[1:2, :] = jnp.where(lane_row == 0, gene_sum, 0.0)
    for b in range(BLOCKS):
        rows = pl.ds(b * LANES, LANES)
        across = jnp.zeros((LANES, LANES), f32)
        for j in range(COLS // LANES):
            lanes = pl.ds(j * LANES, LANES)
            cut = slice(j * LANES, (j + 1) * LANES)
            whole = (grown[rows, lanes] * scale[:, cut]) * (sums[rows, lanes] + grad_density[:, cut])
            sums[rows, lanes] = whole
            across = across + whole
            column_mine[0:1, lanes] += jnp.sum(whole * gate[rows, :], axis=0, keepdims=True)
        filter_msgs[0, b : b + 1, :] = jnp.sum(across.T, axis=0, keepdims=True)
    filter_msgs[0, 11:12, :] = jnp.where(
        row_lane == 0, spot_sum, jnp.where(row_lane == 1, density_part, 0.0)
    )
    filter_msgs[0, 12:16, :] = jnp.zeros((4, LANES), f32)
    near = [wires.send(column_mine, column_near.at[d - 1], away("y", d)) for d in (1, 2, 3)]
    spread = [wires.send(filter_msgs.at[0], filter_msgs.at[d], spot_peer(d)) for d in range(1, 8)]
    for copy in near:
        copy.wait_recv()
    column_far[0] = column_mine[...] + column_near[0] + column_near[1] + column_near[2]
    far = [wires.send(column_far.at[0], column_far.at[d], away("z", d)) for d in range(1, 8)]
    block_third(7)
    for copy in far:
        copy.wait_recv()
    column_total = column_far[0]
    for d in range(1, 8):
        column_total = column_total + column_far[d]
    saves = []
    dot_scale = column_total[0:1, :] * scale
    for b in range(BLOCKS):
        rows = pl.ds(b * LANES, LANES)
        for j in range(COLS // LANES):
            lanes = pl.ds(j * LANES, LANES)
            cut = slice(j * LANES, (j + 1) * LANES)
            sums[rows, lanes] = (
                gate[rows, :] * sums[rows, lanes] - grown[rows, lanes] * dot_scale[:, cut]
            )
        save = pltpu.make_async_copy(
            sums.at[rows, :], logits_out.at[rows, :], local_sems.at[3 + b]
        )
        save.start()
        saves.append(save)
    for copy in spread:
        copy.wait_recv()
    filter_total = filter_msgs[0]
    for d in range(1, 8):
        filter_total = filter_total + filter_msgs[d]
    kept = stats[3:4, 0:1]
    spread_sum = stats[3:4, 1:2]
    gap = kept - target[...]
    root = jnp.sqrt(gap * gap + 1.0)
    on = filter_total[0:BLOCKS, :] + gap / root / cells + (1.0 - 2.0 * gates) / cells
    filter_out[...] = on * gates * (1.0 - gates)
    values = (
        -column_total[1:2, 0:1] * gene_scale,
        -filter_total[11:12, 0:1] * spot_scale,
        filter_total[11:12, 1:2],
        root / cells,
        spread_sum / cells,
    )
    losses = jnp.zeros((1, LANES), f32)
    for k, value in enumerate(values):
        losses = losses + jnp.where(row_lane == k, value, 0.0)
    losses_out[...] = losses

    mine_at = jnp.int32(0)
    for n in range(8):
        here = jnp.logical_and(is_mine(n), distance(n) == 0)
        mine_at = mine_at + jnp.where(here, n, 0)
    near_link(0, high_rows, 0, 10).wait_recv()
    near_link(0, low_rows, 1, 11).wait_recv()
    near_link(0, low_rows, 0, 12).wait_recv()
    near_link(0, high_rows, 1, 13).wait_recv()

    @pl.loop(0, BLOCKS)
    def _(b):
        rows = pl.ds(pl.multiple_of(b * LANES, LANES), LANES)
        profile_out[rows, :] = xp[mine_at, rows, :] + dest_in[0, rows, :] + dest_in[1, rows, :]

    for n in range(8):

        @pl.when(jnp.logical_not(is_mine(n)))
        def _(n=n):
            twin_link(n).wait_send()

    far_low(0).wait_send()
    far_high(0).wait_send()
    near_link(0, high_rows, 0, 10).wait_send()
    near_link(0, low_rows, 1, 11).wait_send()
    near_link(0, low_rows, 0, 12).wait_send()
    near_link(0, high_rows, 1, 13).wait_send()
    for save in saves:
        save.wait()
    wires.close()


def backward(pred, truth, stats, member, prior, filters, target, grown, weights, profiles):
    f32, bf16 = jnp.float32, jnp.bfloat16
    anywhere = pl.BlockSpec(memory_space=pl.ANY)
    inside = pl.BlockSpec(memory_space=pltpu.VMEM)
    count = 110
    return pl.pallas_call(
        backward_kernel,
        out_shape=(
            jax.ShapeDtypeStruct((ROWS, COLS), f32),
            jax.ShapeDtypeStruct((ROWS, OWN), f32),
            jax.ShapeDtypeStruct((BLOCKS, LANES), f32),
            jax.ShapeDtypeStruct((1, LANES), f32),
        ),
        in_specs=[inside] * 7 + [anywhere] * 3,
        out_specs=(anywhere, inside, inside, inside),
        scratch_shapes=[
            pltpu.VMEM((ROWS, COLS), f32),
            pltpu.VMEM((ROWS, COLS), bf16),
            pltpu.VMEM((8, ROWS, OWN), bf16),
            pltpu.VMEM((8, OWN, COLS), bf16),
            pltpu.VMEM((ROWS, COLS), f32),
            pltpu.VMEM((8, ROWS, OWN), f32),
            pltpu.VMEM((4, ROWS, OWN), f32),
            pltpu.VMEM((2, ROWS // 2, OWN), f32),
            pltpu.VMEM((2, ROWS, OWN), f32),
            pltpu.VMEM((ROWS, LANES), f32),
            pltpu.VMEM((LANES, LANES), f32),
            pltpu.VMEM((8, 16, LANES), f32),
            pltpu.VMEM((3, 2, COLS), f32),
            pltpu.VMEM((8, 2, COLS), f32),
            pltpu.VMEM((3, 2, COLS), f32),
            pltpu.VMEM((8, 2, COLS), f32),
            pltpu.VMEM((2, COLS), f32),
            pltpu.VMEM((8, 16, LANES), f32),
            pltpu.VMEM((2, COLS), f32),
            pltpu.SemaphoreType.DMA((count,)),
            pltpu.SemaphoreType.DMA((count,)),
            pltpu.SemaphoreType.DMA((BLOCKS + 3,)),
        ],
        compiler_params=pltpu.CompilerParams(
            collective_id=1, has_side_effects=True, vmem_limit_bytes=LIMIT
        ),
        name="backward",
    )(pred, truth, stats, member, prior, filters, target, grown, weights, profiles)


def on_device(logits, filter_logits, expression, spatial, prior, slide_sizes, target):
    cols = logits.shape[1]
    first = (lax.axis_index("x") * 2 + lax.axis_index("c")) * cols
    positions = first + jnp.arange(cols, dtype=jnp.int32)
    ends = jnp.cumsum(slide_sizes)
    starts = ends - slide_sizes
    member = jnp.logical_and(
        positions[None, :] >= starts[:, None], positions[None, :] < ends[:, None]
    ).astype(jnp.float32)
    filters = filter_logits.reshape(BLOCKS, LANES)
    pred, truth, stats, grown, weights, profiles = forward(logits, filters, expression, spatial)
    grad_logits, grad_expression, grad_filter, losses = backward(
        pred,
        truth,
        stats,
        member,
        prior.reshape(1, cols),
        filters,
        target.astype(jnp.float32).reshape(1, 1),
        grown,
        weights,
        profiles,
    )
    return (losses[0, :5], pred.T, grad_logits, grad_filter.reshape(-1), grad_expression)


def solution(mesh):
    split = Mesh(mesh.devices.reshape(8, 4, 4, 2), ("z", "y", "x", "c"))
    return jax.shard_map(
        on_device,
        mesh=split,
        in_specs=(P(CELL, SPOT), P(CELL), P(CELL, SPOT), P(SPOT, None), P(SPOT), P(), P()),
        out_specs=(P(), P(SPOT, CELL), P(CELL, SPOT), P(CELL), P(CELL, SPOT)),
        check_vma=False,
    )
```

```python
import jax
import jax.numpy as jnp
from jax import lax
from jax.experimental import pallas as pl
from jax.experimental.pallas import tpu as pltpu
from jax.sharding import Mesh
from jax.sharding import PartitionSpec as P

CELL = ("z", "y")
SPOT = ("x", "c")
SIZE = {"z": 8, "y": 4, "x": 4, "c": 2}
MESH = pl.DeviceIdType.MESH
ROWS = 1408
COLS = 1024
OWN = 256
PIECE = 64
LANES = 128
BLOCKS = ROWS // LANES
SLIDES = 4
GENES = PIECE * 32
CELLS = ROWS * 32
SPOTS = COLS * 8
HALF = ROWS // 2
HOP = PIECE // 2
QUARTER = HALF // 4
TOP = 32767.0
SPLIT = 384
GROUPS = SPLIT // LANES
CLOSE = 384
REACH = (0, 1, 7, 2, 6, 3, 5, 4)
COPIES = 320
LIMIT = 62 * 1024 * 1024

epsilon = 1e-06


def ring(position, step, size):
    return lax.rem(position + step + size, size)


def away(axis, step):
    return {axis: ring(lax.axis_index(axis), step, SIZE[axis])}


def spot_peer(step):
    place = lax.rem(lax.axis_index("x") * 2 + lax.axis_index("c") + step, 8)
    return {"x": place // 2, "c": lax.rem(place, 2)}


def block_of(x, step, c):
    return ring(x, step, 4) * 2 + c


def lanes_of(j, size=LANES):
    if isinstance(j, int):
        return pl.ds(j * size, size)
    return pl.ds(pl.multiple_of(j * size, size), size)


def piece(position, extra=0, size=PIECE):
    return pl.ds(pl.multiple_of(position * PIECE, PIECE) + extra, size)


def rows_in(block, extra=0, size=OWN):
    return pl.ds(pl.multiple_of(block * OWN, OWN) + extra, size)


def rows_of(block, position, extra=0, size=PIECE):
    return pl.ds(pl.multiple_of(block * OWN + position * PIECE, PIECE) + extra, size)


class Wires:
    def __init__(self, send_sems, recv_sems):
        self.send_sems, self.recv_sems, self.used, self.sent = send_sems, recv_sems, 0, []

    def take(self, count=1):
        at = self.used
        self.used += count
        return at

    def link(self, source, target, device, at):
        return pltpu.make_async_remote_copy(
            src_ref=source,
            dst_ref=target,
            send_sem=self.send_sems.at[at],
            recv_sem=self.recv_sems.at[at],
            device_id=device,
            device_id_type=MESH,
        )

    def send(self, source, target, device):
        copy = self.link(source, target, device, self.take())
        copy.start()
        self.sent.append(copy)
        return copy

    def close(self):
        for copy in self.sent:
            copy.wait_send()
        self.sent = []


def both(copies):
    copies[0].wait_recv()
    copies[1].wait_recv()


def step_kernel(
    sizes,
    target,
    logits,
    filters,
    expression,
    spatial,
    prior,
    pred_out,
    logits_out,
    profile_out,
    filter_out,
    losses_out,
    grown,
    weights,
    profiles,
    part,
    slab,
    truth_all,
    gate,
    member,
    board,
    mine,
    near_stats,
    far_stats,
    half_y,
    full_y,
    half_bz,
    full_bz,
    half_az,
    full_az,
    half_ay,
    full_ay,
    grads,
    xp,
    xc,
    coded_out,
    coded_in,
    scale_out,
    scale_in,
    slide_msgs,
    spot_mine,
    spot_near,
    spot_far,
    column_mine,
    column_near,
    column_far,
    filter_msgs,
    send_sems,
    recv_sems,
    local_sems,
):
    f32, bf16 = jnp.float32, jnp.bfloat16
    z, y = lax.axis_index("z"), lax.axis_index("y")
    x, c = lax.axis_index("x"), lax.axis_index("c")
    wires = Wires(send_sems, recv_sems)
    own = x * 2 + c
    cell = z * 4 + y
    right, left, twin = away("x", 1), away("x", 3), away("c", 1)
    y_up, y_down, z_up, z_down = away("y", 1), away("y", 3), away("z", 1), away("z", 7)

    loads = []
    for b in range(BLOCKS):
        rows = lanes_of(b)
        loads.append(
            pltpu.make_async_copy(logits.at[rows, :], grown.at[rows, :], local_sems.at[b])
        )
    load_own = pltpu.make_async_copy(expression, profiles.at[own], local_sems.at[BLOCKS])
    aligned = pl.multiple_of((cell // 2) * LANES, LANES)
    load_truth = pltpu.make_async_copy(
        spatial.at[:, pl.ds(aligned, LANES)], slab, local_sems.at[BLOCKS + 1]
    )
    load_own.start()
    for load in loads:
        load.start()
    load_truth.start()
    barrier = pltpu.get_barrier_semaphore()
    targets = (
        [away("y", d) for d in (1, 2, 3)]
        + [away("z", d) for d in range(1, 8)]
        + [spot_peer(d) for d in range(1, 8)]
    )
    for device in targets:
        pl.semaphore_signal(barrier, inc=1, device_id=device, device_id_type=MESH)
    gates = jax.nn.sigmoid(filters[...])
    for b in range(BLOCKS):
        gate[lanes_of(b), :] = jnp.broadcast_to(gates[b : b + 1, :], (LANES, LANES)).T
    kept = jnp.sum(gates, keepdims=True)
    spread = jnp.sum(gates - gates * gates, keepdims=True)
    column = lax.broadcasted_iota(jnp.int32, (1, COLS), 1)
    mine[3:4, :] = jnp.where(column == 0, kept, jnp.where(column == 1, spread, 0.0))
    mine[0:3, :] = jnp.zeros((3, COLS), f32)
    spot = column + own * COLS
    begin = jnp.int32(0)
    for k in range(SLIDES):
        end = begin + sizes[k]
        within = jnp.logical_and(spot >= begin, spot < end)
        member[k : k + 1, :] = jnp.where(within, 1.0, 0.0)
        begin = end

    load_own.wait()
    with jax.named_scope("greeting"):
        pl.semaphore_wait(barrier, len(targets))
    low_rows, high_rows = pl.ds(0, HALF), pl.ds(HALF, HALF)

    def share(block, rows, device):
        return wires.send(profiles.at[block, rows], profiles.at[block, rows], device)

    def share_whole(block, device):
        return wires.send(profiles.at[block], profiles.at[block], device)

    right_low = share(own, low_rows, right)
    left_high = share(own, high_rows, left)
    twin_own = share_whole(own, twin)
    right_high = share(own, high_rows, right)
    left_low = share(own, low_rows, left)

    with jax.named_scope("exponentials"):
        for b in range(BLOCKS):
            loads[b].wait()

            @pl.loop(0, COLS // LANES)
            def _(j, b=b):
                rows, lanes = lanes_of(b), lanes_of(j)
                e = jnp.exp(grown[rows, lanes])
                grown[rows, lanes] = e
                mine[0:1, lanes] += jnp.sum(e, axis=0, keepdims=True)
                mine[1:2, lanes] += jnp.sum(e * gate[rows, :], axis=0, keepdims=True)

    with jax.named_scope("truth"):
        load_truth.wait()
        truth_all[...] = slab[...].T
        truth = truth_all.at[piece(lax.rem(cell, 2)), :]
        held = truth[...]
        mine[2:3, :] = jnp.sum(held * held, axis=0, keepdims=True)

    with jax.named_scope("totals_y"):
        near = [wires.send(mine, near_stats.at[d - 1], away("y", d)) for d in (1, 2, 3)]
        for copy in near:
            copy.wait_recv()
        far_stats[0] = mine[...] + near_stats[0] + near_stats[1] + near_stats[2]
        far = [wires.send(far_stats.at[0], far_stats.at[d], away("z", d)) for d in range(1, 8)]
    with jax.named_scope("pass_halves"):
        right_low.wait_recv()
        onward_low = share(block_of(x, 3, c), low_rows, right)
        left_high.wait_recv()
        onward_high = share(block_of(x, 1, c), high_rows, left)
    with jax.named_scope("totals_z"):
        for copy in far:
            copy.wait_recv()
        stats = far_stats[0]
        for d in range(1, 8):
            stats = stats + far_stats[d]
    totals, filtered, truth_square = stats[0:1, :], stats[1:2, :], stats[2:3, :]
    kept, spread = stats[3:4, 0:1], stats[3:4, 1:2]
    density = filtered / totals
    scale = 1.0 / totals

    with jax.named_scope("weights"):

        @pl.loop(0, BLOCKS)
        def _(b):
            rows = lanes_of(b)
            for j in range(COLS // LANES):
                cut = slice(j * LANES, (j + 1) * LANES)
                weights[rows, lanes_of(j)] = (
                    grown[rows, lanes_of(j)] * scale[:, cut] * gate[rows, :]
                ).astype(bf16)

    def multiply(block):
        part[rows_in(block), :] = lax.dot_general(
            profiles[block], weights[...], (((0,), (0,)), ((), ())), preferred_element_type=f32
        )

    sought = [ring(z, d, 8) for d in (4, 3, 5, 2, 6, 1, 7, 0)]
    order = [own, block_of(x, 0, 1 - c)] + [jnp.int32(0)] * 6
    at = jnp.int32(2)
    for block in sought:
        other = jnp.where(block // 2 != x, 1, 0)
        for i in range(2, 8):
            order[i] = order[i] + block * other * jnp.where(at == i, 1, 0)
        at = at + other
    A, B = pl.ds(0, SPLIT), pl.ds(SPLIT, COLS - SPLIT)
    started, passed = {}, {}

    def y_start(i):
        s, p = order[i], ring(y, 2, 4)
        started[i] = (
            wires.send(part.at[rows_of(s, p, 0, HOP), B], half_y.at[i, 0], y_up),
            wires.send(part.at[rows_of(s, p, HOP, HOP), B], half_y.at[i, 1], y_down),
        )

    def y_pass(i):
        s, up, down = order[i], ring(y, 1, 4), ring(y, 3, 4)
        started[i][0].wait_recv()
        part[rows_of(s, up, 0, HOP), B] += half_y[i, 0]
        first = wires.send(part.at[rows_of(s, up), B], full_y.at[i, 0], y_up)
        started[i][1].wait_recv()
        part[rows_of(s, down, HOP, HOP), B] += half_y[i, 1]
        second = wires.send(part.at[rows_of(s, down), B], full_y.at[i, 1], y_down)
        passed[i] = (first, second)

    def y_end(i):
        both(passed[i])
        part[rows_of(order[i], y), B] += full_y[i, 0] + full_y[i, 1]

    bz, az, ay = {}, {}, {}

    def bz_start():
        d = ring(z, 4, 8)
        bz[0] = (
            wires.send(part.at[rows_of(d, y, 0, HOP), B], half_bz.at[0], z_up),
            wires.send(part.at[rows_of(d, y, HOP, HOP), B], half_bz.at[1], z_down),
        )

    def bz_pass(t):
        up, down = ring(z, 4 - t, 8), ring(z, t - 4, 8)
        bz[t - 1][0].wait_recv()
        if t == 1:
            part[rows_of(up, y, 0, HOP), B] += half_bz[0]
        else:
            part[rows_of(up, y), B] += full_bz[t - 2, 0]
        first = wires.send(part.at[rows_of(up, y), B], full_bz.at[t - 1, 0], z_up)
        bz[t - 1][1].wait_recv()
        if t == 1:
            part[rows_of(down, y, HOP, HOP), B] += half_bz[1]
        else:
            part[rows_of(down, y), B] += full_bz[t - 2, 1]
        second = wires.send(part.at[rows_of(down, y), B], full_bz.at[t - 1, 1], z_down)
        bz[t] = (first, second)

    def bz_end():
        both(bz[3])
        part[rows_of(z, y), B] += full_bz[2, 0] + full_bz[2, 1]

    def az_start(a):
        d, lanes = ring(z, 4, 8), lanes_of(a)
        az[a, 0] = (
            wires.send(part.at[rows_in(d, 0, LANES), lanes], half_az.at[a, 0], z_up),
            wires.send(part.at[rows_in(d, LANES, LANES), lanes], half_az.at[a, 1], z_down),
        )

    def az_pass(a, t):
        up, down, lanes = ring(z, 4 - t, 8), ring(z, t - 4, 8), lanes_of(a)
        az[a, t - 1][0].wait_recv()
        if t == 1:
            part[rows_in(up, 0, LANES), lanes] += half_az[a, 0]
        else:
            part[rows_in(up), lanes] += full_az[a, t - 2, 0]
        first = wires.send(part.at[rows_in(up), lanes], full_az.at[a, t - 1, 0], z_up)
        az[a, t - 1][1].wait_recv()
        if t == 1:
            part[rows_in(down, LANES, LANES), lanes] += half_az[a, 1]
        else:
            part[rows_in(down), lanes] += full_az[a, t - 2, 1]
        second = wires.send(part.at[rows_in(down), lanes], full_az.at[a, t - 1, 1], z_down)
        az[a, t] = (first, second)

    def az_end(a):
        both(az[a, 3])
        part[rows_in(z), lanes_of(a)] += full_az[a, 2, 0] + full_az[a, 2, 1]

    def ay_start():
        p = ring(y, 2, 4)
        ay[0] = (
            wires.send(part.at[rows_of(z, p, 0, HOP), A], half_ay.at[0], y_up),
            wires.send(part.at[rows_of(z, p, HOP, HOP), A], half_ay.at[1], y_down),
        )

    def ay_pass():
        up, down = ring(y, 1, 4), ring(y, 3, 4)
        ay[0][0].wait_recv()
        part[rows_of(z, up, 0, HOP), A] += half_ay[0]
        first = wires.send(part.at[rows_of(z, up), A], full_ay.at[0], y_up)
        ay[0][1].wait_recv()
        part[rows_of(z, down, HOP, HOP), A] += half_ay[1]
        second = wires.send(part.at[rows_of(z, down), A], full_ay.at[1], y_down)
        ay[1] = (first, second)

    def ay_end():
        both(ay[1])
        part[rows_of(z, y), A] += full_ay[0] + full_ay[1]

    def az_all(t):
        for a in range(GROUPS):
            az_pass(a, t)

    with jax.named_scope("multiply_near"):
        multiply(own)
        y_start(0)
        twin_own.wait_recv()
        multiply(order[1])
        y_start(1)
    with jax.named_scope("gather_rest"):
        right_high.wait_recv()
        twin_left = share_whole(block_of(x, 3, c), twin)
        left_low.wait_recv()
        twin_right = share_whole(block_of(x, 1, c), twin)
        y_pass(0)
        onward_low.wait_recv()
        twin_low = share(block_of(x, 2, c), low_rows, twin)
        onward_high.wait_recv()
        twin_high = share(block_of(x, 2, c), high_rows, twin)
        twin_left.wait_recv()
        twin_right.wait_recv()
        twin_low.wait_recv()
        twin_high.wait_recv()
    multiply(order[2])
    y_start(2)
    for a in range(GROUPS):
        az_start(a)
    y_pass(1)
    multiply(order[3])
    y_start(3)
    multiply(order[4])
    y_start(4)
    y_pass(2)
    az_all(1)
    multiply(order[5])
    y_start(5)
    y_pass(3)
    multiply(order[6])
    y_start(6)
    y_pass(4)
    multiply(order[7])
    y_start(7)
    y_end(0)
    y_end(1)
    az_all(2)
    y_end(2)
    bz_start()
    y_pass(5)
    y_end(3)
    y_pass(6)
    az_all(3)
    y_end(4)
    bz_pass(1)
    y_pass(7)
    y_end(5)
    y_end(6)
    bz_pass(2)
    for a in range(GROUPS):
        az_end(a)
    ay_start()
    y_end(7)
    bz_pass(3)
    ay_pass()
    bz_end()
    ay_end()

    gene_scale, spot_scale = 1.0 / (SLIDES * GENES), 1.0 / SPOTS
    with jax.named_scope("local_sums"):
        pv, tv = part[rows_of(z, y), :], truth[...]
        pred_out[...] = pv
        cross, square, tsquare = pv * tv, pv * pv, tv * tv
        spot_mine[0:1, :] = jnp.sum(cross, axis=0, keepdims=True)
        spot_mine[1:2, :] = jnp.sum(square, axis=0, keepdims=True)
        near = [wires.send(spot_mine, spot_near.at[d - 1], away("y", d)) for d in (1, 2, 3)]
        lane = lax.broadcasted_iota(jnp.int32, (PIECE, LANES), 1)
        row_lane = lax.broadcasted_iota(jnp.int32, (1, LANES), 1)
        packed, extra = jnp.zeros((PIECE, LANES), f32), jnp.zeros((1, LANES), f32)
        for k in range(SLIDES):
            inside = member[k : k + 1, :]
            for q, field in enumerate((cross, square, tsquare)):
                summed = jnp.sum(field * inside, axis=1, keepdims=True)
                packed = packed + jnp.where(lane == q * SLIDES + k, summed, 0.0)
            for q, field in enumerate((density, prior[...])):
                summed = jnp.sum(field * inside, axis=1, keepdims=True)
                extra = extra + jnp.where(row_lane == q * SLIDES + k, summed, 0.0)
        board[...] = jnp.zeros((LANES, LANES), f32)
        board[0:PIECE, :] = packed
        slide_msgs[0] = board[...].T[0:16, :]
        slide_msgs[0, 12:13, :] = extra
        slide = [wires.send(slide_msgs.at[0], slide_msgs.at[d], spot_peer(d)) for d in range(1, 8)]
    with jax.named_scope("spot_sums_y"):
        for copy in near:
            copy.wait_recv()
        spot_far[0] = spot_mine[...] + spot_near[0] + spot_near[1] + spot_near[2]
        far = [wires.send(spot_far.at[0], spot_far.at[d], away("z", d)) for d in range(1, 8)]
    with jax.named_scope("slide_sums"):
        for copy in slide:
            copy.wait_recv()
        slide_total = slide_msgs[0]
        for d in range(1, 8):
            slide_total = slide_total + slide_msgs[d]
        s_inner, s_square, s_truth = slide_total[0:4], slide_total[4:8], slide_total[8:12]
        s_left, s_right = lax.rsqrt(s_square + epsilon), lax.rsqrt(s_truth + epsilon)
        own_genes = lax.broadcasted_iota(jnp.int32, (SLIDES, LANES), 1) < PIECE
        gene_sum = jnp.sum(jnp.where(own_genes, s_inner * s_left * s_right, 0.0), keepdims=True)
        board[...] = jnp.zeros((LANES, LANES), f32)
        board[0:4, :] = s_inner * s_left * s_left * s_left * s_right
        board[4:8, :] = s_left * s_right
        columns = board[...].T[0:PIECE, :]
        cube_of, flat_of = jnp.zeros((PIECE, COLS), f32), jnp.zeros((PIECE, COLS), f32)
        spot_density, spot_prior = jnp.zeros((1, COLS), f32), jnp.zeros((1, COLS), f32)
        for k in range(SLIDES):
            inside = member[k : k + 1, :]
            cube_of = cube_of + columns[:, k : k + 1] * inside
            flat_of = flat_of + columns[:, 4 + k : 5 + k] * inside
            spot_density = spot_density + slide_total[12:13, k : k + 1] * inside
            spot_prior = spot_prior + slide_total[12:13, 4 + k : 5 + k] * inside
        target_share = prior[...] / spot_prior
        logs = jnp.log(target_share) - jnp.log(density / spot_density)
        density_part = jnp.sum(target_share * logs, keepdims=True) / SLIDES
        grad_density = (1.0 / spot_density - target_share / density) / SLIDES
        gene_part = gene_scale * (cube_of * pv - flat_of * tv)
    with jax.named_scope("spot_sums_z"):
        for copy in far:
            copy.wait_recv()
        spot_total = spot_far[0]
        for d in range(1, 8):
            spot_total = spot_total + spot_far[d]
        p_inner, p_square = spot_total[0:1, :], spot_total[1:2, :]
        p_left, p_right = lax.rsqrt(p_square + epsilon), lax.rsqrt(truth_square + epsilon)
        spot_sum = jnp.sum(p_inner * p_left * p_right, keepdims=True)
        spot_cube = p_inner * p_left * p_left * p_left * p_right
        grad = gene_part + spot_scale * (spot_cube * pv - (p_left * p_right) * tv)
        grads[z, piece(y), :] = grad.astype(bf16)
    with jax.named_scope("sends_done"):
        wires.close()

    A, B = pl.ds(0, CLOSE), pl.ds(CLOSE, COLS - CLOSE)
    blocks = [ring(z, d, 8) for d in REACH]

    def put(block, rows, lanes, device):
        view = grads.at[block, rows, lanes]
        return wires.send(view, view, device)

    def y_share(block, lanes):
        return put(block, piece(y), lanes, y_up), put(block, piece(y), lanes, y_down)

    def y_onward(block, lanes, shared):
        shared[0].wait_recv()
        up = put(block, piece(ring(y, 3, 4), 0, HOP), lanes, y_up)
        shared[1].wait_recv()
        down = put(block, piece(ring(y, 1, 4), HOP, HOP), lanes, y_down)
        return up, down

    def z_share(step, rows, lanes):
        above, below = ring(z, 1 - step, 8), ring(z, step - 1, 8)
        return put(above, rows[0], lanes, z_up), put(below, rows[1], lanes, z_down)

    own_rows, all_rows = (piece(y), piece(y)), (pl.ds(0, OWN), pl.ds(0, OWN))
    own_halves = (piece(y, 0, HOP), piece(y, HOP, HOP))
    all_halves = (pl.ds(0, LANES), pl.ds(LANES, LANES))
    base = wires.take(20)

    def each(turn, body):
        if turn in (0, 4):
            body(2 * turn - (turn > 0), ring(z, turn, 8))
        else:

            @pl.loop(0, 2)
            def _(i):
                body(2 * turn - 1 + i, ring(z, turn * (1 - 2 * i), 8))

    def twin_link(n, block):
        return wires.link(xp.at[n], xc.at[block // 2], twin, base + n)

    def half_device(k):
        return right if k in (0, 2, 3) else left

    def scale_link(k):
        return wires.link(scale_out.at[k], scale_in.at[k], half_device(k), base + 9 + 2 * k)

    def half_link(k, rows=pl.ds(0, HALF)):
        return wires.link(
            coded_out.at[k, rows], coded_in.at[k, rows], half_device(k), base + 8 + 2 * k
        )

    def quarter_rows(half, i):
        return pl.ds(pl.multiple_of(half * HALF + i * QUARTER, 16), QUARTER)

    def half_send(n, half, k):
        top = jnp.full((1, OWN), 1e-30, f32)
        for i in range(4):
            part_rows = xp[n, pl.ds(half * HALF + i * QUARTER, QUARTER), :]
            top = jnp.maximum(top, jnp.max(jnp.abs(part_rows), axis=0, keepdims=True))
        scale_out[k] = top * (1.0 / TOP)
        scale_link(k).start()
        up = TOP / top

        @pl.loop(0, 4)
        def _(i):
            coded_out[k, quarter_rows(0, i), :] = jnp.round(
                xp[n, quarter_rows(half, i), :] * up
            ).astype(jnp.int16)
            half_link(k, quarter_rows(0, i)).start()

    def half_value(k, i):
        return coded_in[k, quarter_rows(0, i), :].astype(f32) * scale_in[k]

    def half_arrived(k):
        scale_link(k).wait_recv()
        half_link(k).wait_recv()

    def is_mine(block):
        return lax.rem(block, 2) == c

    def distance(block):
        return ring(block // 2 - x, 0, 4)

    def block_first(n, block):
        xp[n] = lax.dot_general(
            weights[...],
            grads[block],
            (((1,), (1,)), ((), ())),
            preferred_element_type=f32,
        )

        @pl.when(jnp.logical_not(is_mine(block)))
        def _():
            twin_link(n, block).start()

    def cell_part(n, block):
        product = jnp.dot(profiles[block], grads[block], preferred_element_type=f32)
        if isinstance(n, int) and n == 0:
            part[0:ROWS, :] = product
        else:
            part[0:ROWS, :] += product

    def block_second(n, block):
        @pl.when(is_mine(block))
        def _():
            twin_link(n, block).wait_recv()

            @pl.loop(0, BLOCKS)
            def _(b):
                rows = lanes_of(b)
                xp[n, rows, :] += xc[block // 2, rows, :]

            @pl.when(distance(block) == 2)
            def _():
                half_send(n, 0, 0)
                half_send(n, 1, 1)

            @pl.when(distance(block) == 1)
            def _():
                half_send(n, 1, 2)

            @pl.when(distance(block) == 3)
            def _():
                half_send(n, 0, 4)

    def add_and_send(n, half, k, onward):
        half_arrived(k)

        @pl.loop(0, 4)
        def _(i):
            xp[n, quarter_rows(half, i), :] += half_value(k, i)

        half_send(n, half, onward)

    def block_third(n, block):
        @pl.when(is_mine(block))
        def _():
            @pl.when(distance(block) == 1)
            def _():
                add_and_send(n, 0, 0, 3)

            @pl.when(distance(block) == 3)
            def _():
                add_and_send(n, 1, 1, 5)

    bz = {1: z_share(1, own_rows, B)}
    shared_a = [put(z, piece(y), A, away("y", d)) for d in (1, 3, 2)]
    shared_b = {0: y_share(z, B)}
    for copy in shared_a:
        copy.wait_recv()
    az = {1: z_share(1, all_rows, A)}
    onward_b = {0: y_onward(z, B, shared_b[0])}
    both(onward_b[0])
    rounds = {0: (0,), 1: (1, 2), 2: (3, 4), 3: (5, 6), 4: (7,)}
    for step in (1, 2, 3, 4):
        both(bz[step])
        if step < 4:
            bz[step + 1] = z_share(step + 1, own_rows if step < 3 else own_halves, B)
        for n in rounds[step]:
            shared_b[n] = y_share(blocks[n], B)
        each(step - 1, block_first)
        both(az[step])
        if step < 4:
            az[step + 1] = z_share(step + 1, all_rows if step < 3 else all_halves, A)
        for n in rounds[step]:
            onward_b[n] = y_onward(blocks[n], B, shared_b[n])
        each(step - 1, cell_part)
        each(step - 1, block_second)
        if step > 2:
            each(step - 3, block_third)
        for n in rounds[step]:
            both(onward_b[n])
    each(4, block_first)
    each(4, cell_part)

    with jax.named_scope("column_sums"):
        column_mine[...] = jnp.zeros((2, COLS), f32)
        column_mine[1:2, :] = jnp.where(column == 0, gene_sum, 0.0)
        for b in range(BLOCKS):
            rows = lanes_of(b)
            across = jnp.zeros((LANES, LANES), f32)
            for j in range(COLS // LANES):
                lanes, cut = lanes_of(j), slice(j * LANES, (j + 1) * LANES)
                whole = (grown[rows, lanes] * scale[:, cut]) * (
                    part[rows, lanes] + grad_density[:, cut]
                )
                part[rows, lanes] = whole
                across = across + whole
                column_mine[0:1, lanes] += jnp.sum(whole * gate[rows, :], axis=0, keepdims=True)
            filter_msgs[0, b : b + 1, :] = jnp.sum(across.T, axis=0, keepdims=True)
        filter_msgs[0, 11:12, :] = jnp.where(
            row_lane == 0, spot_sum, jnp.where(row_lane == 1, density_part, 0.0)
        )
        filter_msgs[0, 12:16, :] = jnp.zeros((4, LANES), f32)
        near = [wires.send(column_mine, column_near.at[d - 1], away("y", d)) for d in (1, 2, 3)]
        sums = [wires.send(filter_msgs.at[0], filter_msgs.at[d], spot_peer(d)) for d in range(1, 8)]
    each(2, block_third)
    each(4, block_second)
    with jax.named_scope("column_sums_y"):
        for copy in near:
            copy.wait_recv()
        column_far[0] = column_mine[...] + column_near[0] + column_near[1] + column_near[2]
        far = [wires.send(column_far.at[0], column_far.at[d], away("z", d)) for d in range(1, 8)]
    each(3, block_third)
    with jax.named_scope("column_sums_z"):
        for copy in far:
            copy.wait_recv()
        column_total = column_far[0]
        for d in range(1, 8):
            column_total = column_total + column_far[d]
    saves = []
    with jax.named_scope("logits_gradient"):
        dot_scale = column_total[0:1, :] * scale
        for b in range(BLOCKS):
            rows = lanes_of(b)
            for j in range(COLS // LANES):
                lanes, cut = lanes_of(j), slice(j * LANES, (j + 1) * LANES)
                part[rows, lanes] = (
                    gate[rows, :] * part[rows, lanes] - grown[rows, lanes] * dot_scale[:, cut]
                )
            save = pltpu.make_async_copy(
                part.at[rows, :], logits_out.at[rows, :], local_sems.at[b]
            )
            save.start()
            saves.append(save)
    each(4, block_third)
    with jax.named_scope("filter_gradient"):
        for copy in sums:
            copy.wait_recv()
        filter_total = filter_msgs[0]
        for d in range(1, 8):
            filter_total = filter_total + filter_msgs[d]
        gap = kept - target[0].astype(f32)
        root = jnp.sqrt(gap * gap + 1.0)
        on = filter_total[0:BLOCKS, :] + gap / root / CELLS + (1.0 - 2.0 * gates) / CELLS
        filter_out[...] = on * gates * (1.0 - gates)
        values = (
            -column_total[1:2, 0:1] * gene_scale,
            -filter_total[11:12, 0:1] * spot_scale,
            filter_total[11:12, 1:2],
            root / CELLS,
            spread / CELLS,
        )
        losses = jnp.zeros((1, LANES), f32)
        for k, value in enumerate(values):
            losses = losses + jnp.where(row_lane == k, value, 0.0)
        losses_out[...] = losses

    mine_at = jnp.int32(0)
    for n in range(8):
        mine_at = mine_at + n * jnp.where(blocks[n] == own, 1, 0)
    with jax.named_scope("last_sums"):
        for half, (low, high) in ((0, (3, 4)), (1, (2, 5))):
            half_arrived(low)
            half_arrived(high)

            @pl.loop(0, 4)
            def _(i, half=half, low=low, high=high):
                xp[mine_at, quarter_rows(half, i), :] += half_value(low, i) + half_value(high, i)

        save = pltpu.make_async_copy(xp.at[mine_at], profile_out, local_sems.at[BLOCKS])
        save.start()
        saves.append(save)
    with jax.named_scope("twin_done"):
        for n in range(8):

            @pl.when(jnp.logical_not(is_mine(blocks[n])))
            def _(n=n):
                twin_link(n, blocks[n]).wait_send()

    with jax.named_scope("halves_done"):
        for k in range(6):
            half_link(k).wait_send()
            scale_link(k).wait_send()
    with jax.named_scope("saves_done"):
        for save in saves:
            save.wait()
    with jax.named_scope("wires_done"):
        wires.close()


def training_step(sizes, target, logits, filters, expression, spatial, prior):
    f32, bf16 = jnp.float32, jnp.bfloat16
    anywhere = pl.BlockSpec(memory_space=pl.ANY)
    inside = pl.BlockSpec(memory_space=pltpu.VMEM)
    scalars = pl.BlockSpec(memory_space=pltpu.SMEM)
    near = COLS - SPLIT
    return pl.pallas_call(
        step_kernel,
        out_shape=(
            jax.ShapeDtypeStruct((PIECE, COLS), f32),
            jax.ShapeDtypeStruct((ROWS, COLS), f32),
            jax.ShapeDtypeStruct((ROWS, OWN), f32),
            jax.ShapeDtypeStruct((BLOCKS, LANES), f32),
            jax.ShapeDtypeStruct((1, LANES), f32),
        ),
        in_specs=[scalars, scalars, anywhere, inside, anywhere, anywhere, inside],
        out_specs=(inside, anywhere, anywhere, inside, inside),
        scratch_shapes=[
            pltpu.VMEM((ROWS, COLS), f32),
            pltpu.VMEM((ROWS, COLS), bf16),
            pltpu.VMEM((8, ROWS, OWN), bf16),
            pltpu.VMEM((GENES, COLS), f32),
            pltpu.VMEM((COLS, LANES), f32),
            pltpu.VMEM((LANES, COLS), f32),
            pltpu.VMEM((ROWS, LANES), f32),
            pltpu.VMEM((SLIDES, COLS), f32),
            pltpu.VMEM((LANES, LANES), f32),
            pltpu.VMEM((4, COLS), f32),
            pltpu.VMEM((3, 4, COLS), f32),
            pltpu.VMEM((8, 4, COLS), f32),
            pltpu.VMEM((8, 2, HOP, near), f32),
            pltpu.VMEM((8, 2, PIECE, near), f32),
            pltpu.VMEM((2, HOP, near), f32),
            pltpu.VMEM((3, 2, PIECE, near), f32),
            pltpu.VMEM((GROUPS, 2, LANES, LANES), f32),
            pltpu.VMEM((GROUPS, 3, 2, OWN, LANES), f32),
            pltpu.VMEM((2, HOP, SPLIT), f32),
            pltpu.VMEM((2, PIECE, SPLIT), f32),
            pltpu.VMEM((8, OWN, COLS), bf16),
            pltpu.VMEM((8, ROWS, OWN), f32),
            pltpu.VMEM((4, ROWS, OWN), f32),
            pltpu.VMEM((6, HALF, OWN), jnp.int16),
            pltpu.VMEM((6, HALF, OWN), jnp.int16),
            pltpu.VMEM((6, 1, OWN), f32),
            pltpu.VMEM((6, 1, OWN), f32),
            pltpu.VMEM((8, 16, LANES), f32),
            pltpu.VMEM((2, COLS), f32),
            pltpu.VMEM((3, 2, COLS), f32),
            pltpu.VMEM((8, 2, COLS), f32),
            pltpu.VMEM((2, COLS), f32),
            pltpu.VMEM((3, 2, COLS), f32),
            pltpu.VMEM((8, 2, COLS), f32),
            pltpu.VMEM((8, 16, LANES), f32),
            pltpu.SemaphoreType.DMA((COPIES,)),
            pltpu.SemaphoreType.DMA((COPIES,)),
            pltpu.SemaphoreType.DMA((BLOCKS + 2,)),
        ],
        compiler_params=pltpu.CompilerParams(
            collective_id=0, has_side_effects=True, vmem_limit_bytes=LIMIT
        ),
        name="training_step",
    )(sizes, target, logits, filters, expression, spatial, prior)


def on_device(logits, filter_logits, expression, spatial, prior, slide_sizes, target):
    pred, grad_logits, grad_expression, grad_filter, losses = training_step(
        slide_sizes,
        target,
        logits,
        filter_logits.reshape(BLOCKS, LANES),
        expression,
        spatial,
        prior.reshape(1, COLS),
    )
    return (losses[0, :5], pred.T, grad_logits, grad_filter.reshape(-1), grad_expression)


def solution(mesh):
    split = Mesh(mesh.devices.reshape(8, 4, 4, 2), ("z", "y", "x", "c"))
    return jax.shard_map(
        on_device,
        mesh=split,
        in_specs=(P(CELL, SPOT), P(CELL), P(CELL, SPOT), P(SPOT, None), P(SPOT), P(), P()),
        out_specs=(P(), P(SPOT, CELL), P(CELL, SPOT), P(CELL), P(CELL, SPOT)),
        check_vma=False,
    )
```

```python
import jax
import jax.numpy as jnp
from jax import lax
from jax.experimental import pallas as pl
from jax.experimental.pallas import tpu as pltpu
from jax.sharding import Mesh
from jax.sharding import PartitionSpec as P

CELL = ("z", "y")
SPOT = ("x", "c")
SIZE = {"z": 8, "y": 4, "x": 4, "c": 2}
MESH = pl.DeviceIdType.MESH
ROWS = 1408
COLS = 1024
OWN = 256
PIECE = 64
LANES = 128
BLOCKS = ROWS // LANES
SLIDES = 4
GENES = PIECE * 32
CELLS = ROWS * 32
SPOTS = COLS * 8
HALF = ROWS // 2
HOP = PIECE // 2
EIGHTH = HALF // 4
TOP = 32767.0
SPLIT = 384
GROUPS = SPLIT // LANES
CLOSE = 384
REACH = (0, 1, 7, 2, 6, 3, 5, 4)
COPIES, SPREADS = 81, 9
LIMIT = 52 * 1024 * 1024

epsilon = 1e-06


def ring(position, step, size):
    return lax.rem(position + step + size, size)


def away(axis, step):
    return {axis: ring(lax.axis_index(axis), step, SIZE[axis])}


def spot_peer(step):
    place = lax.rem(lax.axis_index("x") * 2 + lax.axis_index("c") + step, 8)
    return {"x": place // 2, "c": lax.rem(place, 2)}


def block_of(x, step, c):
    return ring(x, step, 4) * 2 + c


def lanes_of(j, size=LANES):
    if isinstance(j, int):
        return pl.ds(j * size, size)
    return pl.ds(pl.multiple_of(j * size, size), size)


def piece(position, extra=0, size=PIECE):
    return pl.ds(pl.multiple_of(position * PIECE, PIECE) + extra, size)


def rows_in(block, extra=0, size=OWN):
    return pl.ds(pl.multiple_of(block * OWN, OWN) + extra, size)


def rows_of(block, position, extra=0, size=PIECE):
    return pl.ds(pl.multiple_of(block * OWN + position * PIECE, PIECE) + extra, size)


class Wires:
    def __init__(self, send_sems, recv_sems):
        self.send_sems, self.recv_sems, self.sent = send_sems, recv_sems, []
        self.used, self.spreads = 0, 0

    def take(self, count=1):
        at = self.used
        self.used += count
        return at

    def link(self, source, target, device, at):
        return pltpu.make_async_remote_copy(
            src_ref=source,
            dst_ref=target,
            send_sem=self.send_sems.at[at],
            recv_sem=self.recv_sems.at[at],
            device_id=device,
            device_id_type=MESH,
        )

    def send(self, source, target, device):
        copy = self.link(source, target, device, self.take())
        copy.start()
        self.sent.append(copy)
        return copy

    def spread(self, source, targets, slots):
        at = COPIES + self.spreads
        self.spreads += 1
        for target, device in targets:
            self.link(source, target, device, at).start()
        whole = self.link(slots, slots, targets[0][1], at)
        self.sent.append(whole)
        return whole

    def close(self):
        assert self.used <= COPIES and self.spreads <= SPREADS
        for copy in self.sent:
            copy.wait_send()
        self.used, self.sent = 0, []


def both(copies):
    copies[0].wait_recv()
    copies[1].wait_recv()


def step_kernel(
    sizes,
    target,
    logits,
    filters,
    expression,
    spatial,
    prior,
    pred_out,
    part,
    profile_out,
    filter_out,
    losses_out,
    grown,
    weights,
    profiles,
    slab,
    truth_all,
    gate,
    member,
    board,
    mine,
    near_stats,
    far_stats,
    half_y,
    full_y,
    half_bz,
    full_bz,
    half_az,
    full_az,
    half_ay,
    full_ay,
    grads,
    xp,
    xc,
    ended,
    coded_out,
    coded_in,
    scale_out,
    scale_in,
    slide_msgs,
    spot_mine,
    spot_near,
    spot_far,
    column_mine,
    column_near,
    column_far,
    filter_msgs,
    send_sems,
    recv_sems,
    local_sems,
):
    f32, bf16 = jnp.float32, jnp.bfloat16
    z, y = lax.axis_index("z"), lax.axis_index("y")
    x, c = lax.axis_index("x"), lax.axis_index("c")
    wires = Wires(send_sems, recv_sems)
    own = x * 2 + c
    cell = z * 4 + y
    right, left, twin = away("x", 1), away("x", 3), away("c", 1)
    y_up, y_down, z_up, z_down = away("y", 1), away("y", 3), away("z", 1), away("z", 7)

    def spread_y(source, slots):
        return wires.spread(source, [(slots.at[d - 1], away("y", d)) for d in (1, 2, 3)], slots)

    def spread_z(slots):
        others = [(slots.at[d], away("z", d)) for d in range(1, 8)]
        return wires.spread(slots.at[0], others, slots.at[pl.ds(1, 7)])

    def spread_spot(slots):
        others = [(slots.at[d], spot_peer(d)) for d in range(1, 8)]
        return wires.spread(slots.at[0], others, slots.at[pl.ds(1, 7)])

    loads = []
    for b in range(BLOCKS):
        rows = lanes_of(b)
        loads.append(
            pltpu.make_async_copy(logits.at[rows, :], grown.at[rows, :], local_sems.at[b])
        )
    load_own = pltpu.make_async_copy(expression, profiles.at[own], local_sems.at[BLOCKS])
    aligned = pl.multiple_of((cell // 2) * LANES, LANES)
    load_truth = pltpu.make_async_copy(
        spatial.at[:, pl.ds(aligned, LANES)], slab, local_sems.at[BLOCKS + 1]
    )
    load_own.start()
    for load in loads:
        load.start()
    load_truth.start()
    barrier = pltpu.get_barrier_semaphore()
    targets = (
        [away("y", d) for d in (1, 2, 3)]
        + [away("z", d) for d in range(1, 8)]
        + [spot_peer(d) for d in range(1, 8)]
    )
    for device in targets:
        pl.semaphore_signal(barrier, inc=1, device_id=device, device_id_type=MESH)
    gates = jax.nn.sigmoid(filters[...])
    for b in range(BLOCKS):
        gate[lanes_of(b), :] = jnp.broadcast_to(gates[b : b + 1, :], (LANES, LANES)).T
    kept = jnp.sum(gates, keepdims=True)
    spread = jnp.sum(gates - gates * gates, keepdims=True)
    column = lax.broadcasted_iota(jnp.int32, (1, COLS), 1)
    mine[3:4, :] = jnp.where(column == 0, kept, jnp.where(column == 1, spread, 0.0))
    mine[0:3, :] = jnp.zeros((3, COLS), f32)
    spot = column + own * COLS
    begin = jnp.int32(0)
    for k in range(SLIDES):
        end = begin + sizes[k]
        within = jnp.logical_and(spot >= begin, spot < end)
        member[k : k + 1, :] = jnp.where(within, 1.0, 0.0)
        begin = end

    load_own.wait()
    with jax.named_scope("greeting"):
        pl.semaphore_wait(barrier, len(targets))
    low_rows, high_rows = pl.ds(0, HALF), pl.ds(HALF, HALF)

    def share(block, rows, device):
        return wires.send(profiles.at[block, rows], profiles.at[block, rows], device)

    def share_whole(block, device):
        return wires.send(profiles.at[block], profiles.at[block], device)

    right_low = share(own, low_rows, right)
    left_high = share(own, high_rows, left)
    twin_own = share_whole(own, twin)
    with jax.named_scope("exponentials"):
        for b in range(BLOCKS):
            loads[b].wait()

            @pl.loop(0, COLS // LANES)
            def _(j, b=b):
                rows, lanes = lanes_of(b), lanes_of(j)
                e = jnp.exp(grown[rows, lanes])
                grown[rows, lanes] = e
                mine[0:1, lanes] += jnp.sum(e, axis=0, keepdims=True)
                mine[1:2, lanes] += jnp.sum(e * gate[rows, :], axis=0, keepdims=True)

    with jax.named_scope("truth"):
        load_truth.wait()
        truth_all[...] = slab[...].T
        truth = truth_all.at[piece(lax.rem(cell, 2)), :]
        held = truth[...]
        mine[2:3, :] = jnp.sum(held * held, axis=0, keepdims=True)

    with jax.named_scope("totals_y"):
        near = spread_y(mine, near_stats)
        right_high = share(own, high_rows, right)
        left_low = share(own, low_rows, left)
        near.wait_recv()
        far_stats[0] = mine[...] + near_stats[0] + near_stats[1] + near_stats[2]
        far = spread_z(far_stats)
    with jax.named_scope("pass_halves"):
        right_low.wait_recv()
        onward_low = share(block_of(x, 3, c), low_rows, right)
        left_high.wait_recv()
        onward_high = share(block_of(x, 1, c), high_rows, left)
    with jax.named_scope("totals_z"):
        far.wait_recv()
        stats = far_stats[0]
        for d in range(1, 8):
            stats = stats + far_stats[d]
    totals, filtered, truth_square = stats[0:1, :], stats[1:2, :], stats[2:3, :]
    kept, spread = stats[3:4, 0:1], stats[3:4, 1:2]
    density = filtered / totals
    scale = 1.0 / totals

    with jax.named_scope("weights"):

        @pl.loop(0, BLOCKS)
        def _(b):
            rows = lanes_of(b)
            for j in range(COLS // LANES):
                cut = slice(j * LANES, (j + 1) * LANES)
                weights[rows, lanes_of(j)] = (
                    grown[rows, lanes_of(j)] * scale[:, cut] * gate[rows, :]
                ).astype(bf16)

    def multiply(block):
        part[rows_in(block), :] = lax.dot_general(
            profiles[block], weights[...], (((0,), (0,)), ((), ())), preferred_element_type=f32
        )

    sought = [ring(z, d, 8) for d in (4, 3, 5, 2, 6, 1, 7, 0)]
    order = [own, block_of(x, 0, 1 - c)] + [jnp.int32(0)] * 6
    at = jnp.int32(2)
    for block in sought:
        other = jnp.where(block // 2 != x, 1, 0)
        for i in range(2, 8):
            order[i] = order[i] + block * other * jnp.where(at == i, 1, 0)
        at = at + other
    A, B = pl.ds(0, SPLIT), pl.ds(SPLIT, COLS - SPLIT)
    started, passed = {}, {}

    def y_start(i):
        s, p = order[i], ring(y, 2, 4)
        started[i] = (
            wires.send(part.at[rows_of(s, p, 0, HOP), B], half_y.at[i, 0], y_up),
            wires.send(part.at[rows_of(s, p, HOP, HOP), B], half_y.at[i, 1], y_down),
        )

    def y_pass(i):
        s, up, down = order[i], ring(y, 1, 4), ring(y, 3, 4)
        started[i][0].wait_recv()
        part[rows_of(s, up, 0, HOP), B] += half_y[i, 0]
        first = wires.send(part.at[rows_of(s, up), B], full_y.at[i, 0], y_up)
        started[i][1].wait_recv()
        part[rows_of(s, down, HOP, HOP), B] += half_y[i, 1]
        second = wires.send(part.at[rows_of(s, down), B], full_y.at[i, 1], y_down)
        passed[i] = (first, second)

    def y_end(i):
        both(passed[i])
        part[rows_of(order[i], y), B] += full_y[i, 0] + full_y[i, 1]

    bz, az, ay = {}, {}, {}

    def bz_start():
        d = ring(z, 4, 8)
        bz[0] = (
            wires.send(part.at[rows_of(d, y, 0, HOP), B], half_bz.at[0], z_up),
            wires.send(part.at[rows_of(d, y, HOP, HOP), B], half_bz.at[1], z_down),
        )

    def bz_pass(t):
        up, down = ring(z, 4 - t, 8), ring(z, t - 4, 8)
        bz[t - 1][0].wait_recv()
        if t == 1:
            part[rows_of(up, y, 0, HOP), B] += half_bz[0]
        else:
            part[rows_of(up, y), B] += full_bz[t - 2, 0]
        first = wires.send(part.at[rows_of(up, y), B], full_bz.at[t - 1, 0], z_up)
        bz[t - 1][1].wait_recv()
        if t == 1:
            part[rows_of(down, y, HOP, HOP), B] += half_bz[1]
        else:
            part[rows_of(down, y), B] += full_bz[t - 2, 1]
        second = wires.send(part.at[rows_of(down, y), B], full_bz.at[t - 1, 1], z_down)
        bz[t] = (first, second)

    def bz_end():
        both(bz[3])
        part[rows_of(z, y), B] += full_bz[2, 0] + full_bz[2, 1]

    def az_start(a):
        d, lanes = ring(z, 4, 8), lanes_of(a)
        az[a, 0] = (
            wires.send(part.at[rows_in(d, 0, LANES), lanes], half_az.at[a, 0], z_up),
            wires.send(part.at[rows_in(d, LANES, LANES), lanes], half_az.at[a, 1], z_down),
        )

    def az_pass(a, t):
        up, down, lanes = ring(z, 4 - t, 8), ring(z, t - 4, 8), lanes_of(a)
        az[a, t - 1][0].wait_recv()
        if t == 1:
            part[rows_in(up, 0, LANES), lanes] += half_az[a, 0]
        else:
            part[rows_in(up), lanes] += full_az[a, t - 2, 0]
        first = wires.send(part.at[rows_in(up), lanes], full_az.at[a, t - 1, 0], z_up)
        az[a, t - 1][1].wait_recv()
        if t == 1:
            part[rows_in(down, LANES, LANES), lanes] += half_az[a, 1]
        else:
            part[rows_in(down), lanes] += full_az[a, t - 2, 1]
        second = wires.send(part.at[rows_in(down), lanes], full_az.at[a, t - 1, 1], z_down)
        az[a, t] = (first, second)

    def az_end(a):
        both(az[a, 3])
        part[rows_in(z), lanes_of(a)] += full_az[a, 2, 0] + full_az[a, 2, 1]

    def ay_start():
        p = ring(y, 2, 4)
        ay[0] = (
            wires.send(part.at[rows_of(z, p, 0, HOP), A], half_ay.at[0], y_up),
            wires.send(part.at[rows_of(z, p, HOP, HOP), A], half_ay.at[1], y_down),
        )

    def ay_pass():
        up, down = ring(y, 1, 4), ring(y, 3, 4)
        ay[0][0].wait_recv()
        part[rows_of(z, up, 0, HOP), A] += half_ay[0]
        first = wires.send(part.at[rows_of(z, up), A], full_ay.at[0], y_up)
        ay[0][1].wait_recv()
        part[rows_of(z, down, HOP, HOP), A] += half_ay[1]
        second = wires.send(part.at[rows_of(z, down), A], full_ay.at[1], y_down)
        ay[1] = (first, second)

    def ay_end():
        both(ay[1])
        part[rows_of(z, y), A] += full_ay[0] + full_ay[1]

    def az_all(t):
        for a in range(GROUPS):
            az_pass(a, t)

    with jax.named_scope("multiply_near"):
        multiply(own)
        y_start(0)
        twin_own.wait_recv()
        multiply(order[1])
        y_start(1)
    with jax.named_scope("gather_rest"):
        right_high.wait_recv()
        twin_left = share_whole(block_of(x, 3, c), twin)
        left_low.wait_recv()
        twin_right = share_whole(block_of(x, 1, c), twin)
        y_pass(0)
        onward_low.wait_recv()
        twin_low = share(block_of(x, 2, c), low_rows, twin)
        onward_high.wait_recv()
        twin_high = share(block_of(x, 2, c), high_rows, twin)
        twin_left.wait_recv()
        twin_right.wait_recv()
        twin_low.wait_recv()
        twin_high.wait_recv()
    multiply(order[2])
    y_start(2)
    for a in range(GROUPS):
        az_start(a)
    y_pass(1)
    multiply(order[3])
    y_start(3)
    multiply(order[4])
    y_start(4)
    y_pass(2)
    az_all(1)
    multiply(order[5])
    y_start(5)
    y_pass(3)
    multiply(order[6])
    y_start(6)
    y_pass(4)
    multiply(order[7])
    y_start(7)
    y_end(0)
    y_end(1)
    az_all(2)
    y_end(2)
    bz_start()
    y_pass(5)
    y_end(3)
    y_pass(6)
    az_all(3)
    y_end(4)
    bz_pass(1)
    y_pass(7)
    y_end(5)
    y_end(6)
    bz_pass(2)
    for a in range(GROUPS):
        az_end(a)
    ay_start()
    y_end(7)
    bz_pass(3)
    ay_pass()
    bz_end()
    ay_end()

    gene_scale, spot_scale = 1.0 / (SLIDES * GENES), 1.0 / SPOTS
    with jax.named_scope("local_sums"):
        pv, tv = part[rows_of(z, y), :], truth[...]
        pred_out[...] = pv
        cross, square, tsquare = pv * tv, pv * pv, tv * tv
        spot_mine[0:1, :] = jnp.sum(cross, axis=0, keepdims=True)
        spot_mine[1:2, :] = jnp.sum(square, axis=0, keepdims=True)
        near = spread_y(spot_mine, spot_near)
        lane = lax.broadcasted_iota(jnp.int32, (PIECE, LANES), 1)
        row_lane = lax.broadcasted_iota(jnp.int32, (1, LANES), 1)
        packed, extra = jnp.zeros((PIECE, LANES), f32), jnp.zeros((1, LANES), f32)
        for k in range(SLIDES):
            inside = member[k : k + 1, :]
            for q, field in enumerate((cross, square, tsquare)):
                summed = jnp.sum(field * inside, axis=1, keepdims=True)
                packed = packed + jnp.where(lane == q * SLIDES + k, summed, 0.0)
            for q, field in enumerate((density, prior[...])):
                summed = jnp.sum(field * inside, axis=1, keepdims=True)
                extra = extra + jnp.where(row_lane == q * SLIDES + k, summed, 0.0)
        board[...] = jnp.zeros((LANES, LANES), f32)
        board[0:PIECE, :] = packed
        slide_msgs[0] = board[...].T[0:16, :]
        slide_msgs[0, 12:13, :] = extra
        slide = spread_spot(slide_msgs)
    with jax.named_scope("spot_sums_y"):
        near.wait_recv()
        spot_far[0] = spot_mine[...] + spot_near[0] + spot_near[1] + spot_near[2]
        far = spread_z(spot_far)
    with jax.named_scope("slide_sums"):
        slide.wait_recv()
        slide_total = slide_msgs[0]
        for d in range(1, 8):
            slide_total = slide_total + slide_msgs[d]
        s_inner, s_square, s_truth = slide_total[0:4], slide_total[4:8], slide_total[8:12]
        s_left, s_right = lax.rsqrt(s_square + epsilon), lax.rsqrt(s_truth + epsilon)
        own_genes = lax.broadcasted_iota(jnp.int32, (SLIDES, LANES), 1) < PIECE
        gene_sum = jnp.sum(jnp.where(own_genes, s_inner * s_left * s_right, 0.0), keepdims=True)
        board[...] = jnp.zeros((LANES, LANES), f32)
        board[0:4, :] = s_inner * s_left * s_left * s_left * s_right
        board[4:8, :] = s_left * s_right
        columns = board[...].T[0:PIECE, :]
        cube_of, flat_of = jnp.zeros((PIECE, COLS), f32), jnp.zeros((PIECE, COLS), f32)
        spot_density, spot_prior = jnp.zeros((1, COLS), f32), jnp.zeros((1, COLS), f32)
        for k in range(SLIDES):
            inside = member[k : k + 1, :]
            cube_of = cube_of + columns[:, k : k + 1] * inside
            flat_of = flat_of + columns[:, 4 + k : 5 + k] * inside
            spot_density = spot_density + slide_total[12:13, k : k + 1] * inside
            spot_prior = spot_prior + slide_total[12:13, 4 + k : 5 + k] * inside
        target_share = prior[...] / spot_prior
        logs = jnp.log(target_share) - jnp.log(density / spot_density)
        density_part = jnp.sum(target_share * logs, keepdims=True) / SLIDES
        grad_density = (1.0 / spot_density - target_share / density) / SLIDES
        gene_part = gene_scale * (cube_of * pv - flat_of * tv)
    with jax.named_scope("spot_sums_z"):
        far.wait_recv()
        spot_total = spot_far[0]
        for d in range(1, 8):
            spot_total = spot_total + spot_far[d]
        p_inner, p_square = spot_total[0:1, :], spot_total[1:2, :]
        p_left, p_right = lax.rsqrt(p_square + epsilon), lax.rsqrt(truth_square + epsilon)
        spot_sum = jnp.sum(p_inner * p_left * p_right, keepdims=True)
        spot_cube = p_inner * p_left * p_left * p_left * p_right
        grad = gene_part + spot_scale * (spot_cube * pv - (p_left * p_right) * tv)
        grads[z, piece(y), :] = grad.astype(bf16)
    with jax.named_scope("sends_done"):
        wires.close()

    A, B = pl.ds(0, CLOSE), pl.ds(CLOSE, COLS - CLOSE)
    blocks = [ring(z, d, 8) for d in REACH]

    def put(block, rows, lanes, device):
        view = grads.at[block, rows, lanes]
        return wires.send(view, view, device)

    def y_share(block, lanes):
        return put(block, piece(y), lanes, y_up), put(block, piece(y), lanes, y_down)

    def y_onward(block, lanes, shared):
        shared[0].wait_recv()
        up = put(block, piece(ring(y, 3, 4), 0, HOP), lanes, y_up)
        shared[1].wait_recv()
        down = put(block, piece(ring(y, 1, 4), HOP, HOP), lanes, y_down)
        return up, down

    def z_share(step, rows, lanes):
        above, below = ring(z, 1 - step, 8), ring(z, step - 1, 8)
        return put(above, rows[0], lanes, z_up), put(below, rows[1], lanes, z_down)

    own_rows, all_rows = (piece(y), piece(y)), (pl.ds(0, OWN), pl.ds(0, OWN))
    own_halves = (piece(y, 0, HOP), piece(y, HOP, HOP))
    all_halves = (pl.ds(0, LANES), pl.ds(LANES, LANES))
    base = wires.take(33)

    def each(turn, body):
        if turn in (0, 4):
            body(2 * turn - (turn > 0), ring(z, turn, 8))
        else:

            @pl.loop(0, 2)
            def _(i):
                body(2 * turn - 1 + i, ring(z, turn * (1 - 2 * i), 8))

    keep, give = c * HALF, (1 - c) * HALF

    def some_rows(first, size=HALF):
        return pl.ds(pl.multiple_of(first, 16), size)

    def twin_link(n):
        return wires.link(xp.at[n, some_rows(give)], xc.at[n], twin, base + n)

    def quarter_links(k, odd):
        device = right if k in (0, 2, 3) else left
        at = k + 6 * odd
        return (
            wires.link(scale_out.at[at], scale_in.at[at], device, base + 8 + at),
            wires.link(coded_out.at[at], coded_in.at[at], device, base + 20 + at),
        )

    def eighth(i):
        return some_rows(i * EIGHTH, EIGHTH)

    def quarter_send(n, odd, high, k):
        top = jnp.full((1, OWN), 1e-30, f32)
        for i in range(2):
            summed = xp[n, some_rows(keep + (2 * high + i) * EIGHTH, EIGHTH), :]
            top = jnp.maximum(top, jnp.max(jnp.abs(summed), axis=0, keepdims=True))
        at = k + 6 * odd
        scale_out[at] = top * (1.0 / TOP)
        up = TOP / top

        @pl.loop(0, 2)
        def _(i):
            summed = xp[n, some_rows(keep + (2 * high + i) * EIGHTH, EIGHTH), :]
            coded_out[at, eighth(i), :] = jnp.round(summed * up).astype(jnp.int16)

        for link in quarter_links(k, odd):
            link.start()

    def quarter_value(k, odd, i):
        at = k + 6 * odd
        return coded_in[at, eighth(i), :].astype(f32) * scale_in[at]

    def quarter_arrived(k, odd):
        for link in quarter_links(k, odd):
            link.wait_recv()

    def distance(block):
        return ring(block // 2 - x, 0, 4)

    def block_first(n, block):
        xp[n] = lax.dot_general(
            weights[...],
            grads[block],
            (((1,), (1,)), ((), ())),
            preferred_element_type=f32,
        )
        twin_link(n).start()

    def cell_part(n, block):
        product = jnp.dot(profiles[block], grads[block], preferred_element_type=f32)
        if isinstance(n, int) and n == 0:
            part[0:ROWS, :] = product
        else:
            part[0:ROWS, :] += product

    def block_second(n, block):
        odd = lax.rem(block, 2)
        twin_link(n).wait_recv()

        @pl.loop(0, 4)
        def _(i):
            xp[n, some_rows(keep + i * EIGHTH, EIGHTH), :] += xc[n, eighth(i), :]

        @pl.when(distance(block) == 2)
        def _():
            quarter_send(n, odd, 0, 0)
            quarter_send(n, odd, 1, 1)

        @pl.when(distance(block) == 1)
        def _():
            quarter_send(n, odd, 1, 2)

        @pl.when(distance(block) == 3)
        def _():
            quarter_send(n, odd, 0, 4)

    def add_and_send(n, odd, high, k, onward):
        quarter_arrived(k, odd)

        @pl.loop(0, 2)
        def _(i):
            xp[n, some_rows(keep + (2 * high + i) * EIGHTH, EIGHTH), :] += quarter_value(k, odd, i)

        quarter_send(n, odd, high, onward)

    def block_third(n, block):
        odd = lax.rem(block, 2)

        @pl.when(distance(block) == 1)
        def _():
            add_and_send(n, odd, 0, 0, 3)

        @pl.when(distance(block) == 3)
        def _():
            add_and_send(n, odd, 1, 1, 5)

    bz = {1: z_share(1, own_rows, B)}
    straight = wires.spread(
        grads.at[z, piece(y), A],
        [(grads.at[z, piece(y), A], away("y", d)) for d in (1, 3, 2)],
        grads.at[z, pl.ds(0, 3 * PIECE), A],
    )
    shared_b, onward_b = {0: y_share(z, B)}, {}
    straight.wait_recv()
    az = {1: z_share(1, all_rows, A)}
    rounds = {0: (0,), 1: (1, 2), 2: (3, 4), 3: (5, 6), 4: (7,)}

    def y_pass_on(turn):
        for n in rounds[turn]:
            onward_b[n] = y_onward(blocks[n], B, shared_b[n])

    def y_complete(turn):
        for n in rounds[turn]:
            both(onward_b[n])

    for step in (1, 2, 3, 4, 5, 6):
        if step < 5:
            both(bz[step])
            if step < 4:
                bz[step + 1] = z_share(step + 1, own_rows if step < 3 else own_halves, B)
            for n in rounds[step]:
                shared_b[n] = y_share(blocks[n], B)
        if step < 6:
            y_pass_on(step - 1)
        if step < 5:
            both(az[step])
            if step < 4:
                az[step + 1] = z_share(step + 1, all_rows if step < 3 else all_halves, A)
        if step > 1:
            y_complete(step - 2)
            each(step - 2, block_first)
            if step > 2:
                each(step - 3, block_second)
            each(step - 2, cell_part)
            if step > 3:
                each(step - 4, block_third)

    with jax.named_scope("column_sums"):
        column_mine[...] = jnp.zeros((2, COLS), f32)
        column_mine[1:2, :] = jnp.where(column == 0, gene_sum, 0.0)
        for b in range(BLOCKS):
            rows = lanes_of(b)
            across = jnp.zeros((LANES, LANES), f32)
            for j in range(COLS // LANES):
                lanes, cut = lanes_of(j), slice(j * LANES, (j + 1) * LANES)
                whole = (grown[rows, lanes] * scale[:, cut]) * (
                    part[rows, lanes] + grad_density[:, cut]
                )
                part[rows, lanes] = whole
                across = across + whole
                column_mine[0:1, lanes] += jnp.sum(whole * gate[rows, :], axis=0, keepdims=True)
            filter_msgs[0, b : b + 1, :] = jnp.sum(across.T, axis=0, keepdims=True)
        filter_msgs[0, 11:12, :] = jnp.where(
            row_lane == 0, spot_sum, jnp.where(row_lane == 1, density_part, 0.0)
        )
        filter_msgs[0, 12:16, :] = jnp.zeros((4, LANES), f32)
        near = spread_y(column_mine, column_near)
        sums = spread_spot(filter_msgs)
    each(4, block_second)
    with jax.named_scope("column_sums_y"):
        near.wait_recv()
        column_far[0] = column_mine[...] + column_near[0] + column_near[1] + column_near[2]
        far = spread_z(column_far)
    each(3, block_third)
    each(4, block_third)
    with jax.named_scope("column_sums_z"):
        far.wait_recv()
        column_total = column_far[0]
        for d in range(1, 8):
            column_total = column_total + column_far[d]
    with jax.named_scope("logits_gradient"):
        dot_scale = column_total[0:1, :] * scale
        for b in range(BLOCKS):
            rows = lanes_of(b)
            for j in range(COLS // LANES):
                lanes, cut = lanes_of(j), slice(j * LANES, (j + 1) * LANES)
                part[rows, lanes] = (
                    gate[rows, :] * part[rows, lanes] - grown[rows, lanes] * dot_scale[:, cut]
                )
    with jax.named_scope("filter_gradient"):
        sums.wait_recv()
        filter_total = filter_msgs[0]
        for d in range(1, 8):
            filter_total = filter_total + filter_msgs[d]
        gap = kept - target[0].astype(f32)
        root = jnp.sqrt(gap * gap + 1.0)
        on = filter_total[0:BLOCKS, :] + gap / root / CELLS + (1.0 - 2.0 * gates) / CELLS
        filter_out[...] = on * gates * (1.0 - gates)
        values = (
            -column_total[1:2, 0:1] * gene_scale,
            -filter_total[11:12, 0:1] * spot_scale,
            filter_total[11:12, 1:2],
            root / CELLS,
            spread / CELLS,
        )
        losses = jnp.zeros((1, LANES), f32)
        for k, value in enumerate(values):
            losses = losses + jnp.where(row_lane == k, value, 0.0)
        losses_out[...] = losses

    at_own, at_twin = jnp.int32(0), jnp.int32(0)
    for n in range(8):
        at_own = at_own + n * jnp.where(blocks[n] == own, 1, 0)
        at_twin = at_twin + n * jnp.where(blocks[n] == block_of(x, 0, 1 - c), 1, 0)
    ending = wires.link(xp.at[at_twin, some_rows(keep)], ended, twin, base + 32)

    def last_sum(n, odd):
        for high, (low_k, high_k) in ((0, (3, 4)), (1, (2, 5))):
            quarter_arrived(low_k, odd)
            quarter_arrived(high_k, odd)

            @pl.loop(0, 2)
            def _(i, high=high, low_k=low_k, high_k=high_k):
                xp[n, some_rows(keep + (2 * high + i) * EIGHTH, EIGHTH), :] += quarter_value(
                    low_k, odd, i
                ) + quarter_value(high_k, odd, i)

    with jax.named_scope("last_sum_twin"):
        last_sum(at_twin, 1 - c)
        ending.start()
    with jax.named_scope("last_sum_own"):
        last_sum(at_own, c)
        profile_out[some_rows(keep), :] = xp[at_own, some_rows(keep), :]
    with jax.named_scope("ending"):
        ending.wait_recv()
        profile_out[some_rows(give), :] = ended[...]
    with jax.named_scope("sends_done"):
        for n in range(8):
            twin_link(n).wait_send()
        for odd in range(2):
            for k in range(6):
                for link in quarter_links(k, odd):
                    link.wait_send()
        ending.wait_send()
    with jax.named_scope("wires_done"):
        wires.close()


def training_step(sizes, target, logits, filters, expression, spatial, prior):
    f32, bf16 = jnp.float32, jnp.bfloat16
    anywhere = pl.BlockSpec(memory_space=pl.ANY)
    inside = pl.BlockSpec(memory_space=pltpu.VMEM)
    scalars = pl.BlockSpec(memory_space=pltpu.SMEM)
    near = COLS - SPLIT
    return pl.pallas_call(
        step_kernel,
        out_shape=(
            pltpu.VMEM((PIECE, COLS), f32),
            pltpu.VMEM((GENES, COLS), f32),
            pltpu.VMEM((ROWS, OWN), f32),
            pltpu.VMEM((BLOCKS, LANES), f32),
            pltpu.VMEM((1, LANES), f32),
        ),
        in_specs=[scalars, scalars, anywhere, inside, anywhere, anywhere, inside],
        out_specs=(inside, inside, inside, inside, inside),
        scratch_shapes=[
            pltpu.VMEM((ROWS, COLS), f32),
            pltpu.VMEM((ROWS, COLS), bf16),
            pltpu.VMEM((8, ROWS, OWN), bf16),
            pltpu.VMEM((COLS, LANES), f32),
            pltpu.VMEM((LANES, COLS), f32),
            pltpu.VMEM((ROWS, LANES), f32),
            pltpu.VMEM((SLIDES, COLS), f32),
            pltpu.VMEM((LANES, LANES), f32),
            pltpu.VMEM((4, COLS), f32),
            pltpu.VMEM((3, 4, COLS), f32),
            pltpu.VMEM((8, 4, COLS), f32),
            pltpu.VMEM((8, 2, HOP, near), f32),
            pltpu.VMEM((8, 2, PIECE, near), f32),
            pltpu.VMEM((2, HOP, near), f32),
            pltpu.VMEM((3, 2, PIECE, near), f32),
            pltpu.VMEM((GROUPS, 2, LANES, LANES), f32),
            pltpu.VMEM((GROUPS, 3, 2, OWN, LANES), f32),
            pltpu.VMEM((2, HOP, SPLIT), f32),
            pltpu.VMEM((2, PIECE, SPLIT), f32),
            pltpu.VMEM((8, OWN, COLS), bf16),
            pltpu.VMEM((8, ROWS, OWN), f32),
            pltpu.VMEM((8, HALF, OWN), f32),
            pltpu.VMEM((HALF, OWN), f32),
            pltpu.VMEM((12, HALF // 2, OWN), jnp.int16),
            pltpu.VMEM((12, HALF // 2, OWN), jnp.int16),
            pltpu.VMEM((12, 1, OWN), f32),
            pltpu.VMEM((12, 1, OWN), f32),
            pltpu.VMEM((8, 16, LANES), f32),
            pltpu.VMEM((2, COLS), f32),
            pltpu.VMEM((3, 2, COLS), f32),
            pltpu.VMEM((8, 2, COLS), f32),
            pltpu.VMEM((2, COLS), f32),
            pltpu.VMEM((3, 2, COLS), f32),
            pltpu.VMEM((8, 2, COLS), f32),
            pltpu.VMEM((8, 16, LANES), f32),
            pltpu.SemaphoreType.DMA((COPIES + SPREADS,)),
            pltpu.SemaphoreType.DMA((COPIES + SPREADS,)),
            pltpu.SemaphoreType.DMA((BLOCKS + 2,)),
        ],
        compiler_params=pltpu.CompilerParams(
            collective_id=0, has_side_effects=True, vmem_limit_bytes=LIMIT
        ),
        name="training_step",
    )(sizes, target, logits, filters, expression, spatial, prior)


def finish_kernel(
    losses,
    pred,
    part,
    profile,
    filter_rows,
    losses_out,
    pred_out,
    logits_out,
    profile_out,
    filter_out,
    sems,
):
    pieces = [(part.at[0:ROWS], logits_out), (profile, profile_out), (pred, pred_out)]
    pieces.append((filter_rows, filter_out))
    copies = [pltpu.make_async_copy(a, b, sems.at[i]) for i, (a, b) in enumerate(pieces)]
    for copy in copies:
        copy.start()
    row_lane = lax.broadcasted_iota(jnp.int32, (1, LANES), 1)
    for k in range(5):
        losses_out[k] = jnp.sum(jnp.where(row_lane == k, losses[...], 0.0))
    for copy in copies:
        copy.wait()


def finish(losses, pred, part, profile, filter_rows):
    f32 = jnp.float32
    anywhere = pl.BlockSpec(memory_space=pl.ANY)
    inside = pl.BlockSpec(memory_space=pltpu.VMEM)
    scalars = pl.BlockSpec(memory_space=pltpu.SMEM)
    return pl.pallas_call(
        finish_kernel,
        out_shape=(
            jax.ShapeDtypeStruct((5,), f32),
            jax.ShapeDtypeStruct((PIECE, COLS), f32),
            jax.ShapeDtypeStruct((ROWS, COLS), f32),
            jax.ShapeDtypeStruct((ROWS, OWN), f32),
            jax.ShapeDtypeStruct((BLOCKS, LANES), f32),
        ),
        in_specs=[inside] * 5,
        out_specs=(scalars, anywhere, anywhere, anywhere, anywhere),
        scratch_shapes=[pltpu.SemaphoreType.DMA((4,))],
        compiler_params=pltpu.CompilerParams(vmem_limit_bytes=1024 * 1024),
        name="finish",
    )(losses, pred, part, profile, filter_rows)


def on_device(logits, filter_logits, expression, spatial, prior, slide_sizes, target):
    pred, part, profile, filter_rows, losses = training_step(
        slide_sizes,
        target,
        logits,
        filter_logits.reshape(BLOCKS, LANES),
        expression,
        spatial,
        prior.reshape(1, COLS),
    )
    losses, pred, grad_logits, grad_expression, grad_filter = finish(
        losses, pred, part, profile, filter_rows
    )
    return (losses, pred.T, grad_logits, grad_filter.reshape(-1), grad_expression)


def solution(mesh):
    split = Mesh(mesh.devices.reshape(8, 4, 4, 2), ("z", "y", "x", "c"))
    return jax.shard_map(
        on_device,
        mesh=split,
        in_specs=(P(CELL, SPOT), P(CELL), P(CELL, SPOT), P(SPOT, None), P(SPOT), P(), P()),
        out_specs=(P(), P(SPOT, CELL), P(CELL, SPOT), P(CELL), P(CELL, SPOT)),
        check_vma=False,
    )
```

```python
import jax
import jax.numpy as jnp
from jax import lax
from jax.experimental import pallas as pl
from jax.experimental.pallas import tpu as pltpu
from jax.sharding import Mesh
from jax.sharding import PartitionSpec as P

CELL = ("z", "y")
SPOT = ("x", "c")
SIZE = {"z": 8, "y": 4, "x": 4, "c": 2}
MESH = pl.DeviceIdType.MESH
ROWS = 1408
COLS = 1024
OWN = 256
PIECE = 64
LANES = 128
BLOCKS = ROWS // LANES
SLIDES = 4
GENES = PIECE * 32
CELLS = ROWS * 32
SPOTS = COLS * 8
HALF = ROWS // 2
HOP = PIECE // 2
EIGHTH = HALF // 4
TOP = 32767.0
SPLIT = 384
GROUPS = SPLIT // LANES
CLOSE = 384
REACH = (0, 1, 7, 2, 6, 3, 5, 4)
COPIES, SPREADS = 147, 9
LIMIT = 52 * 1024 * 1024

epsilon = 1e-06


def ring(position, step, size):
    return lax.rem(position + step + size, size)


def away(axis, step):
    return {axis: ring(lax.axis_index(axis), step, SIZE[axis])}


def spot_peer(step):
    place = lax.rem(lax.axis_index("x") * 2 + lax.axis_index("c") + step, 8)
    return {"x": place // 2, "c": lax.rem(place, 2)}


def block_of(x, step, c):
    return ring(x, step, 4) * 2 + c


def lanes_of(j, size=LANES):
    if isinstance(j, int):
        return pl.ds(j * size, size)
    return pl.ds(pl.multiple_of(j * size, size), size)


def piece(position, extra=0, size=PIECE):
    return pl.ds(pl.multiple_of(position * PIECE, PIECE) + extra, size)


def rows_in(block, extra=0, size=OWN):
    return pl.ds(pl.multiple_of(block * OWN, OWN) + extra, size)


def rows_of(block, position, extra=0, size=PIECE):
    return pl.ds(pl.multiple_of(block * OWN + position * PIECE, PIECE) + extra, size)


class Wires:
    def __init__(self, send_sems, recv_sems):
        self.send_sems, self.recv_sems, self.sent = send_sems, recv_sems, []
        self.used, self.spreads = 0, 0

    def take(self, count=1):
        at = self.used
        self.used += count
        return at

    def link(self, source, target, device, at):
        return pltpu.make_async_remote_copy(
            src_ref=source,
            dst_ref=target,
            send_sem=self.send_sems.at[at],
            recv_sem=self.recv_sems.at[at],
            device_id=device,
            device_id_type=MESH,
        )

    def send(self, source, target, device):
        copy = self.link(source, target, device, self.take())
        copy.start()
        self.sent.append(copy)
        return copy

    def spread(self, source, targets, slots):
        at = COPIES + self.spreads
        self.spreads += 1
        for target, device in targets:
            self.link(source, target, device, at).start()
        whole = self.link(slots, slots, targets[0][1], at)
        self.sent.append(whole)
        return whole

    def close(self):
        assert self.used <= COPIES and self.spreads <= SPREADS
        for copy in self.sent:
            copy.wait_send()
        self.used, self.sent = 0, []


class Parcel:
    def __init__(self, wires, buffers, source, slot, place, device):
        out, out_scale, into, into_scale = buffers
        value = source[...]
        low = jnp.min(value, axis=0, keepdims=True)
        high = jnp.max(value, axis=0, keepdims=True)
        middle = 0.5 * (low + high)
        reach = jnp.maximum(jnp.maximum(high - middle, middle - low), 1e-30)
        out_scale[slot, 0:1, :] = middle
        out_scale[slot, 1:2, :] = reach * (1.0 / TOP)
        out[slot] = jnp.round((value - middle) * (TOP / reach)).astype(jnp.int16)
        self.rows, self.scale = into.at[place], into_scale.at[place]
        self.copies = (
            wires.link(out.at[slot], self.rows, device, wires.take()),
            wires.link(out_scale.at[slot], self.scale, device, wires.take()),
        )
        for copy in self.copies:
            copy.start()

    def wait_recv(self):
        for copy in self.copies:
            copy.wait_recv()

    def wait_send(self):
        for copy in self.copies:
            copy.wait_send()

    def value(self):
        return self.scale[0:1, :] + self.rows[...].astype(jnp.float32) * self.scale[1:2, :]


def parcel_buffers(rows, columns, out, into):
    return (
        pltpu.VMEM((out, rows, columns), jnp.int16),
        pltpu.VMEM((out, 2, columns), jnp.float32),
        pltpu.VMEM((into, rows, columns), jnp.int16),
        pltpu.VMEM((into, 2, columns), jnp.float32),
    )


def both(copies):
    copies[0].wait_recv()
    copies[1].wait_recv()


def step_kernel(
    sizes,
    target,
    logits,
    filters,
    expression,
    spatial,
    prior,
    pred_out,
    part,
    profile_out,
    filter_out,
    losses_out,
    grown,
    weights,
    profiles,
    slab,
    truth_all,
    gate,
    member,
    board,
    mine,
    near_stats,
    far_stats,
    half_y,
    full_y,
    half_bz,
    full_bz,
    half_az,
    full_az,
    half_ay,
    full_ay,
    grads,
    xp,
    xc,
    ended,
    coded_out,
    coded_in,
    scale_out,
    scale_in,
    slide_msgs,
    spot_mine,
    spot_near,
    spot_far,
    column_mine,
    column_near,
    column_far,
    filter_msgs,
    send_sems,
    recv_sems,
    local_sems,
):
    f32, bf16 = jnp.float32, jnp.bfloat16
    z, y = lax.axis_index("z"), lax.axis_index("y")
    x, c = lax.axis_index("x"), lax.axis_index("c")
    wires = Wires(send_sems, recv_sems)
    own = x * 2 + c
    cell = z * 4 + y
    right, left, twin = away("x", 1), away("x", 3), away("c", 1)
    y_up, y_down, z_up, z_down = away("y", 1), away("y", 3), away("z", 1), away("z", 7)

    def spread_y(source, slots):
        return wires.spread(source, [(slots.at[d - 1], away("y", d)) for d in (1, 2, 3)], slots)

    def spread_z(slots):
        others = [(slots.at[d], away("z", d)) for d in range(1, 8)]
        return wires.spread(slots.at[0], others, slots.at[pl.ds(1, 7)])

    def spread_spot(slots):
        others = [(slots.at[d], spot_peer(d)) for d in range(1, 8)]
        return wires.spread(slots.at[0], others, slots.at[pl.ds(1, 7)])

    loads = []
    for b in range(BLOCKS):
        rows = lanes_of(b)
        loads.append(
            pltpu.make_async_copy(logits.at[rows, :], grown.at[rows, :], local_sems.at[b])
        )
    load_own = pltpu.make_async_copy(expression, profiles.at[own], local_sems.at[BLOCKS])
    aligned = pl.multiple_of((cell // 2) * LANES, LANES)
    load_truth = pltpu.make_async_copy(
        spatial.at[:, pl.ds(aligned, LANES)], slab, local_sems.at[BLOCKS + 1]
    )
    load_own.start()
    for load in loads:
        load.start()
    load_truth.start()
    barrier = pltpu.get_barrier_semaphore()
    targets = (
        [away("y", d) for d in (1, 2, 3)]
        + [away("z", d) for d in range(1, 8)]
        + [spot_peer(d) for d in range(1, 8)]
    )
    for device in targets:
        pl.semaphore_signal(barrier, inc=1, device_id=device, device_id_type=MESH)
    gates = jax.nn.sigmoid(filters[...])
    for b in range(BLOCKS):
        gate[lanes_of(b), :] = jnp.broadcast_to(gates[b : b + 1, :], (LANES, LANES)).T
    kept = jnp.sum(gates, keepdims=True)
    spread = jnp.sum(gates - gates * gates, keepdims=True)
    column = lax.broadcasted_iota(jnp.int32, (1, COLS), 1)
    mine[3:4, :] = jnp.where(column == 0, kept, jnp.where(column == 1, spread, 0.0))
    mine[0:3, :] = jnp.zeros((3, COLS), f32)
    spot = column + own * COLS
    begin = jnp.int32(0)
    for k in range(SLIDES):
        end = begin + sizes[k]
        within = jnp.logical_and(spot >= begin, spot < end)
        member[k : k + 1, :] = jnp.where(within, 1.0, 0.0)
        begin = end

    load_own.wait()
    with jax.named_scope("greeting"):
        pl.semaphore_wait(barrier, len(targets))
    low_rows, high_rows = pl.ds(0, HALF), pl.ds(HALF, HALF)

    def share(block, rows, device):
        return wires.send(profiles.at[block, rows], profiles.at[block, rows], device)

    def share_whole(block, device):
        return wires.send(profiles.at[block], profiles.at[block], device)

    right_low = share(own, low_rows, right)
    left_high = share(own, high_rows, left)
    twin_own = share_whole(own, twin)
    with jax.named_scope("exponentials"):
        for b in range(BLOCKS):
            loads[b].wait()

            @pl.loop(0, COLS // LANES)
            def _(j, b=b):
                rows, lanes = lanes_of(b), lanes_of(j)
                e = jnp.exp(grown[rows, lanes])
                grown[rows, lanes] = e
                mine[0:1, lanes] += jnp.sum(e, axis=0, keepdims=True)
                mine[1:2, lanes] += jnp.sum(e * gate[rows, :], axis=0, keepdims=True)

    with jax.named_scope("truth"):
        load_truth.wait()
        truth_all[...] = slab[...].T
        truth = truth_all.at[piece(lax.rem(cell, 2)), :]
        held = truth[...]
        mine[2:3, :] = jnp.sum(held * held, axis=0, keepdims=True)

    with jax.named_scope("totals_y"):
        near = spread_y(mine, near_stats)
        right_high = share(own, high_rows, right)
        left_low = share(own, low_rows, left)
        near.wait_recv()
        far_stats[0] = mine[...] + near_stats[0] + near_stats[1] + near_stats[2]
        far = spread_z(far_stats)
    with jax.named_scope("pass_halves"):
        right_low.wait_recv()
        onward_low = share(block_of(x, 3, c), low_rows, right)
        left_high.wait_recv()
        onward_high = share(block_of(x, 1, c), high_rows, left)
    with jax.named_scope("totals_z"):
        far.wait_recv()
        stats = far_stats[0]
        for d in range(1, 8):
            stats = stats + far_stats[d]
    totals, filtered, truth_square = stats[0:1, :], stats[1:2, :], stats[2:3, :]
    kept, spread = stats[3:4, 0:1], stats[3:4, 1:2]
    density = filtered / totals
    scale = 1.0 / totals

    with jax.named_scope("weights"):

        @pl.loop(0, BLOCKS)
        def _(b):
            rows = lanes_of(b)
            for j in range(COLS // LANES):
                cut = slice(j * LANES, (j + 1) * LANES)
                weights[rows, lanes_of(j)] = (
                    grown[rows, lanes_of(j)] * scale[:, cut] * gate[rows, :]
                ).astype(bf16)

    def multiply(block):
        part[rows_in(block), :] = lax.dot_general(
            profiles[block], weights[...], (((0,), (0,)), ((), ())), preferred_element_type=f32
        )

    sought = [ring(z, d, 8) for d in (4, 3, 5, 2, 6, 1, 7, 0)]
    order = [own, block_of(x, 0, 1 - c)] + [jnp.int32(0)] * 6
    at = jnp.int32(2)
    for block in sought:
        other = jnp.where(block // 2 != x, 1, 0)
        for i in range(2, 8):
            order[i] = order[i] + block * other * jnp.where(at == i, 1, 0)
        at = at + other
    A, B = pl.ds(0, SPLIT), pl.ds(SPLIT, COLS - SPLIT)
    started, passed, parcels = {}, {}, {}

    def parcel(name, buffers, rows, lanes, slot, place, device):
        if (name, slot) in parcels:
            parcels[name, slot].wait_send()
        sent = Parcel(wires, buffers, part.at[rows, lanes], slot, place, device)
        parcels[name, slot] = sent
        return sent

    def arrive(sent, rows, lanes):
        sent.wait_recv()
        part[rows, lanes] += sent.value()

    def y_start(i):
        s, p, slot = order[i], ring(y, 2, 4), 2 * (i % 4)
        started[i] = (
            parcel("y0", half_y, rows_of(s, p, 0, HOP), B, slot, 2 * i, y_up),
            parcel("y0", half_y, rows_of(s, p, HOP, HOP), B, slot + 1, 2 * i + 1, y_down),
        )

    def y_pass(i):
        s, up, down, slot = order[i], ring(y, 1, 4), ring(y, 3, 4), 2 * (i % 4)
        arrive(started[i][0], rows_of(s, up, 0, HOP), B)
        first = parcel("y1", full_y, rows_of(s, up), B, slot, 2 * i, y_up)
        arrive(started[i][1], rows_of(s, down, HOP, HOP), B)
        second = parcel("y1", full_y, rows_of(s, down), B, slot + 1, 2 * i + 1, y_down)
        passed[i] = (first, second)

    def y_end(i):
        both(passed[i])
        part[rows_of(order[i], y), B] += passed[i][0].value() + passed[i][1].value()

    bz, az, ay = {}, {}, {}

    def bz_start():
        d = ring(z, 4, 8)
        bz[0] = (
            parcel("bz0", half_bz, rows_of(d, y, 0, HOP), B, 0, 0, z_up),
            parcel("bz0", half_bz, rows_of(d, y, HOP, HOP), B, 1, 1, z_down),
        )

    def bz_pass(t):
        up, down, place = ring(z, 4 - t, 8), ring(z, t - 4, 8), 2 * (t - 1)
        arrive(bz[t - 1][0], rows_of(up, y, 0, HOP) if t == 1 else rows_of(up, y), B)
        first = parcel("bz1", full_bz, rows_of(up, y), B, 0, place, z_up)
        arrive(bz[t - 1][1], rows_of(down, y, HOP, HOP) if t == 1 else rows_of(down, y), B)
        second = parcel("bz1", full_bz, rows_of(down, y), B, 1, place + 1, z_down)
        bz[t] = (first, second)

    def bz_end():
        both(bz[3])
        part[rows_of(z, y), B] += bz[3][0].value() + bz[3][1].value()

    def az_start(a):
        d, lanes, slot = ring(z, 4, 8), lanes_of(a), 2 * a
        az[a, 0] = (
            parcel("az0", half_az, rows_in(d, 0, LANES), lanes, slot, slot, z_up),
            parcel("az0", half_az, rows_in(d, LANES, LANES), lanes, slot + 1, slot + 1, z_down),
        )

    def az_pass(a, t):
        up, down, lanes = ring(z, 4 - t, 8), ring(z, t - 4, 8), lanes_of(a)
        slot, place = 2 * a, 6 * a + 2 * (t - 1)
        arrive(az[a, t - 1][0], rows_in(up, 0, LANES) if t == 1 else rows_in(up), lanes)
        first = parcel("az1", full_az, rows_in(up), lanes, slot, place, z_up)
        arrive(az[a, t - 1][1], rows_in(down, LANES, LANES) if t == 1 else rows_in(down), lanes)
        second = parcel("az1", full_az, rows_in(down), lanes, slot + 1, place + 1, z_down)
        az[a, t] = (first, second)

    def az_end(a):
        both(az[a, 3])
        part[rows_in(z), lanes_of(a)] += az[a, 3][0].value() + az[a, 3][1].value()

    def ay_start():
        p = ring(y, 2, 4)
        ay[0] = (
            parcel("ay0", half_ay, rows_of(z, p, 0, HOP), A, 0, 0, y_up),
            parcel("ay0", half_ay, rows_of(z, p, HOP, HOP), A, 1, 1, y_down),
        )

    def ay_pass():
        up, down = ring(y, 1, 4), ring(y, 3, 4)
        arrive(ay[0][0], rows_of(z, up, 0, HOP), A)
        first = parcel("ay1", full_ay, rows_of(z, up), A, 0, 0, y_up)
        arrive(ay[0][1], rows_of(z, down, HOP, HOP), A)
        second = parcel("ay1", full_ay, rows_of(z, down), A, 1, 1, y_down)
        ay[1] = (first, second)

    def ay_end():
        both(ay[1])
        part[rows_of(z, y), A] += ay[1][0].value() + ay[1][1].value()

    with jax.named_scope("multiply_near"):
        multiply(own)
        y_start(0)
        twin_own.wait_recv()
        multiply(order[1])
        y_start(1)
    with jax.named_scope("gather_rest"):
        right_high.wait_recv()
        twin_left = share_whole(block_of(x, 3, c), twin)
        left_low.wait_recv()
        twin_right = share_whole(block_of(x, 1, c), twin)
        y_pass(0)
        onward_low.wait_recv()
        twin_low = share(block_of(x, 2, c), low_rows, twin)
        onward_high.wait_recv()
        twin_high = share(block_of(x, 2, c), high_rows, twin)
        twin_left.wait_recv()
        twin_right.wait_recv()
        twin_low.wait_recv()
        twin_high.wait_recv()
    y_pass(1)
    multiply(order[2])
    az_start(0)
    y_start(2)
    az_start(1)
    multiply(order[3])
    az_start(2)
    y_start(3)
    multiply(order[4])
    y_start(4)
    multiply(order[5])
    az_pass(0, 1)
    az_pass(1, 1)
    y_pass(2)
    multiply(order[6])
    az_pass(2, 1)
    y_start(6)
    y_pass(3)
    y_end(0)
    y_pass(4)
    y_end(1)
    y_start(5)
    multiply(order[7])
    y_start(7)
    az_pass(0, 2)
    y_end(2)
    bz_start()
    az_pass(1, 2)
    y_pass(6)
    az_pass(2, 2)
    y_end(3)
    az_pass(0, 3)
    y_end(4)
    bz_pass(1)
    y_pass(5)
    az_pass(1, 3)
    y_pass(7)
    az_pass(2, 3)
    y_end(6)
    az_end(0)
    y_end(5)
    bz_pass(2)
    az_end(1)
    y_end(7)
    az_end(2)
    ay_start()
    bz_pass(3)
    ay_pass()
    bz_end()
    ay_end()

    gene_scale, spot_scale = 1.0 / (SLIDES * GENES), 1.0 / SPOTS
    with jax.named_scope("local_sums"):
        pv, tv = part[rows_of(z, y), :], truth[...]
        pred_out[...] = pv
        cross, square, tsquare = pv * tv, pv * pv, tv * tv
        spot_mine[0:1, :] = jnp.sum(cross, axis=0, keepdims=True)
        spot_mine[1:2, :] = jnp.sum(square, axis=0, keepdims=True)
        near = spread_y(spot_mine, spot_near)
        lane = lax.broadcasted_iota(jnp.int32, (PIECE, LANES), 1)
        row_lane = lax.broadcasted_iota(jnp.int32, (1, LANES), 1)
        packed, extra = jnp.zeros((PIECE, LANES), f32), jnp.zeros((1, LANES), f32)
        for k in range(SLIDES):
            inside = member[k : k + 1, :]
            for q, field in enumerate((cross, square, tsquare)):
                summed = jnp.sum(field * inside, axis=1, keepdims=True)
                packed = packed + jnp.where(lane == q * SLIDES + k, summed, 0.0)
            for q, field in enumerate((density, prior[...])):
                summed = jnp.sum(field * inside, axis=1, keepdims=True)
                extra = extra + jnp.where(row_lane == q * SLIDES + k, summed, 0.0)
        board[...] = jnp.zeros((LANES, LANES), f32)
        board[0:PIECE, :] = packed
        slide_msgs[0] = board[...].T[0:16, :]
        slide_msgs[0, 12:13, :] = extra
        slide = spread_spot(slide_msgs)
    with jax.named_scope("spot_sums_y"):
        near.wait_recv()
        spot_far[0] = spot_mine[...] + spot_near[0] + spot_near[1] + spot_near[2]
        far = spread_z(spot_far)
    with jax.named_scope("slide_sums"):
        slide.wait_recv()
        slide_total = slide_msgs[0]
        for d in range(1, 8):
            slide_total = slide_total + slide_msgs[d]
        s_inner, s_square, s_truth = slide_total[0:4], slide_total[4:8], slide_total[8:12]
        s_left, s_right = lax.rsqrt(s_square + epsilon), lax.rsqrt(s_truth + epsilon)
        own_genes = lax.broadcasted_iota(jnp.int32, (SLIDES, LANES), 1) < PIECE
        gene_sum = jnp.sum(jnp.where(own_genes, s_inner * s_left * s_right, 0.0), keepdims=True)
        board[...] = jnp.zeros((LANES, LANES), f32)
        board[0:4, :] = s_inner * s_left * s_left * s_left * s_right
        board[4:8, :] = s_left * s_right
        columns = board[...].T[0:PIECE, :]
        cube_of, flat_of = jnp.zeros((PIECE, COLS), f32), jnp.zeros((PIECE, COLS), f32)
        spot_density, spot_prior = jnp.zeros((1, COLS), f32), jnp.zeros((1, COLS), f32)
        for k in range(SLIDES):
            inside = member[k : k + 1, :]
            cube_of = cube_of + columns[:, k : k + 1] * inside
            flat_of = flat_of + columns[:, 4 + k : 5 + k] * inside
            spot_density = spot_density + slide_total[12:13, k : k + 1] * inside
            spot_prior = spot_prior + slide_total[12:13, 4 + k : 5 + k] * inside
        target_share = prior[...] / spot_prior
        logs = jnp.log(target_share) - jnp.log(density / spot_density)
        density_part = jnp.sum(target_share * logs, keepdims=True) / SLIDES
        grad_density = (1.0 / spot_density - target_share / density) / SLIDES
        gene_part = gene_scale * (cube_of * pv - flat_of * tv)
    with jax.named_scope("spot_sums_z"):
        far.wait_recv()
        spot_total = spot_far[0]
        for d in range(1, 8):
            spot_total = spot_total + spot_far[d]
        p_inner, p_square = spot_total[0:1, :], spot_total[1:2, :]
        p_left, p_right = lax.rsqrt(p_square + epsilon), lax.rsqrt(truth_square + epsilon)
        spot_sum = jnp.sum(p_inner * p_left * p_right, keepdims=True)
        spot_cube = p_inner * p_left * p_left * p_left * p_right
        grad = gene_part + spot_scale * (spot_cube * pv - (p_left * p_right) * tv)
        grads[z, piece(y), :] = grad.astype(bf16)
    with jax.named_scope("sends_done"):
        for sent in parcels.values():
            sent.wait_send()
        wires.close()

    A, B = pl.ds(0, CLOSE), pl.ds(CLOSE, COLS - CLOSE)
    blocks = [ring(z, d, 8) for d in REACH]

    def put(block, rows, lanes, device):
        view = grads.at[block, rows, lanes]
        return wires.send(view, view, device)

    def y_share(block, lanes):
        return put(block, piece(y), lanes, y_up), put(block, piece(y), lanes, y_down)

    def y_onward(block, lanes, shared):
        shared[0].wait_recv()
        up = put(block, piece(ring(y, 3, 4), 0, HOP), lanes, y_up)
        shared[1].wait_recv()
        down = put(block, piece(ring(y, 1, 4), HOP, HOP), lanes, y_down)
        return up, down

    def z_share(step, rows, lanes):
        above, below = ring(z, 1 - step, 8), ring(z, step - 1, 8)
        return put(above, rows[0], lanes, z_up), put(below, rows[1], lanes, z_down)

    own_rows, all_rows = (piece(y), piece(y)), (pl.ds(0, OWN), pl.ds(0, OWN))
    own_halves = (piece(y, 0, HOP), piece(y, HOP, HOP))
    all_halves = (pl.ds(0, LANES), pl.ds(LANES, LANES))
    base = wires.take(33)

    def each(turn, body):
        if turn in (0, 4):
            body(2 * turn - (turn > 0), ring(z, turn, 8))
        else:

            @pl.loop(0, 2)
            def _(i):
                body(2 * turn - 1 + i, ring(z, turn * (1 - 2 * i), 8))

    keep, give = c * HALF, (1 - c) * HALF

    def some_rows(first, size=HALF):
        return pl.ds(pl.multiple_of(first, 16), size)

    def twin_link(n):
        return wires.link(xp.at[n, some_rows(give)], xc.at[n], twin, base + n)

    def quarter_links(k, odd):
        device = right if k in (0, 2, 3) else left
        at = k + 6 * odd
        return (
            wires.link(scale_out.at[at], scale_in.at[at], device, base + 8 + at),
            wires.link(coded_out.at[at], coded_in.at[at], device, base + 20 + at),
        )

    def eighth(i):
        return some_rows(i * EIGHTH, EIGHTH)

    def quarter_send(n, odd, high, k):
        top = jnp.full((1, OWN), 1e-30, f32)
        for i in range(2):
            summed = xp[n, some_rows(keep + (2 * high + i) * EIGHTH, EIGHTH), :]
            top = jnp.maximum(top, jnp.max(jnp.abs(summed), axis=0, keepdims=True))
        at = k + 6 * odd
        scale_out[at] = top * (1.0 / TOP)
        up = TOP / top

        @pl.loop(0, 2)
        def _(i):
            summed = xp[n, some_rows(keep + (2 * high + i) * EIGHTH, EIGHTH), :]
            coded_out[at, eighth(i), :] = jnp.round(summed * up).astype(jnp.int16)

        for link in quarter_links(k, odd):
            link.start()

    def quarter_value(k, odd, i):
        at = k + 6 * odd
        return coded_in[at, eighth(i), :].astype(f32) * scale_in[at]

    def quarter_arrived(k, odd):
        for link in quarter_links(k, odd):
            link.wait_recv()

    def distance(block):
        return ring(block // 2 - x, 0, 4)

    def block_first(n, block):
        xp[n] = lax.dot_general(
            weights[...],
            grads[block],
            (((1,), (1,)), ((), ())),
            preferred_element_type=f32,
        )
        twin_link(n).start()

    def cell_part(n, block):
        product = jnp.dot(profiles[block], grads[block], preferred_element_type=f32)
        if isinstance(n, int) and n == 0:
            part[0:ROWS, :] = product
        else:
            part[0:ROWS, :] += product

    def block_second(n, block):
        odd = lax.rem(block, 2)
        twin_link(n).wait_recv()

        @pl.loop(0, 4)
        def _(i):
            xp[n, some_rows(keep + i * EIGHTH, EIGHTH), :] += xc[n, eighth(i), :]

        @pl.when(distance(block) == 2)
        def _():
            quarter_send(n, odd, 0, 0)
            quarter_send(n, odd, 1, 1)

        @pl.when(distance(block) == 1)
        def _():
            quarter_send(n, odd, 1, 2)

        @pl.when(distance(block) == 3)
        def _():
            quarter_send(n, odd, 0, 4)

    def add_and_send(n, odd, high, k, onward):
        quarter_arrived(k, odd)

        @pl.loop(0, 2)
        def _(i):
            xp[n, some_rows(keep + (2 * high + i) * EIGHTH, EIGHTH), :] += quarter_value(k, odd, i)

        quarter_send(n, odd, high, onward)

    def block_third(n, block):
        odd = lax.rem(block, 2)

        @pl.when(distance(block) == 1)
        def _():
            add_and_send(n, odd, 0, 0, 3)

        @pl.when(distance(block) == 3)
        def _():
            add_and_send(n, odd, 1, 1, 5)

    bz, az, shared_b, onward_b = {1: z_share(1, own_rows, B)}, {}, {}, {}
    straight = wires.spread(
        grads.at[z, piece(y), A],
        [(grads.at[z, piece(y), A], away("y", d)) for d in (1, 3, 2)],
        grads.at[z, pl.ds(0, 3 * PIECE), A],
    )
    shared_b[0] = y_share(z, B)
    rounds = {0: (0,), 1: (1, 2), 2: (3, 4), 3: (5, 6), 4: (7,)}

    def turn_b(turn):
        both(bz[turn])
        if turn < 4:
            bz[turn + 1] = z_share(turn + 1, own_rows if turn < 3 else own_halves, B)
        for n in rounds[turn]:
            shared_b[n] = y_share(blocks[n], B)

    def turn_a(turn):
        if turn:
            both(az[turn])
        else:
            straight.wait_recv()
        if turn < 4:
            az[turn + 1] = z_share(turn + 1, all_rows if turn < 3 else all_halves, A)

    def turn_on(turn):
        for n in rounds[turn]:
            onward_b[n] = y_onward(blocks[n], B, shared_b[n])

    def turn_first(turn):
        for n in rounds[turn]:
            both(onward_b[n])
        each(turn, block_first)

    turn_b(1)
    turn_a(0)
    turn_on(0)
    turn_b(2)
    turn_on(1)
    turn_first(0)
    turn_a(1)
    each(0, cell_part)
    turn_on(2)
    turn_b(3)
    turn_first(1)
    each(0, block_second)
    each(1, cell_part)
    turn_a(2)
    turn_b(4)
    turn_first(2)
    turn_on(3)
    each(2, cell_part)
    turn_on(4)
    each(1, block_second)
    each(0, block_third)
    turn_a(3)
    turn_first(3)
    each(2, block_second)
    each(3, cell_part)
    turn_a(4)
    turn_first(4)
    each(3, block_second)
    each(1, block_third)
    each(4, cell_part)
    each(4, block_second)

    with jax.named_scope("column_sums"):
        column_mine[...] = jnp.zeros((2, COLS), f32)
        column_mine[1:2, :] = jnp.where(column == 0, gene_sum, 0.0)
        for b in range(BLOCKS):
            rows = lanes_of(b)
            across = jnp.zeros((LANES, LANES), f32)
            for j in range(COLS // LANES):
                lanes, cut = lanes_of(j), slice(j * LANES, (j + 1) * LANES)
                whole = (grown[rows, lanes] * scale[:, cut]) * (
                    part[rows, lanes] + grad_density[:, cut]
                )
                part[rows, lanes] = whole
                across = across + whole
                column_mine[0:1, lanes] += jnp.sum(whole * gate[rows, :], axis=0, keepdims=True)
            filter_msgs[0, b : b + 1, :] = jnp.sum(across.T, axis=0, keepdims=True)
        filter_msgs[0, 11:12, :] = jnp.where(
            row_lane == 0, spot_sum, jnp.where(row_lane == 1, density_part, 0.0)
        )
        filter_msgs[0, 12:16, :] = jnp.zeros((4, LANES), f32)
        near = spread_y(column_mine, column_near)
        sums = spread_spot(filter_msgs)
    each(2, block_third)
    with jax.named_scope("column_sums_y"):
        near.wait_recv()
        column_far[0] = column_mine[...] + column_near[0] + column_near[1] + column_near[2]
        far = spread_z(column_far)
    each(3, block_third)
    each(4, block_third)
    with jax.named_scope("column_sums_z"):
        far.wait_recv()
        column_total = column_far[0]
        for d in range(1, 8):
            column_total = column_total + column_far[d]
    with jax.named_scope("logits_gradient"):
        dot_scale = column_total[0:1, :] * scale
        for b in range(BLOCKS):
            rows = lanes_of(b)
            for j in range(COLS // LANES):
                lanes, cut = lanes_of(j), slice(j * LANES, (j + 1) * LANES)
                part[rows, lanes] = (
                    gate[rows, :] * part[rows, lanes] - grown[rows, lanes] * dot_scale[:, cut]
                )
    with jax.named_scope("filter_gradient"):
        sums.wait_recv()
        filter_total = filter_msgs[0]
        for d in range(1, 8):
            filter_total = filter_total + filter_msgs[d]
        gap = kept - target[0].astype(f32)
        root = jnp.sqrt(gap * gap + 1.0)
        on = filter_total[0:BLOCKS, :] + gap / root / CELLS + (1.0 - 2.0 * gates) / CELLS
        filter_out[...] = on * gates * (1.0 - gates)
        values = (
            -column_total[1:2, 0:1] * gene_scale,
            -filter_total[11:12, 0:1] * spot_scale,
            filter_total[11:12, 1:2],
            root / CELLS,
            spread / CELLS,
        )
        losses = jnp.zeros((1, LANES), f32)
        for k, value in enumerate(values):
            losses = losses + jnp.where(row_lane == k, value, 0.0)
        losses_out[...] = losses

    at_own, at_twin = jnp.int32(0), jnp.int32(0)
    for n in range(8):
        at_own = at_own + n * jnp.where(blocks[n] == own, 1, 0)
        at_twin = at_twin + n * jnp.where(blocks[n] == block_of(x, 0, 1 - c), 1, 0)
    ending = wires.link(xp.at[at_twin, some_rows(keep)], ended, twin, base + 32)

    def last_sum(n, odd):
        for high, (low_k, high_k) in ((0, (3, 4)), (1, (2, 5))):
            quarter_arrived(low_k, odd)
            quarter_arrived(high_k, odd)

            @pl.loop(0, 2)
            def _(i, high=high, low_k=low_k, high_k=high_k):
                xp[n, some_rows(keep + (2 * high + i) * EIGHTH, EIGHTH), :] += quarter_value(
                    low_k, odd, i
                ) + quarter_value(high_k, odd, i)

    with jax.named_scope("last_sum_twin"):
        last_sum(at_twin, 1 - c)
        ending.start()
    with jax.named_scope("last_sum_own"):
        last_sum(at_own, c)
        profile_out[some_rows(keep), :] = xp[at_own, some_rows(keep), :]
    with jax.named_scope("ending"):
        ending.wait_recv()
        profile_out[some_rows(give), :] = ended[...]
    with jax.named_scope("sends_done"):
        for n in range(8):
            twin_link(n).wait_send()
        for odd in range(2):
            for k in range(6):
                for link in quarter_links(k, odd):
                    link.wait_send()
        ending.wait_send()
    with jax.named_scope("wires_done"):
        wires.close()


def training_step(sizes, target, logits, filters, expression, spatial, prior):
    f32, bf16 = jnp.float32, jnp.bfloat16
    anywhere = pl.BlockSpec(memory_space=pl.ANY)
    inside = pl.BlockSpec(memory_space=pltpu.VMEM)
    scalars = pl.BlockSpec(memory_space=pltpu.SMEM)
    near = COLS - SPLIT
    return pl.pallas_call(
        step_kernel,
        out_shape=(
            pltpu.VMEM((PIECE, COLS), f32),
            pltpu.VMEM((GENES, COLS), f32),
            pltpu.VMEM((ROWS, OWN), f32),
            pltpu.VMEM((BLOCKS, LANES), f32),
            pltpu.VMEM((1, LANES), f32),
        ),
        in_specs=[scalars, scalars, anywhere, inside, anywhere, anywhere, inside],
        out_specs=(inside, inside, inside, inside, inside),
        scratch_shapes=[
            pltpu.VMEM((ROWS, COLS), f32),
            pltpu.VMEM((ROWS, COLS), bf16),
            pltpu.VMEM((8, ROWS, OWN), bf16),
            pltpu.VMEM((COLS, LANES), f32),
            pltpu.VMEM((LANES, COLS), f32),
            pltpu.VMEM((ROWS, LANES), f32),
            pltpu.VMEM((SLIDES, COLS), f32),
            pltpu.VMEM((LANES, LANES), f32),
            pltpu.VMEM((4, COLS), f32),
            pltpu.VMEM((3, 4, COLS), f32),
            pltpu.VMEM((8, 4, COLS), f32),
            parcel_buffers(HOP, near, 8, 16),
            parcel_buffers(PIECE, near, 8, 16),
            parcel_buffers(HOP, near, 2, 2),
            parcel_buffers(PIECE, near, 2, 6),
            parcel_buffers(LANES, LANES, 2 * GROUPS, 2 * GROUPS),
            parcel_buffers(OWN, LANES, 2 * GROUPS, 6 * GROUPS),
            parcel_buffers(HOP, SPLIT, 2, 2),
            parcel_buffers(PIECE, SPLIT, 2, 2),
            pltpu.VMEM((8, OWN, COLS), bf16),
            pltpu.VMEM((8, ROWS, OWN), f32),
            pltpu.VMEM((8, HALF, OWN), f32),
            pltpu.VMEM((HALF, OWN), f32),
            pltpu.VMEM((12, HALF // 2, OWN), jnp.int16),
            pltpu.VMEM((12, HALF // 2, OWN), jnp.int16),
            pltpu.VMEM((12, 1, OWN), f32),
            pltpu.VMEM((12, 1, OWN), f32),
            pltpu.VMEM((8, 16, LANES), f32),
            pltpu.VMEM((2, COLS), f32),
            pltpu.VMEM((3, 2, COLS), f32),
            pltpu.VMEM((8, 2, COLS), f32),
            pltpu.VMEM((2, COLS), f32),
            pltpu.VMEM((3, 2, COLS), f32),
            pltpu.VMEM((8, 2, COLS), f32),
            pltpu.VMEM((8, 16, LANES), f32),
            pltpu.SemaphoreType.DMA((COPIES + SPREADS,)),
            pltpu.SemaphoreType.DMA((COPIES + SPREADS,)),
            pltpu.SemaphoreType.DMA((BLOCKS + 2,)),
        ],
        compiler_params=pltpu.CompilerParams(
            collective_id=0, has_side_effects=True, vmem_limit_bytes=LIMIT
        ),
        name="training_step",
    )(sizes, target, logits, filters, expression, spatial, prior)


def finish_kernel(
    losses,
    pred,
    part,
    profile,
    filter_rows,
    losses_out,
    pred_out,
    logits_out,
    profile_out,
    filter_out,
    sems,
):
    pieces = [(part.at[0:ROWS], logits_out), (profile, profile_out), (pred, pred_out)]
    pieces.append((filter_rows, filter_out))
    copies = [pltpu.make_async_copy(a, b, sems.at[i]) for i, (a, b) in enumerate(pieces)]
    for copy in copies:
        copy.start()
    row_lane = lax.broadcasted_iota(jnp.int32, (1, LANES), 1)
    for k in range(5):
        losses_out[k] = jnp.sum(jnp.where(row_lane == k, losses[...], 0.0))
    for copy in copies:
        copy.wait()


def finish(losses, pred, part, profile, filter_rows):
    f32 = jnp.float32
    anywhere = pl.BlockSpec(memory_space=pl.ANY)
    inside = pl.BlockSpec(memory_space=pltpu.VMEM)
    scalars = pl.BlockSpec(memory_space=pltpu.SMEM)
    return pl.pallas_call(
        finish_kernel,
        out_shape=(
            jax.ShapeDtypeStruct((5,), f32),
            jax.ShapeDtypeStruct((PIECE, COLS), f32),
            jax.ShapeDtypeStruct((ROWS, COLS), f32),
            jax.ShapeDtypeStruct((ROWS, OWN), f32),
            jax.ShapeDtypeStruct((BLOCKS, LANES), f32),
        ),
        in_specs=[inside] * 5,
        out_specs=(scalars, anywhere, anywhere, anywhere, anywhere),
        scratch_shapes=[pltpu.SemaphoreType.DMA((4,))],
        compiler_params=pltpu.CompilerParams(vmem_limit_bytes=1024 * 1024),
        name="finish",
    )(losses, pred, part, profile, filter_rows)


def on_device(logits, filter_logits, expression, spatial, prior, slide_sizes, target):
    pred, part, profile, filter_rows, losses = training_step(
        slide_sizes,
        target,
        logits,
        filter_logits.reshape(BLOCKS, LANES),
        expression,
        spatial,
        prior.reshape(1, COLS),
    )
    losses, pred, grad_logits, grad_expression, grad_filter = finish(
        losses, pred, part, profile, filter_rows
    )
    return (losses, pred.T, grad_logits, grad_filter.reshape(-1), grad_expression)


def solution(mesh):
    split = Mesh(mesh.devices.reshape(8, 4, 4, 2), ("z", "y", "x", "c"))
    return jax.shard_map(
        on_device,
        mesh=split,
        in_specs=(P(CELL, SPOT), P(CELL), P(CELL, SPOT), P(SPOT, None), P(SPOT), P(), P()),
        out_specs=(P(), P(SPOT, CELL), P(CELL, SPOT), P(CELL), P(CELL, SPOT)),
        check_vma=False,
    )
```

```python
import jax
import jax.numpy as jnp
from jax import lax
from jax.experimental import pallas as pl
from jax.experimental.pallas import tpu as pltpu
from jax.sharding import Mesh
from jax.sharding import PartitionSpec as P

CELL = ("z", "y")
SPOT = ("x", "c")
SIZE = {"z": 8, "y": 4, "x": 4, "c": 2}
MESH = pl.DeviceIdType.MESH
ROWS = 1408
COLS = 1024
OWN = 256
PIECE = 64
LANES = 128
BLOCKS = ROWS // LANES
SLIDES = 4
GENES = PIECE * 32
CELLS = ROWS * 32
SPOTS = COLS * 8
HALF = ROWS // 2
HOP = PIECE // 2
EIGHTH = HALF // 4
TOP = 32767.0
SPLIT = 384
GROUPS = SPLIT // LANES
CLOSE = 384
REACH = (0, 1, 7, 2, 6, 3, 5, 4)
COPIES, SPREADS = 147, 9
LIMIT = 52 * 1024 * 1024

epsilon = 1e-06


def ring(position, step, size):
    return lax.rem(position + step + size, size)


def away(axis, step):
    return {axis: ring(lax.axis_index(axis), step, SIZE[axis])}


def spot_peer(step):
    place = lax.rem(lax.axis_index("x") * 2 + lax.axis_index("c") + step, 8)
    return {"x": place // 2, "c": lax.rem(place, 2)}


def block_of(x, step, c):
    return ring(x, step, 4) * 2 + c


def lanes_of(j, size=LANES):
    if isinstance(j, int):
        return pl.ds(j * size, size)
    return pl.ds(pl.multiple_of(j * size, size), size)


def piece(position, extra=0, size=PIECE):
    return pl.ds(pl.multiple_of(position * PIECE, PIECE) + extra, size)


def rows_in(block, extra=0, size=OWN):
    return pl.ds(pl.multiple_of(block * OWN, OWN) + extra, size)


def rows_of(block, position, extra=0, size=PIECE):
    return pl.ds(pl.multiple_of(block * OWN + position * PIECE, PIECE) + extra, size)


class Wires:
    def __init__(self, send_sems, recv_sems):
        self.send_sems, self.recv_sems, self.sent = send_sems, recv_sems, []
        self.used, self.spreads = 0, 0

    def take(self, count=1):
        at = self.used
        self.used += count
        return at

    def link(self, source, target, device, at, at_there=None):
        return pltpu.make_async_remote_copy(
            src_ref=source,
            dst_ref=target,
            send_sem=self.send_sems.at[at],
            recv_sem=self.recv_sems.at[at if at_there is None else at_there],
            device_id=device,
            device_id_type=MESH,
        )

    def send(self, source, target, device):
        copy = self.link(source, target, device, self.take())
        copy.start()
        self.sent.append(copy)
        return copy

    def spread(self, source, targets, slots):
        at = COPIES + self.spreads
        self.spreads += 1
        for target, device in targets:
            self.link(source, target, device, at).start()
        whole = self.link(slots, slots, targets[0][1], at)
        self.sent.append(whole)
        return whole

    def close(self):
        assert self.used <= COPIES and self.spreads <= SPREADS
        for copy in self.sent:
            copy.wait_send()
        self.used, self.sent = 0, []


class Parcel:
    def __init__(self, wires, buffers, source, slot, place, device):
        out, out_scale, into, into_scale = buffers
        value = source[...]
        low = jnp.min(value, axis=0, keepdims=True)
        high = jnp.max(value, axis=0, keepdims=True)
        middle = 0.5 * (low + high)
        reach = jnp.maximum(jnp.maximum(high - middle, middle - low), 1e-30)
        out_scale[slot, 0:1, :] = middle
        out_scale[slot, 1:2, :] = reach * (1.0 / TOP)
        out[slot] = jnp.round((value - middle) * (TOP / reach)).astype(jnp.int16)
        self.rows, self.scale = into.at[place], into_scale.at[place]
        self.copies = (
            wires.link(out.at[slot], self.rows, device, wires.take()),
            wires.link(out_scale.at[slot], self.scale, device, wires.take()),
        )
        for copy in self.copies:
            copy.start()

    def wait_recv(self):
        for copy in self.copies:
            copy.wait_recv()

    def wait_send(self):
        for copy in self.copies:
            copy.wait_send()

    def value(self):
        return self.scale[0:1, :] + self.rows[...].astype(jnp.float32) * self.scale[1:2, :]


def parcel_buffers(rows, columns, out, into):
    return (
        pltpu.VMEM((out, rows, columns), jnp.int16),
        pltpu.VMEM((out, 2, columns), jnp.float32),
        pltpu.VMEM((into, rows, columns), jnp.int16),
        pltpu.VMEM((into, 2, columns), jnp.float32),
    )


def both(copies):
    copies[0].wait_recv()
    copies[1].wait_recv()


def step_kernel(
    sizes,
    target,
    logits,
    filters_in,
    expression,
    spatial,
    prior_in,
    pred_out,
    part,
    profile_out,
    filter_out,
    losses_out,
    filters,
    prior,
    grown,
    weights,
    profiles,
    slab,
    truth_all,
    gate,
    member,
    board,
    mine,
    near_stats,
    far_stats,
    half_y,
    full_y,
    half_bz,
    full_bz,
    half_az,
    full_az,
    half_ay,
    full_ay,
    grads,
    xp,
    xc,
    ended,
    coded_out,
    coded_in,
    scale_out,
    scale_in,
    slide_msgs,
    spot_mine,
    spot_near,
    spot_far,
    column_mine,
    column_near,
    column_far,
    filter_msgs,
    send_sems,
    recv_sems,
    local_sems,
):
    f32, bf16 = jnp.float32, jnp.bfloat16
    z, y = lax.axis_index("z"), lax.axis_index("y")
    x, c = lax.axis_index("x"), lax.axis_index("c")
    wires = Wires(send_sems, recv_sems)
    own = x * 2 + c
    cell = z * 4 + y
    right, left, twin = away("x", 1), away("x", 3), away("c", 1)
    y_up, y_down, z_up, z_down = away("y", 1), away("y", 3), away("z", 1), away("z", 7)

    def spread_y(source, slots):
        return wires.spread(source, [(slots.at[d - 1], away("y", d)) for d in (1, 2, 3)], slots)

    def spread_z(slots):
        others = [(slots.at[d], away("z", d)) for d in range(1, 8)]
        return wires.spread(slots.at[0], others, slots.at[pl.ds(1, 7)])

    def spread_spot(slots):
        others = [(slots.at[d], spot_peer(d)) for d in range(1, 8)]
        return wires.spread(slots.at[0], others, slots.at[pl.ds(1, 7)])

    loads = []
    for b in range(BLOCKS):
        rows = lanes_of(b)
        loads.append(
            pltpu.make_async_copy(logits.at[rows, :], grown.at[rows, :], local_sems.at[b])
        )
    load_own = pltpu.make_async_copy(expression, profiles.at[own], local_sems.at[BLOCKS])
    aligned = pl.multiple_of((cell // 2) * LANES, LANES)
    load_truth = pltpu.make_async_copy(
        spatial.at[:, pl.ds(aligned, LANES)], slab, local_sems.at[BLOCKS + 1]
    )
    load_filters = pltpu.make_async_copy(filters_in, filters, local_sems.at[BLOCKS + 2])
    load_prior = pltpu.make_async_copy(prior_in, prior, local_sems.at[BLOCKS + 3])
    load_filters.start()
    load_own.start()
    for load in loads:
        load.start()
    load_truth.start()
    load_prior.start()
    barrier = pltpu.get_barrier_semaphore()
    targets = (
        [away("y", d) for d in (1, 2, 3)]
        + [away("z", d) for d in range(1, 8)]
        + [spot_peer(d) for d in range(1, 8)]
    )
    for device in targets:
        pl.semaphore_signal(barrier, inc=1, device_id=device, device_id_type=MESH)
    load_filters.wait()
    gates = jax.nn.sigmoid(filters[...])
    for b in range(BLOCKS):
        gate[lanes_of(b), :] = jnp.broadcast_to(gates[b : b + 1, :], (LANES, LANES)).T
    kept = jnp.sum(gates, keepdims=True)
    spread = jnp.sum(gates - gates * gates, keepdims=True)
    column = lax.broadcasted_iota(jnp.int32, (1, COLS), 1)
    mine[3:4, :] = jnp.where(column == 0, kept, jnp.where(column == 1, spread, 0.0))
    mine[0:3, :] = jnp.zeros((3, COLS), f32)
    spot = column + own * COLS
    begin = jnp.int32(0)
    for k in range(SLIDES):
        end = begin + sizes[k]
        within = jnp.logical_and(spot >= begin, spot < end)
        member[k : k + 1, :] = jnp.where(within, 1.0, 0.0)
        begin = end

    load_own.wait()
    with jax.named_scope("greeting"):
        pl.semaphore_wait(barrier, len(targets))
    low_rows, high_rows = pl.ds(0, HALF), pl.ds(HALF, HALF)

    def share(block, rows, device):
        return wires.send(profiles.at[block, rows], profiles.at[block, rows], device)

    def share_whole(block, device):
        return wires.send(profiles.at[block], profiles.at[block], device)

    right_low = share(own, low_rows, right)
    left_high = share(own, high_rows, left)
    twin_own = share_whole(own, twin)
    with jax.named_scope("exponentials"):
        for b in range(BLOCKS):
            loads[b].wait()

            @pl.loop(0, COLS // LANES)
            def _(j, b=b):
                rows, lanes = lanes_of(b), lanes_of(j)
                e = jnp.exp(grown[rows, lanes])
                grown[rows, lanes] = e
                mine[0:1, lanes] += jnp.sum(e, axis=0, keepdims=True)
                mine[1:2, lanes] += jnp.sum(e * gate[rows, :], axis=0, keepdims=True)

    with jax.named_scope("truth"):
        load_truth.wait()
        load_prior.wait()
        truth_all[...] = slab[...].T
        truth = truth_all.at[piece(lax.rem(cell, 2)), :]
        held = truth[...]
        mine[2:3, :] = jnp.sum(held * held, axis=0, keepdims=True)

    with jax.named_scope("totals_y"):
        near = spread_y(mine, near_stats)
        right_high = share(own, high_rows, right)
        left_low = share(own, low_rows, left)
        near.wait_recv()
        far_stats[0] = mine[...] + near_stats[0] + near_stats[1] + near_stats[2]
        far = spread_z(far_stats)
    with jax.named_scope("pass_halves"):
        right_low.wait_recv()
        onward_low = share(block_of(x, 3, c), low_rows, right)
        left_high.wait_recv()
        onward_high = share(block_of(x, 1, c), high_rows, left)
    with jax.named_scope("totals_z"):
        far.wait_recv()
        stats = far_stats[0]
        for d in range(1, 8):
            stats = stats + far_stats[d]
    totals, filtered, truth_square = stats[0:1, :], stats[1:2, :], stats[2:3, :]
    kept, spread = stats[3:4, 0:1], stats[3:4, 1:2]
    density = filtered / totals
    scale = 1.0 / totals

    with jax.named_scope("weights"):

        @pl.loop(0, BLOCKS)
        def _(b):
            rows = lanes_of(b)
            for j in range(COLS // LANES):
                cut = slice(j * LANES, (j + 1) * LANES)
                weights[rows, lanes_of(j)] = (
                    grown[rows, lanes_of(j)] * scale[:, cut] * gate[rows, :]
                ).astype(bf16)

    def multiply(block):
        part[rows_in(block), :] = lax.dot_general(
            profiles[block], weights[...], (((0,), (0,)), ((), ())), preferred_element_type=f32
        )

    sought = [ring(z, d, 8) for d in (4, 3, 5, 2, 6, 1, 7, 0)]
    order = [own, block_of(x, 0, 1 - c)] + [jnp.int32(0)] * 6
    at = jnp.int32(2)
    for block in sought:
        other = jnp.where(block // 2 != x, 1, 0)
        for i in range(2, 8):
            order[i] = order[i] + block * other * jnp.where(at == i, 1, 0)
        at = at + other
    A, B = pl.ds(0, SPLIT), pl.ds(SPLIT, COLS - SPLIT)
    started, passed, parcels = {}, {}, {}

    def parcel(name, buffers, rows, lanes, slot, place, device):
        if (name, slot) in parcels:
            parcels[name, slot].wait_send()
        sent = Parcel(wires, buffers, part.at[rows, lanes], slot, place, device)
        parcels[name, slot] = sent
        return sent

    def arrive(sent, rows, lanes):
        sent.wait_recv()
        part[rows, lanes] += sent.value()

    def y_start(i):
        s, p, slot = order[i], ring(y, 2, 4), 2 * (i % 4)
        started[i] = (
            parcel("y0", half_y, rows_of(s, p, 0, HOP), B, slot, 2 * i, y_up),
            parcel("y0", half_y, rows_of(s, p, HOP, HOP), B, slot + 1, 2 * i + 1, y_down),
        )

    def y_pass(i):
        s, up, down, slot = order[i], ring(y, 1, 4), ring(y, 3, 4), 2 * (i % 4)
        arrive(started[i][0], rows_of(s, up, 0, HOP), B)
        first = parcel("y1", full_y, rows_of(s, up), B, slot, 2 * i, y_up)
        arrive(started[i][1], rows_of(s, down, HOP, HOP), B)
        second = parcel("y1", full_y, rows_of(s, down), B, slot + 1, 2 * i + 1, y_down)
        passed[i] = (first, second)

    def y_end(i):
        both(passed[i])
        part[rows_of(order[i], y), B] += passed[i][0].value() + passed[i][1].value()

    bz, az, ay = {}, {}, {}

    def bz_start():
        d = ring(z, 4, 8)
        bz[0] = (
            parcel("bz0", half_bz, rows_of(d, y, 0, HOP), B, 0, 0, z_up),
            parcel("bz0", half_bz, rows_of(d, y, HOP, HOP), B, 1, 1, z_down),
        )

    def bz_pass(t):
        up, down, place = ring(z, 4 - t, 8), ring(z, t - 4, 8), 2 * (t - 1)
        arrive(bz[t - 1][0], rows_of(up, y, 0, HOP) if t == 1 else rows_of(up, y), B)
        first = parcel("bz1", full_bz, rows_of(up, y), B, 0, place, z_up)
        arrive(bz[t - 1][1], rows_of(down, y, HOP, HOP) if t == 1 else rows_of(down, y), B)
        second = parcel("bz1", full_bz, rows_of(down, y), B, 1, place + 1, z_down)
        bz[t] = (first, second)

    def bz_end():
        both(bz[3])
        part[rows_of(z, y), B] += bz[3][0].value() + bz[3][1].value()

    def az_start(a):
        d, lanes, slot = ring(z, 4, 8), lanes_of(a), 2 * a
        az[a, 0] = (
            parcel("az0", half_az, rows_in(d, 0, LANES), lanes, slot, slot, z_up),
            parcel("az0", half_az, rows_in(d, LANES, LANES), lanes, slot + 1, slot + 1, z_down),
        )

    def az_pass(a, t):
        up, down, lanes = ring(z, 4 - t, 8), ring(z, t - 4, 8), lanes_of(a)
        slot, place = 2 * a, 6 * a + 2 * (t - 1)
        arrive(az[a, t - 1][0], rows_in(up, 0, LANES) if t == 1 else rows_in(up), lanes)
        first = parcel("az1", full_az, rows_in(up), lanes, slot, place, z_up)
        arrive(az[a, t - 1][1], rows_in(down, LANES, LANES) if t == 1 else rows_in(down), lanes)
        second = parcel("az1", full_az, rows_in(down), lanes, slot + 1, place + 1, z_down)
        az[a, t] = (first, second)

    def az_end(a):
        both(az[a, 3])
        part[rows_in(z), lanes_of(a)] += az[a, 3][0].value() + az[a, 3][1].value()

    def ay_start():
        p = ring(y, 2, 4)
        ay[0] = (
            parcel("ay0", half_ay, rows_of(z, p, 0, HOP), A, 0, 0, y_up),
            parcel("ay0", half_ay, rows_of(z, p, HOP, HOP), A, 1, 1, y_down),
        )

    def ay_pass():
        up, down = ring(y, 1, 4), ring(y, 3, 4)
        arrive(ay[0][0], rows_of(z, up, 0, HOP), A)
        first = parcel("ay1", full_ay, rows_of(z, up), A, 0, 0, y_up)
        arrive(ay[0][1], rows_of(z, down, HOP, HOP), A)
        second = parcel("ay1", full_ay, rows_of(z, down), A, 1, 1, y_down)
        ay[1] = (first, second)

    def ay_end():
        both(ay[1])
        part[rows_of(z, y), A] += ay[1][0].value() + ay[1][1].value()

    with jax.named_scope("multiply_near"):
        multiply(own)
        y_start(0)
        twin_own.wait_recv()
        multiply(order[1])
        y_start(1)
    with jax.named_scope("gather_rest"):
        right_high.wait_recv()
        twin_left = share_whole(block_of(x, 3, c), twin)
        left_low.wait_recv()
        twin_right = share_whole(block_of(x, 1, c), twin)
        y_pass(0)
        onward_low.wait_recv()
        twin_low = share(block_of(x, 2, c), low_rows, twin)
        onward_high.wait_recv()
        twin_high = share(block_of(x, 2, c), high_rows, twin)
        twin_left.wait_recv()
        twin_right.wait_recv()
        twin_low.wait_recv()
        twin_high.wait_recv()
    y_pass(1)
    multiply(order[2])
    az_start(0)
    y_start(2)
    az_start(1)
    multiply(order[3])
    az_start(2)
    y_start(3)
    multiply(order[4])
    y_start(4)
    multiply(order[5])
    az_pass(0, 1)
    az_pass(1, 1)
    y_pass(2)
    multiply(order[6])
    az_pass(2, 1)
    y_start(6)
    y_pass(3)
    y_end(0)
    y_pass(4)
    y_end(1)
    y_start(5)
    multiply(order[7])
    y_start(7)
    az_pass(0, 2)
    y_end(2)
    bz_start()
    az_pass(1, 2)
    y_pass(6)
    az_pass(2, 2)
    y_end(3)
    az_pass(0, 3)
    y_end(4)
    bz_pass(1)
    y_pass(5)
    az_pass(1, 3)
    y_pass(7)
    az_pass(2, 3)
    y_end(6)
    az_end(0)
    y_end(5)
    bz_pass(2)
    az_end(1)
    y_end(7)
    az_end(2)
    ay_start()
    bz_pass(3)
    ay_pass()
    bz_end()
    ay_end()

    gene_scale, spot_scale = 1.0 / (SLIDES * GENES), 1.0 / SPOTS
    with jax.named_scope("local_sums"):
        pv, tv = part[rows_of(z, y), :], truth[...]
        pred_out[...] = pv
        cross, square, tsquare = pv * tv, pv * pv, tv * tv
        spot_mine[0:1, :] = jnp.sum(cross, axis=0, keepdims=True)
        spot_mine[1:2, :] = jnp.sum(square, axis=0, keepdims=True)
        near = spread_y(spot_mine, spot_near)
        lane = lax.broadcasted_iota(jnp.int32, (PIECE, LANES), 1)
        row_lane = lax.broadcasted_iota(jnp.int32, (1, LANES), 1)
        packed, extra = jnp.zeros((PIECE, LANES), f32), jnp.zeros((1, LANES), f32)
        for k in range(SLIDES):
            inside = member[k : k + 1, :]
            for q, field in enumerate((cross, square, tsquare)):
                summed = jnp.sum(field * inside, axis=1, keepdims=True)
                packed = packed + jnp.where(lane == q * SLIDES + k, summed, 0.0)
            for q, field in enumerate((density, prior[...])):
                summed = jnp.sum(field * inside, axis=1, keepdims=True)
                extra = extra + jnp.where(row_lane == q * SLIDES + k, summed, 0.0)
        board[...] = jnp.zeros((LANES, LANES), f32)
        board[0:PIECE, :] = packed
        slide_msgs[0] = board[...].T[0:16, :]
        slide_msgs[0, 12:13, :] = extra
        slide = spread_spot(slide_msgs)
    with jax.named_scope("spot_sums_y"):
        near.wait_recv()
        spot_far[0] = spot_mine[...] + spot_near[0] + spot_near[1] + spot_near[2]
        far = spread_z(spot_far)
    with jax.named_scope("slide_sums"):
        slide.wait_recv()
        slide_total = slide_msgs[0]
        for d in range(1, 8):
            slide_total = slide_total + slide_msgs[d]
        s_inner, s_square, s_truth = slide_total[0:4], slide_total[4:8], slide_total[8:12]
        s_left, s_right = lax.rsqrt(s_square + epsilon), lax.rsqrt(s_truth + epsilon)
        own_genes = lax.broadcasted_iota(jnp.int32, (SLIDES, LANES), 1) < PIECE
        gene_sum = jnp.sum(jnp.where(own_genes, s_inner * s_left * s_right, 0.0), keepdims=True)
        board[...] = jnp.zeros((LANES, LANES), f32)
        board[0:4, :] = s_inner * s_left * s_left * s_left * s_right
        board[4:8, :] = s_left * s_right
        columns = board[...].T[0:PIECE, :]
        cube_of, flat_of = jnp.zeros((PIECE, COLS), f32), jnp.zeros((PIECE, COLS), f32)
        spot_density, spot_prior = jnp.zeros((1, COLS), f32), jnp.zeros((1, COLS), f32)
        for k in range(SLIDES):
            inside = member[k : k + 1, :]
            cube_of = cube_of + columns[:, k : k + 1] * inside
            flat_of = flat_of + columns[:, 4 + k : 5 + k] * inside
            spot_density = spot_density + slide_total[12:13, k : k + 1] * inside
            spot_prior = spot_prior + slide_total[12:13, 4 + k : 5 + k] * inside
        target_share = prior[...] / spot_prior
        logs = jnp.log(target_share) - jnp.log(density / spot_density)
        density_part = jnp.sum(target_share * logs, keepdims=True) / SLIDES
        grad_density = (1.0 / spot_density - target_share / density) / SLIDES
        gene_part = gene_scale * (cube_of * pv - flat_of * tv)
    with jax.named_scope("spot_sums_z"):
        far.wait_recv()
        spot_total = spot_far[0]
        for d in range(1, 8):
            spot_total = spot_total + spot_far[d]
        p_inner, p_square = spot_total[0:1, :], spot_total[1:2, :]
        p_left, p_right = lax.rsqrt(p_square + epsilon), lax.rsqrt(truth_square + epsilon)
        spot_sum = jnp.sum(p_inner * p_left * p_right, keepdims=True)
        spot_cube = p_inner * p_left * p_left * p_left * p_right
        grad = gene_part + spot_scale * (spot_cube * pv - (p_left * p_right) * tv)
        grads[z, piece(y), :] = grad.astype(bf16)
    with jax.named_scope("sends_done"):
        for sent in parcels.values():
            sent.wait_send()
        wires.close()

    A, B = pl.ds(0, CLOSE), pl.ds(CLOSE, COLS - CLOSE)
    blocks = [ring(z, d, 8) for d in REACH]

    def put(block, rows, lanes, device):
        view = grads.at[block, rows, lanes]
        return wires.send(view, view, device)

    def y_share(block, lanes):
        return put(block, piece(y), lanes, y_up), put(block, piece(y), lanes, y_down)

    def y_onward(block, lanes, shared):
        shared[0].wait_recv()
        up = put(block, piece(ring(y, 3, 4), 0, HOP), lanes, y_up)
        shared[1].wait_recv()
        down = put(block, piece(ring(y, 1, 4), HOP, HOP), lanes, y_down)
        return up, down

    def z_share(step, rows, lanes):
        above, below = ring(z, 1 - step, 8), ring(z, step - 1, 8)
        return put(above, rows[0], lanes, z_up), put(below, rows[1], lanes, z_down)

    own_rows, all_rows = (piece(y), piece(y)), (pl.ds(0, OWN), pl.ds(0, OWN))
    own_halves = (piece(y, 0, HOP), piece(y, HOP, HOP))
    all_halves = (pl.ds(0, LANES), pl.ds(LANES, LANES))
    base = wires.take(57)

    def each(turn, body):
        if turn in (0, 4):
            body(2 * turn - (turn > 0), ring(z, turn, 8))
        else:

            @pl.loop(0, 2)
            def _(i):
                body(2 * turn - 1 + i, ring(z, turn * (1 - 2 * i), 8))

    keep, give = c * HALF, (1 - c) * HALF

    def some_rows(first, size=HALF):
        return pl.ds(pl.multiple_of(first, 16), size)

    def twin_link(n):
        return wires.link(xp.at[n, some_rows(give)], xc.at[n], twin, base + n)

    def out_slot(k, odd, i):
        return 2 * (k + 6 * odd) + i

    def in_slot(k, odd, i, core):
        if k < 2:
            return 16 + 2 * (k + 2 * odd) + i
        return 2 * (k - 2 + 4 * core) + i

    def eighth_links(k, odd, i):
        here, there = out_slot(k, odd, i), in_slot(k, odd, i, c)
        device = right if k in (0, 2, 3) else left
        if k > 1:
            device = {"x": device["x"], "c": odd}
        return (
            wires.link(
                scale_out.at[here], scale_in.at[there], device, base + 8 + here, base + 8 + there
            ),
            wires.link(
                coded_out.at[here], coded_in.at[there], device, base + 32 + here, base + 32 + there
            ),
        )

    def eighth(i):
        return some_rows(i * EIGHTH, EIGHTH)

    def kept_eighth(high, i):
        return some_rows(keep + (2 * high + i) * EIGHTH, EIGHTH)

    def eighth_send(n, odd, high, k, i):
        summed = xp[n, kept_eighth(high, i), :]
        top = jnp.maximum(jnp.max(jnp.abs(summed), axis=0, keepdims=True), 1e-30)
        here = out_slot(k, odd, i)
        scale_out[here] = top * (1.0 / TOP)
        coded_out[here] = jnp.round(summed * (TOP / top)).astype(jnp.int16)
        for link in eighth_links(k, odd, i):
            link.start()

    def eighth_value(k, odd, i, core):
        there = in_slot(k, odd, i, core)
        wires.link(scale_in.at[there], scale_in.at[there], twin, base + 8 + there).wait_recv()
        wires.link(coded_in.at[there], coded_in.at[there], twin, base + 32 + there).wait_recv()
        return coded_in[there].astype(f32) * scale_in[there]

    def distance(block):
        return ring(block // 2 - x, 0, 4)

    def block_first(n, block):
        xp[n] = lax.dot_general(
            weights[...],
            grads[block],
            (((1,), (1,)), ((), ())),
            preferred_element_type=f32,
        )
        twin_link(n).start()

    def cell_part(n, block):
        product = jnp.dot(profiles[block], grads[block], preferred_element_type=f32)
        if isinstance(n, int) and n == 0:
            part[0:ROWS, :] = product
        else:
            part[0:ROWS, :] += product

    at_own, at_twin = jnp.int32(0), jnp.int32(0)
    for n in range(8):
        at_own = at_own + n * jnp.where(blocks[n] == own, 1, 0)
        at_twin = at_twin + n * jnp.where(blocks[n] == block_of(x, 0, 1 - c), 1, 0)
    ending = wires.link(xp.at[at_twin, some_rows(keep)], ended, twin, base + 56)

    def block_second(n, block):
        odd = lax.rem(block, 2)
        twin_link(n).wait_recv()

        @pl.loop(0, 4)
        def _(i):
            xp[n, some_rows(keep + i * EIGHTH, EIGHTH), :] += xc[n, eighth(i), :]

        @pl.when(distance(block) == 2)
        def _():
            @pl.loop(0, 2)
            def _(i):
                eighth_send(n, odd, 0, 0, i)
                eighth_send(n, odd, 1, 1, i)

        @pl.when(distance(block) == 1)
        def _():
            @pl.loop(0, 2)
            def _(i):
                eighth_send(n, odd, 1, 2, i)

        @pl.when(distance(block) == 3)
        def _():
            @pl.loop(0, 2)
            def _(i):
                eighth_send(n, odd, 0, 4, i)

        @pl.when(block == block_of(x, 0, 1 - c))
        def _():
            ending.start()

    def add_and_send(n, odd, high, k, onward):
        @pl.loop(0, 2)
        def _(i):
            xp[n, kept_eighth(high, i), :] += eighth_value(k, odd, i, c)
            eighth_send(n, odd, high, onward, i)

    def block_third(n, block):
        odd = lax.rem(block, 2)

        @pl.when(distance(block) == 1)
        def _():
            add_and_send(n, odd, 0, 0, 3)

        @pl.when(distance(block) == 3)
        def _():
            add_and_send(n, odd, 1, 1, 5)

    def one(body, n):
        body(n, blocks[n])

    bz, az, shared_b, onward_b = {1: z_share(1, own_rows, B)}, {}, {}, {}
    straight = wires.spread(
        grads.at[z, piece(y), A],
        [(grads.at[z, piece(y), A], away("y", d)) for d in (1, 3, 2)],
        grads.at[z, pl.ds(0, 3 * PIECE), A],
    )
    shared_b[0] = y_share(z, B)
    rounds = {0: (0,), 1: (1, 2), 2: (3, 4), 3: (5, 6), 4: (7,)}

    def turn_b(turn):
        both(bz[turn])
        if turn < 4:
            bz[turn + 1] = z_share(turn + 1, own_rows if turn < 3 else own_halves, B)
        for n in rounds[turn]:
            shared_b[n] = y_share(blocks[n], B)

    def turn_a(turn):
        if turn:
            both(az[turn])
        else:
            straight.wait_recv()
        if turn < 4:
            az[turn + 1] = z_share(turn + 1, all_rows if turn < 3 else all_halves, A)

    def turn_on(turn):
        for n in rounds[turn]:
            onward_b[n] = y_onward(blocks[n], B, shared_b[n])

    def turn_first(turn):
        for n in rounds[turn]:
            both(onward_b[n])
        each(turn, block_first)

    turn_b(1)
    turn_a(0)
    turn_b(2)
    turn_on(0)
    turn_a(1)
    turn_on(1)
    turn_on(2)
    turn_b(3)
    turn_first(0)
    turn_a(2)
    turn_first(2)
    turn_on(3)
    turn_first(1)
    one(block_second, 0)
    one(block_second, 3)
    one(block_second, 4)
    turn_b(4)
    turn_a(3)
    turn_first(3)
    each(0, cell_part)
    turn_a(4)
    turn_on(4)
    one(block_second, 1)
    one(block_second, 2)
    one(block_second, 5)
    each(1, cell_part)
    one(block_second, 6)
    turn_first(4)
    each(2, cell_part)
    each(3, cell_part)
    one(block_second, 7)
    each(4, cell_part)

    with jax.named_scope("column_sums"):
        column_mine[...] = jnp.zeros((2, COLS), f32)
        column_mine[1:2, :] = jnp.where(column == 0, gene_sum, 0.0)
        for b in range(BLOCKS):
            rows = lanes_of(b)
            across = jnp.zeros((LANES, LANES), f32)
            for j in range(COLS // LANES):
                lanes, cut = lanes_of(j), slice(j * LANES, (j + 1) * LANES)
                whole = (grown[rows, lanes] * scale[:, cut]) * (
                    part[rows, lanes] + grad_density[:, cut]
                )
                part[rows, lanes] = whole
                across = across + whole
                column_mine[0:1, lanes] += jnp.sum(whole * gate[rows, :], axis=0, keepdims=True)
            filter_msgs[0, b : b + 1, :] = jnp.sum(across.T, axis=0, keepdims=True)
        filter_msgs[0, 11:12, :] = jnp.where(
            row_lane == 0, spot_sum, jnp.where(row_lane == 1, density_part, 0.0)
        )
        filter_msgs[0, 12:16, :] = jnp.zeros((4, LANES), f32)
        near = spread_y(column_mine, column_near)
        sums = spread_spot(filter_msgs)
    for n in (0, 1, 2, 4):
        one(block_third, n)
    with jax.named_scope("column_sums_y"):
        near.wait_recv()
        column_far[0] = column_mine[...] + column_near[0] + column_near[1] + column_near[2]
        far = spread_z(column_far)
    for n in (3, 5, 6, 7):
        one(block_third, n)
    with jax.named_scope("column_sums_z"):
        far.wait_recv()
        column_total = column_far[0]
        for d in range(1, 8):
            column_total = column_total + column_far[d]
    with jax.named_scope("logits_gradient"):
        dot_scale = column_total[0:1, :] * scale
        for b in range(BLOCKS):
            rows = lanes_of(b)
            for j in range(COLS // LANES):
                lanes, cut = lanes_of(j), slice(j * LANES, (j + 1) * LANES)
                part[rows, lanes] = (
                    gate[rows, :] * part[rows, lanes] - grown[rows, lanes] * dot_scale[:, cut]
                )
    with jax.named_scope("filter_gradient"):
        sums.wait_recv()
        filter_total = filter_msgs[0]
        for d in range(1, 8):
            filter_total = filter_total + filter_msgs[d]
        gap = kept - target[0].astype(f32)
        root = jnp.sqrt(gap * gap + 1.0)
        on = filter_total[0:BLOCKS, :] + gap / root / CELLS + (1.0 - 2.0 * gates) / CELLS
        filter_out[...] = on * gates * (1.0 - gates)
        values = (
            -column_total[1:2, 0:1] * gene_scale,
            -filter_total[11:12, 0:1] * spot_scale,
            filter_total[11:12, 1:2],
            root / CELLS,
            spread / CELLS,
        )
        losses = jnp.zeros((1, LANES), f32)
        for k, value in enumerate(values):
            losses = losses + jnp.where(row_lane == k, value, 0.0)
        losses_out[...] = losses

    with jax.named_scope("last_sum"):
        ending.wait_recv()
        for core_rows, core in ((keep, c), (give, 1 - c)):
            for high, ks in ((0, (3, 4)), (1, (2, 5))):

                @pl.loop(0, 2)
                def _(i, core_rows=core_rows, core=core, high=high, ks=ks):
                    rows = some_rows(core_rows + (2 * high + i) * EIGHTH, EIGHTH)
                    if core is c:
                        start = xp[at_own, rows, :]
                    else:
                        start = ended[some_rows((2 * high + i) * EIGHTH, EIGHTH), :]
                    total = start + eighth_value(ks[0], 0, i, core)
                    profile_out[rows, :] = total + eighth_value(ks[1], 0, i, core)

    with jax.named_scope("sends_done"):
        for n in range(8):
            twin_link(n).wait_send()
        for odd in range(2):
            for k in range(6):
                for i in range(2):
                    for link in eighth_links(k, odd, i):
                        link.wait_send()
        ending.wait_send()
    with jax.named_scope("wires_done"):
        wires.close()


def training_step(sizes, target, logits, filters, expression, spatial, prior):
    f32, bf16 = jnp.float32, jnp.bfloat16
    anywhere = pl.BlockSpec(memory_space=pl.ANY)
    inside = pl.BlockSpec(memory_space=pltpu.VMEM)
    scalars = pl.BlockSpec(memory_space=pltpu.SMEM)
    near = COLS - SPLIT
    return pl.pallas_call(
        step_kernel,
        out_shape=(
            pltpu.VMEM((PIECE, COLS), f32),
            pltpu.VMEM((GENES, COLS), f32),
            pltpu.VMEM((ROWS, OWN), f32),
            pltpu.VMEM((BLOCKS, LANES), f32),
            pltpu.VMEM((1, LANES), f32),
        ),
        in_specs=[scalars, scalars, anywhere, anywhere, anywhere, anywhere, anywhere],
        out_specs=(inside, inside, inside, inside, inside),
        scratch_shapes=[
            pltpu.VMEM((BLOCKS, LANES), f32),
            pltpu.VMEM((1, COLS), f32),
            pltpu.VMEM((ROWS, COLS), f32),
            pltpu.VMEM((ROWS, COLS), bf16),
            pltpu.VMEM((8, ROWS, OWN), bf16),
            pltpu.VMEM((COLS, LANES), f32),
            pltpu.VMEM((LANES, COLS), f32),
            pltpu.VMEM((ROWS, LANES), f32),
            pltpu.VMEM((SLIDES, COLS), f32),
            pltpu.VMEM((LANES, LANES), f32),
            pltpu.VMEM((4, COLS), f32),
            pltpu.VMEM((3, 4, COLS), f32),
            pltpu.VMEM((8, 4, COLS), f32),
            parcel_buffers(HOP, near, 8, 16),
            parcel_buffers(PIECE, near, 8, 16),
            parcel_buffers(HOP, near, 2, 2),
            parcel_buffers(PIECE, near, 2, 6),
            parcel_buffers(LANES, LANES, 2 * GROUPS, 2 * GROUPS),
            parcel_buffers(OWN, LANES, 2 * GROUPS, 6 * GROUPS),
            parcel_buffers(HOP, SPLIT, 2, 2),
            parcel_buffers(PIECE, SPLIT, 2, 2),
            pltpu.VMEM((8, OWN, COLS), bf16),
            pltpu.VMEM((8, ROWS, OWN), f32),
            pltpu.VMEM((8, HALF, OWN), f32),
            pltpu.VMEM((HALF, OWN), f32),
            pltpu.VMEM((24, EIGHTH, OWN), jnp.int16),
            pltpu.VMEM((24, EIGHTH, OWN), jnp.int16),
            pltpu.VMEM((24, 1, OWN), f32),
            pltpu.VMEM((24, 1, OWN), f32),
            pltpu.VMEM((8, 16, LANES), f32),
            pltpu.VMEM((2, COLS), f32),
            pltpu.VMEM((3, 2, COLS), f32),
            pltpu.VMEM((8, 2, COLS), f32),
            pltpu.VMEM((2, COLS), f32),
            pltpu.VMEM((3, 2, COLS), f32),
            pltpu.VMEM((8, 2, COLS), f32),
            pltpu.VMEM((8, 16, LANES), f32),
            pltpu.SemaphoreType.DMA((COPIES + SPREADS,)),
            pltpu.SemaphoreType.DMA((COPIES + SPREADS,)),
            pltpu.SemaphoreType.DMA((BLOCKS + 4,)),
        ],
        compiler_params=pltpu.CompilerParams(
            collective_id=0, has_side_effects=True, vmem_limit_bytes=LIMIT
        ),
        name="training_step",
    )(sizes, target, logits, filters, expression, spatial, prior)


def finish_kernel(
    losses,
    pred,
    part,
    profile,
    filter_rows,
    losses_out,
    pred_out,
    logits_out,
    profile_out,
    filter_out,
    sems,
):
    pieces = [(part.at[0:ROWS], logits_out), (profile, profile_out), (pred, pred_out)]
    pieces.append((filter_rows, filter_out))
    copies = [pltpu.make_async_copy(a, b, sems.at[i]) for i, (a, b) in enumerate(pieces)]
    for copy in copies:
        copy.start()
    row_lane = lax.broadcasted_iota(jnp.int32, (1, LANES), 1)
    for k in range(5):
        losses_out[k] = jnp.sum(jnp.where(row_lane == k, losses[...], 0.0))
    for copy in copies:
        copy.wait()


def finish(losses, pred, part, profile, filter_rows):
    f32 = jnp.float32
    anywhere = pl.BlockSpec(memory_space=pl.ANY)
    inside = pl.BlockSpec(memory_space=pltpu.VMEM)
    scalars = pl.BlockSpec(memory_space=pltpu.SMEM)
    return pl.pallas_call(
        finish_kernel,
        out_shape=(
            jax.ShapeDtypeStruct((5,), f32),
            jax.ShapeDtypeStruct((PIECE, COLS), f32),
            jax.ShapeDtypeStruct((ROWS, COLS), f32),
            jax.ShapeDtypeStruct((ROWS, OWN), f32),
            jax.ShapeDtypeStruct((BLOCKS, LANES), f32),
        ),
        in_specs=[inside] * 5,
        out_specs=(scalars, anywhere, anywhere, anywhere, anywhere),
        scratch_shapes=[pltpu.SemaphoreType.DMA((4,))],
        compiler_params=pltpu.CompilerParams(vmem_limit_bytes=1024 * 1024),
        name="finish",
    )(losses, pred, part, profile, filter_rows)


def on_device(logits, filter_logits, expression, spatial, prior, slide_sizes, target):
    pred, part, profile, filter_rows, losses = training_step(
        slide_sizes,
        target,
        logits,
        filter_logits.reshape(BLOCKS, LANES),
        expression,
        spatial,
        prior.reshape(1, COLS),
    )
    losses, pred, grad_logits, grad_expression, grad_filter = finish(
        losses, pred, part, profile, filter_rows
    )
    return (losses, pred.T, grad_logits, grad_filter.reshape(-1), grad_expression)


def solution(mesh):
    split = Mesh(mesh.devices.reshape(8, 4, 4, 2), ("z", "y", "x", "c"))
    return jax.shard_map(
        on_device,
        mesh=split,
        in_specs=(P(CELL, SPOT), P(CELL), P(CELL, SPOT), P(SPOT, None), P(SPOT), P(), P()),
        out_specs=(P(), P(SPOT, CELL), P(CELL, SPOT), P(CELL), P(CELL, SPOT)),
        check_vma=False,
    )
```

```python
import jax
import jax.numpy as jnp
from jax import lax
from jax.experimental import pallas as pl
from jax.experimental.pallas import tpu as pltpu
from jax.sharding import Mesh
from jax.sharding import PartitionSpec as P

CELL = ("z", "y")
SPOT = ("x", "c")
SIZE = {"z": 8, "y": 4, "x": 4, "c": 2}
MESH = pl.DeviceIdType.MESH
ROWS = 1408
COLS = 1024
OWN = 256
PIECE = 64
LANES = 128
BLOCKS = ROWS // LANES
SLIDES = 4
GENES = PIECE * 32
CELLS = ROWS * 32
SPOTS = COLS * 8
HALF = ROWS // 2
HOP = PIECE // 2
EIGHTH = HALF // 4
TOP = 32767.0
SPLIT = 384
GROUPS = SPLIT // LANES
CLOSE = 384
REACH = (0, 1, 7, 2, 6, 3, 5, 4)
COPIES, SPREADS = 149, 10
LIMIT = 52 * 1024 * 1024

epsilon = 1e-06


def ring(position, step, size):
    return lax.rem(position + step + size, size)


def away(axis, step):
    return {axis: ring(lax.axis_index(axis), step, SIZE[axis])}


def spot_peer(step):
    place = lax.rem(lax.axis_index("x") * 2 + lax.axis_index("c") + step, 8)
    return {"x": place // 2, "c": lax.rem(place, 2)}


def block_of(x, step, c):
    return ring(x, step, 4) * 2 + c


def lanes_of(j, size=LANES):
    if isinstance(j, int):
        return pl.ds(j * size, size)
    return pl.ds(pl.multiple_of(j * size, size), size)


def piece(position, extra=0, size=PIECE):
    return pl.ds(pl.multiple_of(position * PIECE, PIECE) + extra, size)


def rows_in(block, extra=0, size=OWN):
    return pl.ds(pl.multiple_of(block * OWN, OWN) + extra, size)


def rows_of(block, position, extra=0, size=PIECE):
    return pl.ds(pl.multiple_of(block * OWN + position * PIECE, PIECE) + extra, size)


class Wires:
    def __init__(self, send_sems, recv_sems):
        self.send_sems, self.recv_sems, self.sent = send_sems, recv_sems, []
        self.used, self.spreads = 0, 0

    def take(self, count=1):
        at = self.used
        self.used += count
        return at

    def link(self, source, target, device, at, at_there=None):
        return pltpu.make_async_remote_copy(
            src_ref=source,
            dst_ref=target,
            send_sem=self.send_sems.at[at],
            recv_sem=self.recv_sems.at[at if at_there is None else at_there],
            device_id=device,
            device_id_type=MESH,
        )

    def send(self, source, target, device):
        copy = self.link(source, target, device, self.take())
        copy.start()
        self.sent.append(copy)
        return copy

    def spread(self, source, targets, slots):
        at = COPIES + self.spreads
        self.spreads += 1
        for target, device in targets:
            self.link(source, target, device, at).start()
        whole = self.link(slots, slots, targets[0][1], at)
        self.sent.append(whole)
        return whole

    def close(self):
        assert self.used <= COPIES and self.spreads <= SPREADS
        for copy in self.sent:
            copy.wait_send()
        self.used, self.sent = 0, []


class Parcel:
    def __init__(self, wires, buffers, source, slot, place, device):
        out, out_scale, into, into_scale = buffers
        value = source[...]
        low = jnp.min(value, axis=0, keepdims=True)
        high = jnp.max(value, axis=0, keepdims=True)
        middle = 0.5 * (low + high)
        reach = jnp.maximum(jnp.maximum(high - middle, middle - low), 1e-30)
        out_scale[slot, 0:1, :] = middle
        out_scale[slot, 1:2, :] = reach * (1.0 / TOP)
        out[slot] = jnp.round((value - middle) * (TOP / reach)).astype(jnp.int16)
        self.rows, self.scale = into.at[place], into_scale.at[place]
        self.copies = (
            wires.link(out.at[slot], self.rows, device, wires.take()),
            wires.link(out_scale.at[slot], self.scale, device, wires.take()),
        )
        for copy in self.copies:
            copy.start()

    def wait_recv(self):
        for copy in self.copies:
            copy.wait_recv()

    def wait_send(self):
        for copy in self.copies:
            copy.wait_send()

    def value(self):
        return self.scale[0:1, :] + self.rows[...].astype(jnp.float32) * self.scale[1:2, :]


def parcel_buffers(rows, columns, out, into):
    return (
        pltpu.VMEM((out, rows, columns), jnp.int16),
        pltpu.VMEM((out, 2, columns), jnp.float32),
        pltpu.VMEM((into, rows, columns), jnp.int16),
        pltpu.VMEM((into, 2, columns), jnp.float32),
    )


def both(copies):
    copies[0].wait_recv()
    copies[1].wait_recv()


def step_kernel(
    sizes,
    target,
    logits,
    filters_in,
    expression,
    spatial,
    prior_in,
    pred_out,
    part,
    profile_out,
    filter_out,
    losses_out,
    filters,
    prior,
    grown,
    weights,
    profiles,
    slab,
    truth_all,
    gate,
    member,
    board,
    mine,
    near_stats,
    far_stats,
    half_y,
    full_y,
    half_bz,
    full_bz,
    half_az,
    full_az,
    half_ay,
    full_ay,
    grads,
    xp,
    xc,
    ended,
    coded_out,
    coded_in,
    scale_out,
    scale_in,
    slide_msgs,
    spot_mine,
    spot_near,
    spot_far,
    column_mine,
    column_near,
    column_far,
    filter_msgs,
    send_sems,
    recv_sems,
    local_sems,
):
    f32, bf16 = jnp.float32, jnp.bfloat16
    z, y = lax.axis_index("z"), lax.axis_index("y")
    x, c = lax.axis_index("x"), lax.axis_index("c")
    wires = Wires(send_sems, recv_sems)
    own = x * 2 + c
    cell = z * 4 + y
    right, left, twin = away("x", 1), away("x", 3), away("c", 1)
    y_up, y_down, z_up, z_down = away("y", 1), away("y", 3), away("z", 1), away("z", 7)

    def spread_y(source, slots):
        return wires.spread(source, [(slots.at[d - 1], away("y", d)) for d in (1, 2, 3)], slots)

    def spread_z(slots):
        others = [(slots.at[d], away("z", d)) for d in range(1, 8)]
        return wires.spread(slots.at[0], others, slots.at[pl.ds(1, 7)])

    def spread_spot(slots):
        others = [(slots.at[d], spot_peer(d)) for d in range(1, 8)]
        return wires.spread(slots.at[0], others, slots.at[pl.ds(1, 7)])

    barrier = pltpu.get_barrier_semaphore()
    targets = (
        [away("y", d) for d in (1, 2, 3)]
        + [away("z", d) for d in range(1, 8)]
        + [spot_peer(d) for d in range(1, 8)]
    )
    for device in targets:
        pl.semaphore_signal(barrier, inc=1, device_id=device, device_id_type=MESH)
    loads = []
    for b in range(BLOCKS):
        rows = lanes_of(b)
        loads.append(
            pltpu.make_async_copy(logits.at[rows, :], grown.at[rows, :], local_sems.at[b])
        )
    load_own = pltpu.make_async_copy(expression, profiles.at[own], local_sems.at[BLOCKS])
    aligned = pl.multiple_of((cell // 2) * LANES, LANES)
    load_truth = pltpu.make_async_copy(
        spatial.at[:, pl.ds(aligned, LANES)], slab, local_sems.at[BLOCKS + 1]
    )
    load_filters = pltpu.make_async_copy(filters_in, filters, local_sems.at[BLOCKS + 2])
    load_prior = pltpu.make_async_copy(prior_in, prior, local_sems.at[BLOCKS + 3])
    load_filters.start()
    load_own.start()
    for load in loads:
        load.start()
    load_truth.start()
    load_prior.start()
    load_own.wait()
    with jax.named_scope("greeting"):
        pl.semaphore_wait(barrier, len(targets))
    low_rows, high_rows = pl.ds(0, HALF), pl.ds(HALF, HALF)

    def share(block, rows, device):
        return wires.send(profiles.at[block, rows], profiles.at[block, rows], device)

    def share_whole(block, device):
        return wires.send(profiles.at[block], profiles.at[block], device)

    right_low = share(own, low_rows, right)
    left_high = share(own, high_rows, left)
    twin_own = share_whole(own, twin)
    load_filters.wait()
    gates = jax.nn.sigmoid(filters[...])
    for b in range(BLOCKS):
        gate[lanes_of(b), :] = jnp.broadcast_to(gates[b : b + 1, :], (LANES, LANES)).T
    kept = jnp.sum(gates, keepdims=True)
    spread = jnp.sum(gates - gates * gates, keepdims=True)
    column = lax.broadcasted_iota(jnp.int32, (1, COLS), 1)
    mine[3:4, :] = jnp.where(column == 0, kept, jnp.where(column == 1, spread, 0.0))
    mine[0:3, :] = jnp.zeros((3, COLS), f32)
    spot = column + own * COLS
    begin = jnp.int32(0)
    for k in range(SLIDES):
        end = begin + sizes[k]
        within = jnp.logical_and(spot >= begin, spot < end)
        member[k : k + 1, :] = jnp.where(within, 1.0, 0.0)
        begin = end

    with jax.named_scope("exponentials"):
        for b in range(BLOCKS):
            loads[b].wait()

            @pl.loop(0, COLS // LANES)
            def _(j, b=b):
                rows, lanes = lanes_of(b), lanes_of(j)
                e = jnp.exp(grown[rows, lanes])
                grown[rows, lanes] = e
                mine[0:1, lanes] += jnp.sum(e, axis=0, keepdims=True)
                mine[1:2, lanes] += jnp.sum(e * gate[rows, :], axis=0, keepdims=True)

    with jax.named_scope("truth"):
        load_truth.wait()
        load_prior.wait()
        truth_all[...] = slab[...].T
        truth = truth_all.at[piece(lax.rem(cell, 2)), :]
        held = truth[...]
        mine[2:3, :] = jnp.sum(held * held, axis=0, keepdims=True)

    with jax.named_scope("totals_y"):
        near = spread_y(mine, near_stats)
        right_high = share(own, high_rows, right)
        left_low = share(own, low_rows, left)
        near.wait_recv()
        far_stats[0] = mine[...] + near_stats[0] + near_stats[1] + near_stats[2]
        far = spread_z(far_stats)
    with jax.named_scope("pass_halves"):
        right_low.wait_recv()
        onward_low = share(block_of(x, 3, c), low_rows, right)
        twin_left_low = share(block_of(x, 3, c), low_rows, twin)
        left_high.wait_recv()
        onward_high = share(block_of(x, 1, c), high_rows, left)
        twin_right_high = share(block_of(x, 1, c), high_rows, twin)
    with jax.named_scope("totals_z"):
        far.wait_recv()
        stats = far_stats[0]
        for d in range(1, 8):
            stats = stats + far_stats[d]
    totals, filtered, truth_square = stats[0:1, :], stats[1:2, :], stats[2:3, :]
    kept, spread = stats[3:4, 0:1], stats[3:4, 1:2]
    density = filtered / totals
    scale = 1.0 / totals

    with jax.named_scope("weights"):

        @pl.loop(0, BLOCKS)
        def _(b):
            rows = lanes_of(b)
            for j in range(COLS // LANES):
                cut = slice(j * LANES, (j + 1) * LANES)
                weights[rows, lanes_of(j)] = (
                    grown[rows, lanes_of(j)] * scale[:, cut] * gate[rows, :]
                ).astype(bf16)

    def multiply(block):
        part[rows_in(block), :] = lax.dot_general(
            profiles[block], weights[...], (((0,), (0,)), ((), ())), preferred_element_type=f32
        )

    sought = [ring(z, d, 8) for d in (4, 3, 5, 2, 6, 1, 7, 0)]
    order = [own, block_of(x, 0, 1 - c)] + [jnp.int32(0)] * 6
    at = jnp.int32(2)
    for block in sought:
        other = jnp.where(block // 2 != x, 1, 0)
        for i in range(2, 8):
            order[i] = order[i] + block * other * jnp.where(at == i, 1, 0)
        at = at + other
    A, B = pl.ds(0, SPLIT), pl.ds(SPLIT, COLS - SPLIT)
    started, passed, parcels = {}, {}, {}

    def parcel(name, buffers, rows, lanes, slot, place, device):
        if (name, slot) in parcels:
            parcels[name, slot].wait_send()
        sent = Parcel(wires, buffers, part.at[rows, lanes], slot, place, device)
        parcels[name, slot] = sent
        return sent

    def arrive(sent, rows, lanes):
        sent.wait_recv()
        part[rows, lanes] += sent.value()

    def y_start(i):
        s, p, slot = order[i], ring(y, 2, 4), 2 * (i % 4)
        started[i] = (
            parcel("y0", half_y, rows_of(s, p, 0, HOP), B, slot, 2 * i, y_up),
            parcel("y0", half_y, rows_of(s, p, HOP, HOP), B, slot + 1, 2 * i + 1, y_down),
        )

    def y_pass(i):
        s, up, down, slot = order[i], ring(y, 1, 4), ring(y, 3, 4), 2 * (i % 4)
        arrive(started[i][0], rows_of(s, up, 0, HOP), B)
        first = parcel("y1", full_y, rows_of(s, up), B, slot, 2 * i, y_up)
        arrive(started[i][1], rows_of(s, down, HOP, HOP), B)
        second = parcel("y1", full_y, rows_of(s, down), B, slot + 1, 2 * i + 1, y_down)
        passed[i] = (first, second)

    def y_end(i):
        both(passed[i])
        part[rows_of(order[i], y), B] += passed[i][0].value() + passed[i][1].value()

    bz, az, ay = {}, {}, {}

    def bz_start():
        d = ring(z, 4, 8)
        bz[0] = (
            parcel("bz0", half_bz, rows_of(d, y, 0, HOP), B, 0, 0, z_up),
            parcel("bz0", half_bz, rows_of(d, y, HOP, HOP), B, 1, 1, z_down),
        )

    def bz_pass(t):
        up, down, place = ring(z, 4 - t, 8), ring(z, t - 4, 8), 2 * (t - 1)
        arrive(bz[t - 1][0], rows_of(up, y, 0, HOP) if t == 1 else rows_of(up, y), B)
        first = parcel("bz1", full_bz, rows_of(up, y), B, 0, place, z_up)
        arrive(bz[t - 1][1], rows_of(down, y, HOP, HOP) if t == 1 else rows_of(down, y), B)
        second = parcel("bz1", full_bz, rows_of(down, y), B, 1, place + 1, z_down)
        bz[t] = (first, second)

    def bz_end():
        both(bz[3])
        part[rows_of(z, y), B] += bz[3][0].value() + bz[3][1].value()

    def az_start(a):
        d, lanes, slot = ring(z, 4, 8), lanes_of(a), 2 * a
        az[a, 0] = (
            parcel("az0", half_az, rows_in(d, 0, LANES), lanes, slot, slot, z_up),
            parcel("az0", half_az, rows_in(d, LANES, LANES), lanes, slot + 1, slot + 1, z_down),
        )

    def az_pass(a, t):
        up, down, lanes = ring(z, 4 - t, 8), ring(z, t - 4, 8), lanes_of(a)
        slot, place = 2 * a, 6 * a + 2 * (t - 1)
        arrive(az[a, t - 1][0], rows_in(up, 0, LANES) if t == 1 else rows_in(up), lanes)
        first = parcel("az1", full_az, rows_in(up), lanes, slot, place, z_up)
        arrive(az[a, t - 1][1], rows_in(down, LANES, LANES) if t == 1 else rows_in(down), lanes)
        second = parcel("az1", full_az, rows_in(down), lanes, slot + 1, place + 1, z_down)
        az[a, t] = (first, second)

    def az_end(a):
        both(az[a, 3])
        part[rows_in(z), lanes_of(a)] += az[a, 3][0].value() + az[a, 3][1].value()

    def ay_start():
        p = ring(y, 2, 4)
        ay[0] = (
            parcel("ay0", half_ay, rows_of(z, p, 0, HOP), A, 0, 0, y_up),
            parcel("ay0", half_ay, rows_of(z, p, HOP, HOP), A, 1, 1, y_down),
        )

    def ay_pass():
        up, down = ring(y, 1, 4), ring(y, 3, 4)
        arrive(ay[0][0], rows_of(z, up, 0, HOP), A)
        first = parcel("ay1", full_ay, rows_of(z, up), A, 0, 0, y_up)
        arrive(ay[0][1], rows_of(z, down, HOP, HOP), A)
        second = parcel("ay1", full_ay, rows_of(z, down), A, 1, 1, y_down)
        ay[1] = (first, second)

    def ay_end():
        both(ay[1])
        part[rows_of(z, y), A] += ay[1][0].value() + ay[1][1].value()

    with jax.named_scope("multiply_near"):
        multiply(own)
        y_start(0)
        twin_own.wait_recv()
        multiply(order[1])
        y_start(1)
    with jax.named_scope("gather_rest"):
        right_high.wait_recv()
        twin_left_high = share(block_of(x, 3, c), high_rows, twin)
        left_low.wait_recv()
        twin_right_low = share(block_of(x, 1, c), low_rows, twin)
        y_pass(0)
        onward_low.wait_recv()
        twin_low = share(block_of(x, 2, c), low_rows, twin)
        onward_high.wait_recv()
        twin_high = share(block_of(x, 2, c), high_rows, twin)
        for copy in (twin_left_low, twin_left_high, twin_right_low, twin_right_high):
            copy.wait_recv()
        twin_low.wait_recv()
        twin_high.wait_recv()
    y_pass(1)
    multiply(order[2])
    az_start(0)
    y_start(2)
    az_start(1)
    multiply(order[3])
    az_start(2)
    y_start(3)
    multiply(order[4])
    y_start(4)
    multiply(order[5])
    az_pass(0, 1)
    az_pass(1, 1)
    y_pass(2)
    multiply(order[6])
    az_pass(2, 1)
    y_start(6)
    y_pass(3)
    y_end(0)
    y_pass(4)
    y_end(1)
    y_start(5)
    multiply(order[7])
    y_start(7)
    az_pass(0, 2)
    y_end(2)
    bz_start()
    az_pass(1, 2)
    y_pass(6)
    az_pass(2, 2)
    y_end(3)
    az_pass(0, 3)
    y_end(4)
    bz_pass(1)
    y_pass(5)
    az_pass(1, 3)
    y_pass(7)
    az_pass(2, 3)
    y_end(6)
    az_end(0)
    y_end(5)
    bz_pass(2)
    az_end(1)
    y_end(7)
    az_end(2)
    ay_start()
    bz_pass(3)
    ay_pass()
    bz_end()
    ay_end()

    gene_scale, spot_scale = 1.0 / (SLIDES * GENES), 1.0 / SPOTS
    with jax.named_scope("local_sums"):
        pv, tv = part[rows_of(z, y), :], truth[...]
        pred_out[...] = pv
        cross, square, tsquare = pv * tv, pv * pv, tv * tv
        spot_mine[0:1, :] = jnp.sum(cross, axis=0, keepdims=True)
        spot_mine[1:2, :] = jnp.sum(square, axis=0, keepdims=True)
        near = spread_y(spot_mine, spot_near)
        lane = lax.broadcasted_iota(jnp.int32, (PIECE, LANES), 1)
        row_lane = lax.broadcasted_iota(jnp.int32, (1, LANES), 1)
        packed, extra = jnp.zeros((PIECE, LANES), f32), jnp.zeros((1, LANES), f32)
        for k in range(SLIDES):
            inside = member[k : k + 1, :]
            for q, field in enumerate((cross, square, tsquare)):
                summed = jnp.sum(field * inside, axis=1, keepdims=True)
                packed = packed + jnp.where(lane == q * SLIDES + k, summed, 0.0)
            for q, field in enumerate((density, prior[...])):
                summed = jnp.sum(field * inside, axis=1, keepdims=True)
                extra = extra + jnp.where(row_lane == q * SLIDES + k, summed, 0.0)
        board[...] = jnp.zeros((LANES, LANES), f32)
        board[0:PIECE, :] = packed
        slide_msgs[0] = board[...].T[0:16, :]
        slide_msgs[0, 12:13, :] = extra
        slide = spread_spot(slide_msgs)
    with jax.named_scope("spot_sums_y"):
        near.wait_recv()
        spot_far[0] = spot_mine[...] + spot_near[0] + spot_near[1] + spot_near[2]
        far = spread_z(spot_far)
    with jax.named_scope("slide_sums"):
        slide.wait_recv()
        slide_total = slide_msgs[0]
        for d in range(1, 8):
            slide_total = slide_total + slide_msgs[d]
        s_inner, s_square, s_truth = slide_total[0:4], slide_total[4:8], slide_total[8:12]
        s_left, s_right = lax.rsqrt(s_square + epsilon), lax.rsqrt(s_truth + epsilon)
        own_genes = lax.broadcasted_iota(jnp.int32, (SLIDES, LANES), 1) < PIECE
        gene_sum = jnp.sum(jnp.where(own_genes, s_inner * s_left * s_right, 0.0), keepdims=True)
        board[...] = jnp.zeros((LANES, LANES), f32)
        board[0:4, :] = s_inner * s_left * s_left * s_left * s_right
        board[4:8, :] = s_left * s_right
        columns = board[...].T[0:PIECE, :]
        cube_of, flat_of = jnp.zeros((PIECE, COLS), f32), jnp.zeros((PIECE, COLS), f32)
        spot_density, spot_prior = jnp.zeros((1, COLS), f32), jnp.zeros((1, COLS), f32)
        for k in range(SLIDES):
            inside = member[k : k + 1, :]
            cube_of = cube_of + columns[:, k : k + 1] * inside
            flat_of = flat_of + columns[:, 4 + k : 5 + k] * inside
            spot_density = spot_density + slide_total[12:13, k : k + 1] * inside
            spot_prior = spot_prior + slide_total[12:13, 4 + k : 5 + k] * inside
        target_share = prior[...] / spot_prior
        logs = jnp.log(target_share) - jnp.log(density / spot_density)
        density_part = jnp.sum(target_share * logs, keepdims=True) / SLIDES
        grad_density = (1.0 / spot_density - target_share / density) / SLIDES
        gene_part = gene_scale * (cube_of * pv - flat_of * tv)
    with jax.named_scope("spot_sums_z"):
        far.wait_recv()
        spot_total = spot_far[0]
        for d in range(1, 8):
            spot_total = spot_total + spot_far[d]
        p_inner, p_square = spot_total[0:1, :], spot_total[1:2, :]
        p_left, p_right = lax.rsqrt(p_square + epsilon), lax.rsqrt(truth_square + epsilon)
        spot_sum = jnp.sum(p_inner * p_left * p_right, keepdims=True)
        spot_cube = p_inner * p_left * p_left * p_left * p_right
        grad = gene_part + spot_scale * (spot_cube * pv - (p_left * p_right) * tv)
        grads[z, piece(y), :] = grad.astype(bf16)
    with jax.named_scope("sends_done"):
        for sent in parcels.values():
            sent.wait_send()
        wires.close()

    A, B = pl.ds(0, CLOSE), pl.ds(CLOSE, COLS - CLOSE)
    blocks = [ring(z, d, 8) for d in REACH]

    def put(block, rows, lanes, device):
        view = grads.at[block, rows, lanes]
        return wires.send(view, view, device)

    def y_share(block, lanes):
        return put(block, piece(y), lanes, y_up), put(block, piece(y), lanes, y_down)

    def y_straight(block, lanes):
        view = grads.at[block, piece(y), lanes]
        others = [(view, away("y", d)) for d in (1, 3, 2)]
        return wires.spread(view, others, grads.at[block, pl.ds(0, 3 * PIECE), lanes])

    def y_onward(block, lanes, shared):
        shared[0].wait_recv()
        up = put(block, piece(ring(y, 3, 4), 0, HOP), lanes, y_up)
        shared[1].wait_recv()
        down = put(block, piece(ring(y, 1, 4), HOP, HOP), lanes, y_down)
        return up, down

    def z_share(step, rows, lanes):
        above, below = ring(z, 1 - step, 8), ring(z, step - 1, 8)
        return put(above, rows[0], lanes, z_up), put(below, rows[1], lanes, z_down)

    own_rows, all_rows = (piece(y), piece(y)), (pl.ds(0, OWN), pl.ds(0, OWN))
    own_halves = (piece(y, 0, HOP), piece(y, HOP, HOP))
    all_halves = (pl.ds(0, LANES), pl.ds(LANES, LANES))
    base = wires.take(57)

    def each(turn, body):
        if turn in (0, 4):
            body(2 * turn - (turn > 0), ring(z, turn, 8))
        else:

            @pl.loop(0, 2)
            def _(i):
                body(2 * turn - 1 + i, ring(z, turn * (1 - 2 * i), 8))

    keep, give = c * HALF, (1 - c) * HALF

    def some_rows(first, size=HALF):
        return pl.ds(pl.multiple_of(first, 16), size)

    def twin_link(n):
        return wires.link(xp.at[n, some_rows(give)], xc.at[n], twin, base + n)

    def out_slot(k, odd, i):
        return 2 * (k + 6 * odd) + i

    def in_slot(k, odd, i, core):
        if k < 2:
            return 16 + 2 * (k + 2 * odd) + i
        return 2 * (k - 2 + 4 * core) + i

    def eighth_links(k, odd, i):
        here, there = out_slot(k, odd, i), in_slot(k, odd, i, c)
        device = right if k in (0, 2, 3) else left
        if k > 1:
            device = {"x": device["x"], "c": odd}
        return (
            wires.link(
                scale_out.at[here], scale_in.at[there], device, base + 8 + here, base + 8 + there
            ),
            wires.link(
                coded_out.at[here], coded_in.at[there], device, base + 32 + here, base + 32 + there
            ),
        )

    def eighth(i):
        return some_rows(i * EIGHTH, EIGHTH)

    def kept_eighth(high, i):
        return some_rows(keep + (2 * high + i) * EIGHTH, EIGHTH)

    def eighth_send(n, odd, high, k, i):
        summed = xp[n, kept_eighth(high, i), :]
        top = jnp.maximum(jnp.max(jnp.abs(summed), axis=0, keepdims=True), 1e-30)
        here = out_slot(k, odd, i)
        scale_out[here] = top * (1.0 / TOP)
        coded_out[here] = jnp.round(summed * (TOP / top)).astype(jnp.int16)
        for link in eighth_links(k, odd, i):
            link.start()

    def eighth_value(k, odd, i, core):
        there = in_slot(k, odd, i, core)
        wires.link(scale_in.at[there], scale_in.at[there], twin, base + 8 + there).wait_recv()
        wires.link(coded_in.at[there], coded_in.at[there], twin, base + 32 + there).wait_recv()
        return coded_in[there].astype(f32) * scale_in[there]

    def distance(block):
        return ring(block // 2 - x, 0, 4)

    def block_first(n, block):
        xp[n] = lax.dot_general(
            weights[...],
            grads[block],
            (((1,), (1,)), ((), ())),
            preferred_element_type=f32,
        )
        twin_link(n).start()

    def cell_part(n, block):
        product = jnp.dot(profiles[block], grads[block], preferred_element_type=f32)
        if isinstance(n, int) and n == 0:
            part[0:ROWS, :] = product
        else:
            part[0:ROWS, :] += product

    at_own, at_twin = jnp.int32(0), jnp.int32(0)
    for n in range(8):
        at_own = at_own + n * jnp.where(blocks[n] == own, 1, 0)
        at_twin = at_twin + n * jnp.where(blocks[n] == block_of(x, 0, 1 - c), 1, 0)
    ending = wires.link(xp.at[at_twin, some_rows(keep)], ended, twin, base + 56)

    def block_second(n, block):
        odd = lax.rem(block, 2)
        twin_link(n).wait_recv()

        @pl.loop(0, 4)
        def _(i):
            xp[n, some_rows(keep + i * EIGHTH, EIGHTH), :] += xc[n, eighth(i), :]

        @pl.when(distance(block) == 2)
        def _():
            @pl.loop(0, 2)
            def _(i):
                eighth_send(n, odd, 0, 0, i)
                eighth_send(n, odd, 1, 1, i)

        @pl.when(distance(block) == 1)
        def _():
            @pl.loop(0, 2)
            def _(i):
                eighth_send(n, odd, 1, 2, i)

        @pl.when(distance(block) == 3)
        def _():
            @pl.loop(0, 2)
            def _(i):
                eighth_send(n, odd, 0, 4, i)

        @pl.when(block == block_of(x, 0, 1 - c))
        def _():
            ending.start()

    def add_and_send(n, odd, high, k, onward):
        @pl.loop(0, 2)
        def _(i):
            xp[n, kept_eighth(high, i), :] += eighth_value(k, odd, i, c)
            eighth_send(n, odd, high, onward, i)

    def block_third(n, block):
        odd = lax.rem(block, 2)

        @pl.when(distance(block) == 1)
        def _():
            add_and_send(n, odd, 0, 0, 3)

        @pl.when(distance(block) == 3)
        def _():
            add_and_send(n, odd, 1, 1, 5)

    def one(body, n):
        body(n, blocks[n])

    bz, az, shared_b, onward_b = {1: z_share(1, own_rows, B)}, {}, {}, {}
    straight = y_straight(z, A)
    shared_b[0] = y_share(z, B)
    rounds = {0: (0,), 1: (1, 2), 2: (3, 4), 3: (5, 6), 4: (7,)}

    def turn_b(turn):
        both(bz[turn])
        if turn < 4:
            bz[turn + 1] = z_share(turn + 1, own_rows if turn < 3 else own_halves, B)
        if turn == 4:
            shared_b[7] = y_straight(blocks[7], B)
        else:
            for n in rounds[turn]:
                shared_b[n] = y_share(blocks[n], B)

    def turn_a(turn):
        if turn:
            both(az[turn])
        else:
            straight.wait_recv()
        if turn < 4:
            az[turn + 1] = z_share(turn + 1, all_rows if turn < 3 else all_halves, A)

    def turn_on(turn):
        for n in rounds[turn]:
            onward_b[n] = y_onward(blocks[n], B, shared_b[n])

    def turn_first(turn):
        if turn == 4:
            shared_b[7].wait_recv()
        else:
            for n in rounds[turn]:
                both(onward_b[n])
        each(turn, block_first)

    turn_b(1)
    turn_a(0)
    turn_b(2)
    turn_on(0)
    turn_a(1)
    turn_on(1)
    turn_on(2)
    turn_b(3)
    turn_first(0)
    turn_a(2)
    turn_first(2)
    turn_on(3)
    turn_first(1)
    one(block_second, 0)
    one(block_second, 3)
    one(block_second, 4)
    turn_b(4)
    turn_a(3)
    turn_first(3)
    each(0, cell_part)
    turn_a(4)
    one(block_second, 1)
    one(block_second, 2)
    one(block_second, 5)
    each(1, cell_part)
    one(block_second, 6)
    turn_first(4)
    each(2, cell_part)
    each(3, cell_part)
    one(block_second, 7)
    each(4, cell_part)

    with jax.named_scope("column_sums"):
        column_mine[...] = jnp.zeros((2, COLS), f32)
        column_mine[1:2, :] = jnp.where(column == 0, gene_sum, 0.0)
        for b in range(BLOCKS):
            rows = lanes_of(b)
            across = jnp.zeros((LANES, LANES), f32)
            for j in range(COLS // LANES):
                lanes, cut = lanes_of(j), slice(j * LANES, (j + 1) * LANES)
                whole = (grown[rows, lanes] * scale[:, cut]) * (
                    part[rows, lanes] + grad_density[:, cut]
                )
                part[rows, lanes] = whole
                across = across + whole
                column_mine[0:1, lanes] += jnp.sum(whole * gate[rows, :], axis=0, keepdims=True)
            filter_msgs[0, b : b + 1, :] = jnp.sum(across.T, axis=0, keepdims=True)
        filter_msgs[0, 11:12, :] = jnp.where(
            row_lane == 0, spot_sum, jnp.where(row_lane == 1, density_part, 0.0)
        )
        filter_msgs[0, 12:16, :] = jnp.zeros((4, LANES), f32)
        near = spread_y(column_mine, column_near)
        sums = spread_spot(filter_msgs)
    for n in (0, 1, 2, 4):
        one(block_third, n)
    with jax.named_scope("column_sums_y"):
        near.wait_recv()
        column_far[0] = column_mine[...] + column_near[0] + column_near[1] + column_near[2]
        far = spread_z(column_far)
    for n in (3, 7, 5, 6):
        one(block_third, n)
    with jax.named_scope("column_sums_z"):
        far.wait_recv()
        column_total = column_far[0]
        for d in range(1, 8):
            column_total = column_total + column_far[d]
    with jax.named_scope("logits_gradient"):
        dot_scale = column_total[0:1, :] * scale
        for b in range(BLOCKS):
            rows = lanes_of(b)
            for j in range(COLS // LANES):
                lanes, cut = lanes_of(j), slice(j * LANES, (j + 1) * LANES)
                part[rows, lanes] = (
                    gate[rows, :] * part[rows, lanes] - grown[rows, lanes] * dot_scale[:, cut]
                )
    with jax.named_scope("filter_gradient"):
        sums.wait_recv()
        filter_total = filter_msgs[0]
        for d in range(1, 8):
            filter_total = filter_total + filter_msgs[d]
        gap = kept - target[0].astype(f32)
        root = jnp.sqrt(gap * gap + 1.0)
        on = filter_total[0:BLOCKS, :] + gap / root / CELLS + (1.0 - 2.0 * gates) / CELLS
        filter_out[...] = on * gates * (1.0 - gates)
        values = (
            -column_total[1:2, 0:1] * gene_scale,
            -filter_total[11:12, 0:1] * spot_scale,
            filter_total[11:12, 1:2],
            root / CELLS,
            spread / CELLS,
        )
        losses = jnp.zeros((1, LANES), f32)
        for k, value in enumerate(values):
            losses = losses + jnp.where(row_lane == k, value, 0.0)
        losses_out[...] = losses

    with jax.named_scope("last_sum"):
        ending.wait_recv()
        for core_rows, core in ((keep, c), (give, 1 - c)):
            for high, ks in ((0, (3, 4)), (1, (2, 5))):

                @pl.loop(0, 2)
                def _(i, core_rows=core_rows, core=core, high=high, ks=ks):
                    rows = some_rows(core_rows + (2 * high + i) * EIGHTH, EIGHTH)
                    if core is c:
                        start = xp[at_own, rows, :]
                    else:
                        start = ended[some_rows((2 * high + i) * EIGHTH, EIGHTH), :]
                    total = start + eighth_value(ks[0], 0, i, core)
                    profile_out[rows, :] = total + eighth_value(ks[1], 0, i, core)

    with jax.named_scope("sends_done"):
        for n in range(8):
            twin_link(n).wait_send()
        for odd in range(2):
            for k in range(6):
                for i in range(2):
                    for link in eighth_links(k, odd, i):
                        link.wait_send()
        ending.wait_send()
    with jax.named_scope("wires_done"):
        wires.close()


def training_step(sizes, target, logits, filters, expression, spatial, prior):
    f32, bf16 = jnp.float32, jnp.bfloat16
    anywhere = pl.BlockSpec(memory_space=pl.ANY)
    inside = pl.BlockSpec(memory_space=pltpu.VMEM)
    scalars = pl.BlockSpec(memory_space=pltpu.SMEM)
    near = COLS - SPLIT
    return pl.pallas_call(
        step_kernel,
        out_shape=(
            pltpu.VMEM((PIECE, COLS), f32),
            pltpu.VMEM((GENES, COLS), f32),
            pltpu.VMEM((ROWS, OWN), f32),
            pltpu.VMEM((BLOCKS, LANES), f32),
            pltpu.VMEM((1, LANES), f32),
        ),
        in_specs=[scalars, scalars, anywhere, anywhere, anywhere, anywhere, anywhere],
        out_specs=(inside, inside, inside, inside, inside),
        scratch_shapes=[
            pltpu.VMEM((BLOCKS, LANES), f32),
            pltpu.VMEM((1, COLS), f32),
            pltpu.VMEM((ROWS, COLS), f32),
            pltpu.VMEM((ROWS, COLS), bf16),
            pltpu.VMEM((8, ROWS, OWN), bf16),
            pltpu.VMEM((COLS, LANES), f32),
            pltpu.VMEM((LANES, COLS), f32),
            pltpu.VMEM((ROWS, LANES), f32),
            pltpu.VMEM((SLIDES, COLS), f32),
            pltpu.VMEM((LANES, LANES), f32),
            pltpu.VMEM((4, COLS), f32),
            pltpu.VMEM((3, 4, COLS), f32),
            pltpu.VMEM((8, 4, COLS), f32),
            parcel_buffers(HOP, near, 8, 16),
            parcel_buffers(PIECE, near, 8, 16),
            parcel_buffers(HOP, near, 2, 2),
            parcel_buffers(PIECE, near, 2, 6),
            parcel_buffers(LANES, LANES, 2 * GROUPS, 2 * GROUPS),
            parcel_buffers(OWN, LANES, 2 * GROUPS, 6 * GROUPS),
            parcel_buffers(HOP, SPLIT, 2, 2),
            parcel_buffers(PIECE, SPLIT, 2, 2),
            pltpu.VMEM((8, OWN, COLS), bf16),
            pltpu.VMEM((8, ROWS, OWN), f32),
            pltpu.VMEM((8, HALF, OWN), f32),
            pltpu.VMEM((HALF, OWN), f32),
            pltpu.VMEM((24, EIGHTH, OWN), jnp.int16),
            pltpu.VMEM((24, EIGHTH, OWN), jnp.int16),
            pltpu.VMEM((24, 1, OWN), f32),
            pltpu.VMEM((24, 1, OWN), f32),
            pltpu.VMEM((8, 16, LANES), f32),
            pltpu.VMEM((2, COLS), f32),
            pltpu.VMEM((3, 2, COLS), f32),
            pltpu.VMEM((8, 2, COLS), f32),
            pltpu.VMEM((2, COLS), f32),
            pltpu.VMEM((3, 2, COLS), f32),
            pltpu.VMEM((8, 2, COLS), f32),
            pltpu.VMEM((8, 16, LANES), f32),
            pltpu.SemaphoreType.DMA((COPIES + SPREADS,)),
            pltpu.SemaphoreType.DMA((COPIES + SPREADS,)),
            pltpu.SemaphoreType.DMA((BLOCKS + 4,)),
        ],
        compiler_params=pltpu.CompilerParams(
            collective_id=0, has_side_effects=True, vmem_limit_bytes=LIMIT
        ),
        name="training_step",
    )(sizes, target, logits, filters, expression, spatial, prior)


def finish_kernel(
    losses,
    pred,
    part,
    profile,
    filter_rows,
    losses_out,
    pred_out,
    logits_out,
    profile_out,
    filter_out,
    sems,
):
    pieces = [(part.at[0:ROWS], logits_out), (profile, profile_out), (pred, pred_out)]
    pieces.append((filter_rows, filter_out))
    copies = [pltpu.make_async_copy(a, b, sems.at[i]) for i, (a, b) in enumerate(pieces)]
    for copy in copies:
        copy.start()
    row_lane = lax.broadcasted_iota(jnp.int32, (1, LANES), 1)
    for k in range(5):
        losses_out[k] = jnp.sum(jnp.where(row_lane == k, losses[...], 0.0))
    for copy in copies:
        copy.wait()


def finish(losses, pred, part, profile, filter_rows):
    f32 = jnp.float32
    anywhere = pl.BlockSpec(memory_space=pl.ANY)
    inside = pl.BlockSpec(memory_space=pltpu.VMEM)
    scalars = pl.BlockSpec(memory_space=pltpu.SMEM)
    return pl.pallas_call(
        finish_kernel,
        out_shape=(
            jax.ShapeDtypeStruct((5,), f32),
            jax.ShapeDtypeStruct((PIECE, COLS), f32),
            jax.ShapeDtypeStruct((ROWS, COLS), f32),
            jax.ShapeDtypeStruct((ROWS, OWN), f32),
            jax.ShapeDtypeStruct((BLOCKS, LANES), f32),
        ),
        in_specs=[inside] * 5,
        out_specs=(scalars, anywhere, anywhere, anywhere, anywhere),
        scratch_shapes=[pltpu.SemaphoreType.DMA((4,))],
        compiler_params=pltpu.CompilerParams(vmem_limit_bytes=1024 * 1024),
        name="finish",
    )(losses, pred, part, profile, filter_rows)


def on_device(logits, filter_logits, expression, spatial, prior, slide_sizes, target):
    pred, part, profile, filter_rows, losses = training_step(
        slide_sizes,
        target,
        logits,
        filter_logits.reshape(BLOCKS, LANES),
        expression,
        spatial,
        prior.reshape(1, COLS),
    )
    losses, pred, grad_logits, grad_expression, grad_filter = finish(
        losses, pred, part, profile, filter_rows
    )
    return (losses, pred.T, grad_logits, grad_filter.reshape(-1), grad_expression)


def solution(mesh):
    split = Mesh(mesh.devices.reshape(8, 4, 4, 2), ("z", "y", "x", "c"))
    return jax.shard_map(
        on_device,
        mesh=split,
        in_specs=(P(CELL, SPOT), P(CELL), P(CELL, SPOT), P(SPOT, None), P(SPOT), P(), P()),
        out_specs=(P(), P(SPOT, CELL), P(CELL, SPOT), P(CELL), P(CELL, SPOT)),
        check_vma=False,
    )
```

```python
import jax
import jax.numpy as jnp
from jax import lax
from jax.experimental import pallas as pl
from jax.experimental.pallas import tpu as pltpu
from jax.sharding import Mesh
from jax.sharding import PartitionSpec as P

CELL = ("z", "y")
SPOT = ("x", "c")
SIZE = {"z": 8, "y": 4, "x": 4, "c": 2}
MESH = pl.DeviceIdType.MESH
ROWS = 1408
COLS = 1024
OWN = 256
PIECE = 64
LANES = 128
BLOCKS = ROWS // LANES
SLIDES = 4
GENES = PIECE * 32
CELLS = ROWS * 32
SPOTS = COLS * 8
HALF = ROWS // 2
HOP = PIECE // 2
EIGHTH = HALF // 4
TOP = 32767.0
SPLIT = 384
GROUPS = SPLIT // LANES
CLOSE = 384
REACH = (0, 1, 7, 2, 6, 3, 5, 4)
COPIES, SPREADS = 149, 11
LIMIT = 52 * 1024 * 1024

epsilon = 1e-06


def ring(position, step, size):
    return lax.rem(position + step + size, size)


def away(axis, step):
    return {axis: ring(lax.axis_index(axis), step, SIZE[axis])}


def spot_peer(step):
    place = lax.rem(lax.axis_index("x") * 2 + lax.axis_index("c") + step, 8)
    return {"x": place // 2, "c": lax.rem(place, 2)}


def block_of(x, step, c):
    return ring(x, step, 4) * 2 + c


def lanes_of(j, size=LANES):
    if isinstance(j, int):
        return pl.ds(j * size, size)
    return pl.ds(pl.multiple_of(j * size, size), size)


def piece(position, extra=0, size=PIECE):
    return pl.ds(pl.multiple_of(position * PIECE, PIECE) + extra, size)


def rows_in(block, extra=0, size=OWN):
    return pl.ds(pl.multiple_of(block * OWN, OWN) + extra, size)


def rows_of(block, position, extra=0, size=PIECE):
    return pl.ds(pl.multiple_of(block * OWN + position * PIECE, PIECE) + extra, size)


class Wires:
    def __init__(self, send_sems, recv_sems):
        self.send_sems, self.recv_sems, self.sent = send_sems, recv_sems, []
        self.used, self.spreads = 0, 0

    def take(self, count=1):
        at = self.used
        self.used += count
        return at

    def link(self, source, target, device, at, at_there=None):
        return pltpu.make_async_remote_copy(
            src_ref=source,
            dst_ref=target,
            send_sem=self.send_sems.at[at],
            recv_sem=self.recv_sems.at[at if at_there is None else at_there],
            device_id=device,
            device_id_type=MESH,
        )

    def send(self, source, target, device):
        copy = self.link(source, target, device, self.take())
        copy.start()
        self.sent.append(copy)
        return copy

    def spread(self, source, targets, slots):
        at = COPIES + self.spreads
        self.spreads += 1
        for target, device in targets:
            self.link(source, target, device, at).start()
        whole = self.link(slots, slots, targets[0][1], at)
        self.sent.append(whole)
        return whole

    def close(self):
        assert self.used <= COPIES and self.spreads <= SPREADS
        for copy in self.sent:
            copy.wait_send()
        self.used, self.sent = 0, []


class Parcel:
    def __init__(self, wires, buffers, source, slot, place, device):
        out, out_scale, into, into_scale = buffers
        value = source[...]
        low = jnp.min(value, axis=0, keepdims=True)
        high = jnp.max(value, axis=0, keepdims=True)
        middle = 0.5 * (low + high)
        reach = jnp.maximum(jnp.maximum(high - middle, middle - low), 1e-30)
        out_scale[slot, 0:1, :] = middle
        out_scale[slot, 1:2, :] = reach * (1.0 / TOP)
        out[slot] = jnp.round((value - middle) * (TOP / reach)).astype(jnp.int16)
        self.rows, self.scale = into.at[place], into_scale.at[place]
        self.copies = (
            wires.link(out.at[slot], self.rows, device, wires.take()),
            wires.link(out_scale.at[slot], self.scale, device, wires.take()),
        )
        for copy in self.copies:
            copy.start()

    def wait_recv(self):
        for copy in self.copies:
            copy.wait_recv()

    def wait_send(self):
        for copy in self.copies:
            copy.wait_send()

    def value(self):
        return self.scale[0:1, :] + self.rows[...].astype(jnp.float32) * self.scale[1:2, :]


def parcel_buffers(rows, columns, out, into):
    return (
        pltpu.VMEM((out, rows, columns), jnp.int16),
        pltpu.VMEM((out, 2, columns), jnp.float32),
        pltpu.VMEM((into, rows, columns), jnp.int16),
        pltpu.VMEM((into, 2, columns), jnp.float32),
    )


def both(copies):
    copies[0].wait_recv()
    copies[1].wait_recv()


def step_kernel(
    sizes,
    target,
    logits,
    filters_in,
    expression,
    spatial,
    prior_in,
    pred_out,
    part,
    profile_out,
    filter_out,
    losses_out,
    filters,
    prior,
    grown,
    weights,
    profiles,
    slab,
    truth_all,
    gate,
    member,
    board,
    mine,
    near_stats,
    far_stats,
    half_y,
    full_y,
    half_bz,
    full_bz,
    half_az,
    full_az,
    half_ay,
    full_ay,
    grads,
    xp,
    xc,
    ended,
    coded_out,
    coded_in,
    scale_out,
    scale_in,
    slide_msgs,
    spot_mine,
    spot_near,
    spot_far,
    column_mine,
    column_near,
    column_far,
    filter_msgs,
    send_sems,
    recv_sems,
    local_sems,
):
    f32, bf16 = jnp.float32, jnp.bfloat16
    z, y = lax.axis_index("z"), lax.axis_index("y")
    x, c = lax.axis_index("x"), lax.axis_index("c")
    wires = Wires(send_sems, recv_sems)
    own = x * 2 + c
    cell = z * 4 + y
    right, left, twin = away("x", 1), away("x", 3), away("c", 1)
    y_up, y_down, z_up, z_down = away("y", 1), away("y", 3), away("z", 1), away("z", 7)

    def spread_y(source, slots):
        return wires.spread(source, [(slots.at[d - 1], away("y", d)) for d in (1, 2, 3)], slots)

    def spread_z(slots):
        others = [(slots.at[d], away("z", d)) for d in range(1, 8)]
        return wires.spread(slots.at[0], others, slots.at[pl.ds(1, 7)])

    def spread_spot(slots):
        others = [(slots.at[d], spot_peer(d)) for d in range(1, 8)]
        return wires.spread(slots.at[0], others, slots.at[pl.ds(1, 7)])

    barrier = pltpu.get_barrier_semaphore()
    targets = (
        [away("y", d) for d in (1, 2, 3)]
        + [away("z", d) for d in range(1, 8)]
        + [spot_peer(d) for d in range(1, 8)]
    )
    for device in targets:
        pl.semaphore_signal(barrier, inc=1, device_id=device, device_id_type=MESH)
    loads = []
    for b in range(BLOCKS):
        rows = lanes_of(b)
        loads.append(
            pltpu.make_async_copy(logits.at[rows, :], grown.at[rows, :], local_sems.at[b])
        )
    load_own = pltpu.make_async_copy(expression, profiles.at[own], local_sems.at[BLOCKS])
    aligned = pl.multiple_of((cell // 2) * LANES, LANES)
    load_truth = pltpu.make_async_copy(
        spatial.at[:, pl.ds(aligned, LANES)], slab, local_sems.at[BLOCKS + 1]
    )
    load_filters = pltpu.make_async_copy(filters_in, filters, local_sems.at[BLOCKS + 2])
    load_prior = pltpu.make_async_copy(prior_in, prior, local_sems.at[BLOCKS + 3])
    load_filters.start()
    load_own.start()
    for load in loads:
        load.start()
    load_truth.start()
    load_prior.start()
    load_own.wait()
    with jax.named_scope("greeting"):
        pl.semaphore_wait(barrier, len(targets))
    low_rows, high_rows = pl.ds(0, HALF), pl.ds(HALF, HALF)

    def share(block, rows, device):
        return wires.send(profiles.at[block, rows], profiles.at[block, rows], device)

    def share_whole(block, device):
        return wires.send(profiles.at[block], profiles.at[block], device)

    right_low = share(own, low_rows, right)
    left_high = share(own, high_rows, left)
    twin_own = share_whole(own, twin)
    load_filters.wait()
    gates = jax.nn.sigmoid(filters[...])
    for b in range(BLOCKS):
        gate[lanes_of(b), :] = jnp.broadcast_to(gates[b : b + 1, :], (LANES, LANES)).T
    kept = jnp.sum(gates, keepdims=True)
    spread = jnp.sum(gates - gates * gates, keepdims=True)
    column = lax.broadcasted_iota(jnp.int32, (1, COLS), 1)
    mine[3:4, :] = jnp.where(column == 0, kept, jnp.where(column == 1, spread, 0.0))
    mine[0:3, :] = jnp.zeros((3, COLS), f32)
    spot = column + own * COLS
    begin = jnp.int32(0)
    for k in range(SLIDES):
        end = begin + sizes[k]
        within = jnp.logical_and(spot >= begin, spot < end)
        member[k : k + 1, :] = jnp.where(within, 1.0, 0.0)
        begin = end

    with jax.named_scope("exponentials"):
        for b in range(BLOCKS):
            loads[b].wait()

            @pl.loop(0, COLS // LANES)
            def _(j, b=b):
                rows, lanes = lanes_of(b), lanes_of(j)
                e = jnp.exp(grown[rows, lanes])
                grown[rows, lanes] = e
                mine[0:1, lanes] += jnp.sum(e, axis=0, keepdims=True)
                mine[1:2, lanes] += jnp.sum(e * gate[rows, :], axis=0, keepdims=True)

    with jax.named_scope("truth"):
        load_truth.wait()
        load_prior.wait()
        truth_all[...] = slab[...].T
        truth = truth_all.at[piece(lax.rem(cell, 2)), :]
        held = truth[...]
        mine[2:3, :] = jnp.sum(held * held, axis=0, keepdims=True)

    with jax.named_scope("totals_y"):
        near = spread_y(mine, near_stats)
        right_high = share(own, high_rows, right)
        left_low = share(own, low_rows, left)
        near.wait_recv()
        far_stats[0] = mine[...] + near_stats[0] + near_stats[1] + near_stats[2]
        far = spread_z(far_stats)
    with jax.named_scope("pass_halves"):
        right_low.wait_recv()
        onward_low = share(block_of(x, 3, c), low_rows, right)
        twin_left_low = share(block_of(x, 3, c), low_rows, twin)
        left_high.wait_recv()
        onward_high = share(block_of(x, 1, c), high_rows, left)
        twin_right_high = share(block_of(x, 1, c), high_rows, twin)
    with jax.named_scope("totals_z"):
        far.wait_recv()
        stats = far_stats[0]
        for d in range(1, 8):
            stats = stats + far_stats[d]
    totals, filtered, truth_square = stats[0:1, :], stats[1:2, :], stats[2:3, :]
    kept, spread = stats[3:4, 0:1], stats[3:4, 1:2]
    density = filtered / totals
    scale = 1.0 / totals

    with jax.named_scope("weights"):

        @pl.loop(0, BLOCKS)
        def _(b):
            rows = lanes_of(b)
            for j in range(COLS // LANES):
                cut = slice(j * LANES, (j + 1) * LANES)
                weights[rows, lanes_of(j)] = (
                    grown[rows, lanes_of(j)] * scale[:, cut] * gate[rows, :]
                ).astype(bf16)

    def multiply(block):
        part[rows_in(block), :] = lax.dot_general(
            profiles[block], weights[...], (((0,), (0,)), ((), ())), preferred_element_type=f32
        )

    sought = [ring(z, d, 8) for d in (4, 3, 5, 2, 6, 1, 7, 0)]
    order = [own, block_of(x, 0, 1 - c)] + [jnp.int32(0)] * 6
    at = jnp.int32(2)
    for block in sought:
        other = jnp.where(block // 2 != x, 1, 0)
        for i in range(2, 8):
            order[i] = order[i] + block * other * jnp.where(at == i, 1, 0)
        at = at + other
    A, B = pl.ds(0, SPLIT), pl.ds(SPLIT, COLS - SPLIT)
    started, passed, parcels = {}, {}, {}

    def parcel(name, buffers, rows, lanes, slot, place, device):
        if (name, slot) in parcels:
            parcels[name, slot].wait_send()
        sent = Parcel(wires, buffers, part.at[rows, lanes], slot, place, device)
        parcels[name, slot] = sent
        return sent

    def arrive(sent, rows, lanes):
        sent.wait_recv()
        part[rows, lanes] += sent.value()

    def y_start(i):
        s, p, slot = order[i], ring(y, 2, 4), 2 * (i % 4)
        started[i] = (
            parcel("y0", half_y, rows_of(s, p, 0, HOP), B, slot, 2 * i, y_up),
            parcel("y0", half_y, rows_of(s, p, HOP, HOP), B, slot + 1, 2 * i + 1, y_down),
        )

    def y_pass(i):
        s, up, down, slot = order[i], ring(y, 1, 4), ring(y, 3, 4), 2 * (i % 4)
        arrive(started[i][0], rows_of(s, up, 0, HOP), B)
        first = parcel("y1", full_y, rows_of(s, up), B, slot, 2 * i, y_up)
        arrive(started[i][1], rows_of(s, down, HOP, HOP), B)
        second = parcel("y1", full_y, rows_of(s, down), B, slot + 1, 2 * i + 1, y_down)
        passed[i] = (first, second)

    def y_end(i):
        both(passed[i])
        part[rows_of(order[i], y), B] += passed[i][0].value() + passed[i][1].value()

    bz, az, ay = {}, {}, {}

    def bz_start():
        d = ring(z, 4, 8)
        bz[0] = (
            parcel("bz0", half_bz, rows_of(d, y, 0, HOP), B, 0, 0, z_up),
            parcel("bz0", half_bz, rows_of(d, y, HOP, HOP), B, 1, 1, z_down),
        )

    def bz_pass(t):
        up, down, place = ring(z, 4 - t, 8), ring(z, t - 4, 8), 2 * (t - 1)
        arrive(bz[t - 1][0], rows_of(up, y, 0, HOP) if t == 1 else rows_of(up, y), B)
        first = parcel("bz1", full_bz, rows_of(up, y), B, 0, place, z_up)
        arrive(bz[t - 1][1], rows_of(down, y, HOP, HOP) if t == 1 else rows_of(down, y), B)
        second = parcel("bz1", full_bz, rows_of(down, y), B, 1, place + 1, z_down)
        bz[t] = (first, second)

    def bz_end():
        both(bz[3])
        part[rows_of(z, y), B] += bz[3][0].value() + bz[3][1].value()

    def az_start(a):
        d, lanes, slot = ring(z, 4, 8), lanes_of(a), 2 * a
        az[a, 0] = (
            parcel("az0", half_az, rows_in(d, 0, LANES), lanes, slot, slot, z_up),
            parcel("az0", half_az, rows_in(d, LANES, LANES), lanes, slot + 1, slot + 1, z_down),
        )

    def az_pass(a, t):
        up, down, lanes = ring(z, 4 - t, 8), ring(z, t - 4, 8), lanes_of(a)
        slot, place = 2 * a, 6 * a + 2 * (t - 1)
        arrive(az[a, t - 1][0], rows_in(up, 0, LANES) if t == 1 else rows_in(up), lanes)
        first = parcel("az1", full_az, rows_in(up), lanes, slot, place, z_up)
        arrive(az[a, t - 1][1], rows_in(down, LANES, LANES) if t == 1 else rows_in(down), lanes)
        second = parcel("az1", full_az, rows_in(down), lanes, slot + 1, place + 1, z_down)
        az[a, t] = (first, second)

    def az_end(a):
        both(az[a, 3])
        part[rows_in(z), lanes_of(a)] += az[a, 3][0].value() + az[a, 3][1].value()

    def ay_start():
        p = ring(y, 2, 4)
        ay[0] = (
            parcel("ay0", half_ay, rows_of(z, p, 0, HOP), A, 0, 0, y_up),
            parcel("ay0", half_ay, rows_of(z, p, HOP, HOP), A, 1, 1, y_down),
        )

    def ay_pass():
        up, down = ring(y, 1, 4), ring(y, 3, 4)
        arrive(ay[0][0], rows_of(z, up, 0, HOP), A)
        first = parcel("ay1", full_ay, rows_of(z, up), A, 0, 0, y_up)
        arrive(ay[0][1], rows_of(z, down, HOP, HOP), A)
        second = parcel("ay1", full_ay, rows_of(z, down), A, 1, 1, y_down)
        ay[1] = (first, second)

    def ay_end():
        both(ay[1])
        part[rows_of(z, y), A] += ay[1][0].value() + ay[1][1].value()

    with jax.named_scope("multiply_near"):
        multiply(own)
        y_start(0)
        twin_own.wait_recv()
        multiply(order[1])
        y_start(1)
    with jax.named_scope("gather_rest"):
        right_high.wait_recv()
        twin_left_high = share(block_of(x, 3, c), high_rows, twin)
        left_low.wait_recv()
        twin_right_low = share(block_of(x, 1, c), low_rows, twin)
        y_pass(0)
        onward_low.wait_recv()
        twin_low = share(block_of(x, 2, c), low_rows, twin)
        onward_high.wait_recv()
        twin_high = share(block_of(x, 2, c), high_rows, twin)
        for copy in (twin_left_low, twin_left_high, twin_right_low, twin_right_high):
            copy.wait_recv()
        twin_low.wait_recv()
        twin_high.wait_recv()
    y_pass(1)
    multiply(order[2])
    az_start(0)
    y_start(2)
    az_start(1)
    multiply(order[3])
    az_start(2)
    y_start(3)
    multiply(order[4])
    y_start(4)
    multiply(order[5])
    az_pass(0, 1)
    az_pass(1, 1)
    y_pass(2)
    multiply(order[6])
    az_pass(2, 1)
    y_start(6)
    y_pass(3)
    y_end(0)
    y_pass(4)
    y_end(1)
    y_start(5)
    multiply(order[7])
    y_start(7)
    az_pass(0, 2)
    y_end(2)
    bz_start()
    az_pass(1, 2)
    y_pass(6)
    az_pass(2, 2)
    y_end(3)
    az_pass(0, 3)
    y_end(4)
    bz_pass(1)
    y_pass(5)
    az_pass(1, 3)
    y_pass(7)
    az_pass(2, 3)
    y_end(6)
    az_end(0)
    y_end(5)
    bz_pass(2)
    az_end(1)
    y_end(7)
    az_end(2)
    ay_start()
    bz_pass(3)
    ay_pass()
    bz_end()
    ay_end()

    gene_scale, spot_scale = 1.0 / (SLIDES * GENES), 1.0 / SPOTS
    with jax.named_scope("local_sums"):
        pv, tv = part[rows_of(z, y), :], truth[...]
        pred_out[...] = pv
        cross, square, tsquare = pv * tv, pv * pv, tv * tv
        spot_mine[0:1, :] = jnp.sum(cross, axis=0, keepdims=True)
        spot_mine[1:2, :] = jnp.sum(square, axis=0, keepdims=True)
        near = spread_y(spot_mine, spot_near)
        lane = lax.broadcasted_iota(jnp.int32, (PIECE, LANES), 1)
        row_lane = lax.broadcasted_iota(jnp.int32, (1, LANES), 1)
        packed, extra = jnp.zeros((PIECE, LANES), f32), jnp.zeros((1, LANES), f32)
        for k in range(SLIDES):
            inside = member[k : k + 1, :]
            for q, field in enumerate((cross, square, tsquare)):
                summed = jnp.sum(field * inside, axis=1, keepdims=True)
                packed = packed + jnp.where(lane == q * SLIDES + k, summed, 0.0)
            for q, field in enumerate((density, prior[...])):
                summed = jnp.sum(field * inside, axis=1, keepdims=True)
                extra = extra + jnp.where(row_lane == q * SLIDES + k, summed, 0.0)
        board[...] = jnp.zeros((LANES, LANES), f32)
        board[0:PIECE, :] = packed
        slide_msgs[0] = board[...].T[0:16, :]
        slide_msgs[0, 12:13, :] = extra
        slide = spread_spot(slide_msgs)
    with jax.named_scope("spot_sums_y"):
        near.wait_recv()
        spot_far[0] = spot_mine[...] + spot_near[0] + spot_near[1] + spot_near[2]
        far = spread_z(spot_far)
    with jax.named_scope("slide_sums"):
        slide.wait_recv()
        slide_total = slide_msgs[0]
        for d in range(1, 8):
            slide_total = slide_total + slide_msgs[d]
        s_inner, s_square, s_truth = slide_total[0:4], slide_total[4:8], slide_total[8:12]
        s_left, s_right = lax.rsqrt(s_square + epsilon), lax.rsqrt(s_truth + epsilon)
        own_genes = lax.broadcasted_iota(jnp.int32, (SLIDES, LANES), 1) < PIECE
        gene_sum = jnp.sum(jnp.where(own_genes, s_inner * s_left * s_right, 0.0), keepdims=True)
        board[...] = jnp.zeros((LANES, LANES), f32)
        board[0:4, :] = s_inner * s_left * s_left * s_left * s_right
        board[4:8, :] = s_left * s_right
        columns = board[...].T[0:PIECE, :]
        cube_of, flat_of = jnp.zeros((PIECE, COLS), f32), jnp.zeros((PIECE, COLS), f32)
        spot_density, spot_prior = jnp.zeros((1, COLS), f32), jnp.zeros((1, COLS), f32)
        for k in range(SLIDES):
            inside = member[k : k + 1, :]
            cube_of = cube_of + columns[:, k : k + 1] * inside
            flat_of = flat_of + columns[:, 4 + k : 5 + k] * inside
            spot_density = spot_density + slide_total[12:13, k : k + 1] * inside
            spot_prior = spot_prior + slide_total[12:13, 4 + k : 5 + k] * inside
        target_share = prior[...] / spot_prior
        logs = jnp.log(target_share) - jnp.log(density / spot_density)
        density_part = jnp.sum(target_share * logs, keepdims=True) / SLIDES
        grad_density = (1.0 / spot_density - target_share / density) / SLIDES
        gene_part = gene_scale * (cube_of * pv - flat_of * tv)
    with jax.named_scope("spot_sums_z"):
        far.wait_recv()
        spot_total = spot_far[0]
        for d in range(1, 8):
            spot_total = spot_total + spot_far[d]
        p_inner, p_square = spot_total[0:1, :], spot_total[1:2, :]
        p_left, p_right = lax.rsqrt(p_square + epsilon), lax.rsqrt(truth_square + epsilon)
        spot_sum = jnp.sum(p_inner * p_left * p_right, keepdims=True)
        spot_cube = p_inner * p_left * p_left * p_left * p_right
        grad = gene_part + spot_scale * (spot_cube * pv - (p_left * p_right) * tv)
        grads[z, piece(y), :] = grad.astype(bf16)
    with jax.named_scope("sends_done"):
        for sent in parcels.values():
            sent.wait_send()
        wires.close()

    A, B = pl.ds(0, CLOSE), pl.ds(CLOSE, COLS - CLOSE)
    blocks = [ring(z, d, 8) for d in REACH]

    def put(block, rows, lanes, device):
        view = grads.at[block, rows, lanes]
        return wires.send(view, view, device)

    def y_share(block, lanes):
        return put(block, piece(y), lanes, y_up), put(block, piece(y), lanes, y_down)

    def y_straight(block, lanes):
        view = grads.at[block, piece(y), lanes]
        others = [(view, away("y", d)) for d in (1, 3, 2)]
        return wires.spread(view, others, grads.at[block, pl.ds(0, 3 * PIECE), lanes])

    def y_onward(block, lanes, shared):
        shared[0].wait_recv()
        up = put(block, piece(ring(y, 3, 4), 0, HOP), lanes, y_up)
        shared[1].wait_recv()
        down = put(block, piece(ring(y, 1, 4), HOP, HOP), lanes, y_down)
        return up, down

    def z_share(step, rows, lanes):
        above, below = ring(z, 1 - step, 8), ring(z, step - 1, 8)
        return put(above, rows[0], lanes, z_up), put(below, rows[1], lanes, z_down)

    own_rows, all_rows = (piece(y), piece(y)), (pl.ds(0, OWN), pl.ds(0, OWN))
    own_halves = (piece(y, 0, HOP), piece(y, HOP, HOP))
    all_halves = (pl.ds(0, LANES), pl.ds(LANES, LANES))
    base = wires.take(57)

    def each(turn, body):
        if turn in (0, 4):
            body(2 * turn - (turn > 0), ring(z, turn, 8))
        else:

            @pl.loop(0, 2)
            def _(i):
                body(2 * turn - 1 + i, ring(z, turn * (1 - 2 * i), 8))

    keep, give = c * HALF, (1 - c) * HALF

    def some_rows(first, size=HALF):
        return pl.ds(pl.multiple_of(first, 16), size)

    def twin_link(n):
        return wires.link(xp.at[n, some_rows(give)], xc.at[n], twin, base + n)

    def out_slot(k, odd, i):
        return 2 * (k + 6 * odd) + i

    def in_slot(k, odd, i, core):
        if k < 2:
            return 16 + 2 * (k + 2 * odd) + i
        return 2 * (k - 2 + 4 * core) + i

    def eighth_links(k, odd, i):
        here, there = out_slot(k, odd, i), in_slot(k, odd, i, c)
        device = right if k in (0, 2, 3) else left
        if k > 1:
            device = {"x": device["x"], "c": odd}
        return (
            wires.link(
                scale_out.at[here], scale_in.at[there], device, base + 8 + here, base + 8 + there
            ),
            wires.link(
                coded_out.at[here], coded_in.at[there], device, base + 32 + here, base + 32 + there
            ),
        )

    def eighth(i):
        return some_rows(i * EIGHTH, EIGHTH)

    def kept_eighth(high, i):
        return some_rows(keep + (2 * high + i) * EIGHTH, EIGHTH)

    def eighth_send(n, odd, high, k, i):
        summed = xp[n, kept_eighth(high, i), :]
        top = jnp.maximum(jnp.max(jnp.abs(summed), axis=0, keepdims=True), 1e-30)
        here = out_slot(k, odd, i)
        scale_out[here] = top * (1.0 / TOP)
        coded_out[here] = jnp.round(summed * (TOP / top)).astype(jnp.int16)
        for link in eighth_links(k, odd, i):
            link.start()

    def eighth_value(k, odd, i, core):
        there = in_slot(k, odd, i, core)
        wires.link(scale_in.at[there], scale_in.at[there], twin, base + 8 + there).wait_recv()
        wires.link(coded_in.at[there], coded_in.at[there], twin, base + 32 + there).wait_recv()
        return coded_in[there].astype(f32) * scale_in[there]

    def distance(block):
        return ring(block // 2 - x, 0, 4)

    def block_first(n, block):
        xp[n] = lax.dot_general(
            weights[...],
            grads[block],
            (((1,), (1,)), ((), ())),
            preferred_element_type=f32,
        )
        twin_link(n).start()

    def cell_part(n, block):
        product = jnp.dot(profiles[block], grads[block], preferred_element_type=f32)
        if isinstance(n, int) and n == 0:
            part[0:ROWS, :] = product
        else:
            part[0:ROWS, :] += product

    at_own, at_twin = jnp.int32(0), jnp.int32(0)
    for n in range(8):
        at_own = at_own + n * jnp.where(blocks[n] == own, 1, 0)
        at_twin = at_twin + n * jnp.where(blocks[n] == block_of(x, 0, 1 - c), 1, 0)
    ending = wires.link(xp.at[at_twin, some_rows(keep)], ended, twin, base + 56)

    def block_second(n, block):
        odd = lax.rem(block, 2)
        twin_link(n).wait_recv()

        @pl.loop(0, 4)
        def _(i):
            xp[n, some_rows(keep + i * EIGHTH, EIGHTH), :] += xc[n, eighth(i), :]

        @pl.when(distance(block) == 2)
        def _():
            @pl.loop(0, 2)
            def _(i):
                eighth_send(n, odd, 0, 0, i)
                eighth_send(n, odd, 1, 1, i)

        @pl.when(distance(block) == 1)
        def _():
            @pl.loop(0, 2)
            def _(i):
                eighth_send(n, odd, 1, 2, i)

        @pl.when(distance(block) == 3)
        def _():
            @pl.loop(0, 2)
            def _(i):
                eighth_send(n, odd, 0, 4, i)

        @pl.when(block == block_of(x, 0, 1 - c))
        def _():
            ending.start()

    def add_and_send(n, odd, high, k, onward):
        @pl.loop(0, 2)
        def _(i):
            xp[n, kept_eighth(high, i), :] += eighth_value(k, odd, i, c)
            eighth_send(n, odd, high, onward, i)

    def block_third(n, block):
        odd = lax.rem(block, 2)

        @pl.when(distance(block) == 1)
        def _():
            add_and_send(n, odd, 0, 0, 3)

        @pl.when(distance(block) == 3)
        def _():
            add_and_send(n, odd, 1, 1, 5)

    def one(body, n):
        body(n, blocks[n])

    bz, az, shared_b, onward_b = {1: z_share(1, own_rows, B)}, {}, {}, {}
    straight = y_straight(z, A)
    shared_b[0] = y_straight(z, B)
    rounds = {0: (0,), 1: (1, 2), 2: (3, 4), 3: (5, 6), 4: (7,)}

    def turn_b(turn):
        both(bz[turn])
        if turn < 4:
            bz[turn + 1] = z_share(turn + 1, own_rows if turn < 3 else own_halves, B)
        if turn == 4:
            shared_b[7] = y_straight(blocks[7], B)
        else:
            for n in rounds[turn]:
                shared_b[n] = y_share(blocks[n], B)

    def turn_a(turn):
        if turn:
            both(az[turn])
        else:
            straight.wait_recv()
        if turn < 4:
            az[turn + 1] = z_share(turn + 1, all_rows if turn < 3 else all_halves, A)

    def turn_on(turn):
        for n in rounds[turn]:
            onward_b[n] = y_onward(blocks[n], B, shared_b[n])

    def turn_first(turn):
        if turn in (0, 4):
            shared_b[rounds[turn][0]].wait_recv()
        else:
            for n in rounds[turn]:
                both(onward_b[n])
        each(turn, block_first)

    turn_b(1)
    turn_a(0)
    turn_b(2)
    turn_a(1)
    turn_on(1)
    turn_on(2)
    turn_b(3)
    turn_first(0)
    turn_a(2)
    turn_first(2)
    turn_on(3)
    turn_first(1)
    one(block_second, 0)
    one(block_second, 3)
    one(block_second, 4)
    turn_b(4)
    turn_a(3)
    turn_first(3)
    each(0, cell_part)
    turn_a(4)
    one(block_second, 1)
    one(block_second, 2)
    one(block_second, 5)
    each(1, cell_part)
    one(block_second, 6)
    turn_first(4)
    each(2, cell_part)
    each(3, cell_part)
    one(block_second, 7)
    each(4, cell_part)

    with jax.named_scope("column_sums"):
        column_mine[...] = jnp.zeros((2, COLS), f32)
        column_mine[1:2, :] = jnp.where(column == 0, gene_sum, 0.0)
        for b in range(BLOCKS):
            rows = lanes_of(b)
            across = jnp.zeros((LANES, LANES), f32)
            for j in range(COLS // LANES):
                lanes, cut = lanes_of(j), slice(j * LANES, (j + 1) * LANES)
                whole = (grown[rows, lanes] * scale[:, cut]) * (
                    part[rows, lanes] + grad_density[:, cut]
                )
                part[rows, lanes] = whole
                across = across + whole
                column_mine[0:1, lanes] += jnp.sum(whole * gate[rows, :], axis=0, keepdims=True)
            filter_msgs[0, b : b + 1, :] = jnp.sum(across.T, axis=0, keepdims=True)
        filter_msgs[0, 11:12, :] = jnp.where(
            row_lane == 0, spot_sum, jnp.where(row_lane == 1, density_part, 0.0)
        )
        filter_msgs[0, 12:16, :] = jnp.zeros((4, LANES), f32)
        near = spread_y(column_mine, column_near)
        sums = spread_spot(filter_msgs)
    for n in (0, 1, 2, 4):
        one(block_third, n)
    with jax.named_scope("column_sums_y"):
        near.wait_recv()
        column_far[0] = column_mine[...] + column_near[0] + column_near[1] + column_near[2]
        far = spread_z(column_far)
    for n in (3, 7, 5, 6):
        one(block_third, n)
    with jax.named_scope("column_sums_z"):
        far.wait_recv()
        column_total = column_far[0]
        for d in range(1, 8):
            column_total = column_total + column_far[d]
    with jax.named_scope("logits_gradient"):
        dot_scale = column_total[0:1, :] * scale
        for b in range(BLOCKS):
            rows = lanes_of(b)
            for j in range(COLS // LANES):
                lanes, cut = lanes_of(j), slice(j * LANES, (j + 1) * LANES)
                part[rows, lanes] = (
                    gate[rows, :] * part[rows, lanes] - grown[rows, lanes] * dot_scale[:, cut]
                )
    with jax.named_scope("filter_gradient"):
        sums.wait_recv()
        filter_total = filter_msgs[0]
        for d in range(1, 8):
            filter_total = filter_total + filter_msgs[d]
        gap = kept - target[0].astype(f32)
        root = jnp.sqrt(gap * gap + 1.0)
        on = filter_total[0:BLOCKS, :] + gap / root / CELLS + (1.0 - 2.0 * gates) / CELLS
        filter_out[...] = on * gates * (1.0 - gates)
        values = (
            -column_total[1:2, 0:1] * gene_scale,
            -filter_total[11:12, 0:1] * spot_scale,
            filter_total[11:12, 1:2],
            root / CELLS,
            spread / CELLS,
        )
        losses = jnp.zeros((1, LANES), f32)
        for k, value in enumerate(values):
            losses = losses + jnp.where(row_lane == k, value, 0.0)
        losses_out[...] = losses

    with jax.named_scope("last_sum"):
        ending.wait_recv()
        for core_rows, core in ((keep, c), (give, 1 - c)):
            for high, ks in ((0, (3, 4)), (1, (2, 5))):

                @pl.loop(0, 2)
                def _(i, core_rows=core_rows, core=core, high=high, ks=ks):
                    rows = some_rows(core_rows + (2 * high + i) * EIGHTH, EIGHTH)
                    if core is c:
                        start = xp[at_own, rows, :]
                    else:
                        start = ended[some_rows((2 * high + i) * EIGHTH, EIGHTH), :]
                    total = start + eighth_value(ks[0], 0, i, core)
                    profile_out[rows, :] = total + eighth_value(ks[1], 0, i, core)

    with jax.named_scope("sends_done"):
        for n in range(8):
            twin_link(n).wait_send()
        for odd in range(2):
            for k in range(6):
                for i in range(2):
                    for link in eighth_links(k, odd, i):
                        link.wait_send()
        ending.wait_send()
    with jax.named_scope("wires_done"):
        wires.close()


def training_step(sizes, target, logits, filters, expression, spatial, prior):
    f32, bf16 = jnp.float32, jnp.bfloat16
    anywhere = pl.BlockSpec(memory_space=pl.ANY)
    inside = pl.BlockSpec(memory_space=pltpu.VMEM)
    scalars = pl.BlockSpec(memory_space=pltpu.SMEM)
    near = COLS - SPLIT
    return pl.pallas_call(
        step_kernel,
        out_shape=(
            pltpu.VMEM((PIECE, COLS), f32),
            pltpu.VMEM((GENES, COLS), f32),
            pltpu.VMEM((ROWS, OWN), f32),
            pltpu.VMEM((BLOCKS, LANES), f32),
            pltpu.VMEM((1, LANES), f32),
        ),
        in_specs=[scalars, scalars, anywhere, anywhere, anywhere, anywhere, anywhere],
        out_specs=(inside, inside, inside, inside, inside),
        scratch_shapes=[
            pltpu.VMEM((BLOCKS, LANES), f32),
            pltpu.VMEM((1, COLS), f32),
            pltpu.VMEM((ROWS, COLS), f32),
            pltpu.VMEM((ROWS, COLS), bf16),
            pltpu.VMEM((8, ROWS, OWN), bf16),
            pltpu.VMEM((COLS, LANES), f32),
            pltpu.VMEM((LANES, COLS), f32),
            pltpu.VMEM((ROWS, LANES), f32),
            pltpu.VMEM((SLIDES, COLS), f32),
            pltpu.VMEM((LANES, LANES), f32),
            pltpu.VMEM((4, COLS), f32),
            pltpu.VMEM((3, 4, COLS), f32),
            pltpu.VMEM((8, 4, COLS), f32),
            parcel_buffers(HOP, near, 8, 16),
            parcel_buffers(PIECE, near, 8, 16),
            parcel_buffers(HOP, near, 2, 2),
            parcel_buffers(PIECE, near, 2, 6),
            parcel_buffers(LANES, LANES, 2 * GROUPS, 2 * GROUPS),
            parcel_buffers(OWN, LANES, 2 * GROUPS, 6 * GROUPS),
            parcel_buffers(HOP, SPLIT, 2, 2),
            parcel_buffers(PIECE, SPLIT, 2, 2),
            pltpu.VMEM((8, OWN, COLS), bf16),
            pltpu.VMEM((8, ROWS, OWN), f32),
            pltpu.VMEM((8, HALF, OWN), f32),
            pltpu.VMEM((HALF, OWN), f32),
            pltpu.VMEM((24, EIGHTH, OWN), jnp.int16),
            pltpu.VMEM((24, EIGHTH, OWN), jnp.int16),
            pltpu.VMEM((24, 1, OWN), f32),
            pltpu.VMEM((24, 1, OWN), f32),
            pltpu.VMEM((8, 16, LANES), f32),
            pltpu.VMEM((2, COLS), f32),
            pltpu.VMEM((3, 2, COLS), f32),
            pltpu.VMEM((8, 2, COLS), f32),
            pltpu.VMEM((2, COLS), f32),
            pltpu.VMEM((3, 2, COLS), f32),
            pltpu.VMEM((8, 2, COLS), f32),
            pltpu.VMEM((8, 16, LANES), f32),
            pltpu.SemaphoreType.DMA((COPIES + SPREADS,)),
            pltpu.SemaphoreType.DMA((COPIES + SPREADS,)),
            pltpu.SemaphoreType.DMA((BLOCKS + 4,)),
        ],
        compiler_params=pltpu.CompilerParams(
            collective_id=0, has_side_effects=True, vmem_limit_bytes=LIMIT
        ),
        name="training_step",
    )(sizes, target, logits, filters, expression, spatial, prior)


def finish_kernel(
    losses,
    pred,
    part,
    profile,
    filter_rows,
    losses_out,
    pred_out,
    logits_out,
    profile_out,
    filter_out,
    sems,
):
    pieces = [(part.at[0:ROWS], logits_out), (profile, profile_out), (pred, pred_out)]
    pieces.append((filter_rows, filter_out))
    copies = [pltpu.make_async_copy(a, b, sems.at[i]) for i, (a, b) in enumerate(pieces)]
    for copy in copies:
        copy.start()
    row_lane = lax.broadcasted_iota(jnp.int32, (1, LANES), 1)
    for k in range(5):
        losses_out[k] = jnp.sum(jnp.where(row_lane == k, losses[...], 0.0))
    for copy in copies:
        copy.wait()


def finish(losses, pred, part, profile, filter_rows):
    f32 = jnp.float32
    anywhere = pl.BlockSpec(memory_space=pl.ANY)
    inside = pl.BlockSpec(memory_space=pltpu.VMEM)
    scalars = pl.BlockSpec(memory_space=pltpu.SMEM)
    return pl.pallas_call(
        finish_kernel,
        out_shape=(
            jax.ShapeDtypeStruct((5,), f32),
            jax.ShapeDtypeStruct((PIECE, COLS), f32),
            jax.ShapeDtypeStruct((ROWS, COLS), f32),
            jax.ShapeDtypeStruct((ROWS, OWN), f32),
            jax.ShapeDtypeStruct((BLOCKS, LANES), f32),
        ),
        in_specs=[inside] * 5,
        out_specs=(scalars, anywhere, anywhere, anywhere, anywhere),
        scratch_shapes=[pltpu.SemaphoreType.DMA((4,))],
        compiler_params=pltpu.CompilerParams(vmem_limit_bytes=1024 * 1024),
        name="finish",
    )(losses, pred, part, profile, filter_rows)


def on_device(logits, filter_logits, expression, spatial, prior, slide_sizes, target):
    pred, part, profile, filter_rows, losses = training_step(
        slide_sizes,
        target,
        logits,
        filter_logits.reshape(BLOCKS, LANES),
        expression,
        spatial,
        prior.reshape(1, COLS),
    )
    losses, pred, grad_logits, grad_expression, grad_filter = finish(
        losses, pred, part, profile, filter_rows
    )
    return (losses, pred.T, grad_logits, grad_filter.reshape(-1), grad_expression)


def solution(mesh):
    split = Mesh(mesh.devices.reshape(8, 4, 4, 2), ("z", "y", "x", "c"))
    return jax.shard_map(
        on_device,
        mesh=split,
        in_specs=(P(CELL, SPOT), P(CELL), P(CELL, SPOT), P(SPOT, None), P(SPOT), P(), P()),
        out_specs=(P(), P(SPOT, CELL), P(CELL, SPOT), P(CELL), P(CELL, SPOT)),
        check_vma=False,
    )
```
